32 devices in a mesh: groups: 2 (over y), chan: 4 (over z), day: 2 (over x), sub: 2 (over core).
Axes of the slice: x: 2, y: 2, z: 4, core: 2. Of those that a mesh axis runs over, the one named last changes fastest.
Arguments:
- spectra: bfloat16 [4, 16, 128, 2, 512], P(('groups', 'day'), 'sub', 'chan'), parts along dimension 0, may hold values from -6 to 6
- tile_offset: int32 [4, 3], P('chan'), may hold values from -1 to 3, as said below
- pair_reach: int32 [4, 3], P('chan'), may hold values from 0 to 128, as said below
Outputs:
- correlations: float32 [8, 3, 32, 32, 256], P(('groups', 'chan'), None, ('day', 'sub')), parts along dimension 0
The draws below stay inside these ranges and needn't reach their ends.
There are 2 independent parts, one for each index of `groups`. The reference program is written for one: setup_inputs(seed, part) draws one part's arguments, and reference() takes and returns one part's arrays. A program takes and returns all parts, laid end to end along the dimension named above; an argument that names none is the same for every part. Nothing has to cross between parts.
Inputs may be any that keep to these rules, and one draw needn't show every extreme that they name: `tile_offset`: in row a the first 1 to 3 slots hold distinct offsets s with a + s < 4, the rest hold -1; row 0 is full and holds 3. `pair_reach`: A slot with offset s holds a value from max(2, (s - 1) * 32 + 2) to (s + 1) * 32; a padding slot holds 0.
All inputs are finite; a program needn't handle non-finite values.
Results may differ from the reference program's by a relative error of at most 0.004.
Values may be sent and summed in bfloat16 or wider, within the bound.
No kernel may reach another device: no remote copies, remote signals or barrier semaphores. Data moves between devices by JAX's collectives and lax.ppermute only.
A program may use at most 128 MiB of HBM per device.

```python
import math
import jax
import jax.numpy as jnp
from jax import lax

CB = 32
F = 512
BAND = 32
LAGS = 256
MAXT = 3
STEPS = 3
BLOCKS = 4
CHANNELS = 128
DAYS = 2
W = 16


def tile_plan(key):
    key_order, key_count, key_reach = jax.random.split(key, 3)
    block_ids = jnp.arange(BLOCKS, dtype=jnp.int32)
    available = jnp.minimum(STEPS, BLOCKS - 1 - block_ids) + 1
    offset_ids = jnp.arange(STEPS + 1, dtype=jnp.int32)
    raw_scores = jax.random.randint(key_order, (BLOCKS, STEPS + 1), 0, 1 << 20)
    scores = raw_scores * (STEPS + 1) + offset_ids[None, :]
    scores = jnp.where(offset_ids[None, :] < available[:, None], scores, (1 << 28) + offset_ids[None, :])
    scores = scores.at[0, STEPS].set(-1)
    order = jnp.argsort(scores, axis=1, stable=True)[:, :MAXT].astype(jnp.int32)
    count = jax.random.randint(key_count, (BLOCKS,), 1, MAXT + 1)
    count = jnp.minimum(count, available).at[0].set(MAXT)
    valid = jnp.arange(MAXT, dtype=jnp.int32)[None, :] < count[:, None]
    offsets = jnp.where(valid, order, -1).astype(jnp.int32)
    lower = jnp.maximum(2, (order - 1) * CB + 2)
    upper = (order + 1) * CB
    reach_vals = jax.random.randint(key_reach, (BLOCKS, MAXT), lower, upper + 1)
    reach_vals = reach_vals.at[0, 0].set((STEPS + 1) * CB)
    reach_vals = jnp.where(valid, reach_vals, 0).astype(jnp.int32)
    return (offsets, reach_vals)


def draw_tile_offset(key, part):
    offsets, reach_vals = tile_plan(key)
    return offsets


def draw_pair_reach(key, part):
    offsets, reach_vals = tile_plan(key)
    return reach_vals


def levels(own_key, shape, pieces, smallest, top_value):
    loudness, own = 1.0, jax.random.fold_in(own_key, 6)
    for axis_at, blocks in pieces:
        heights = jnp.exp(jax.random.uniform(jax.random.fold_in(own, axis_at), (blocks,), jnp.float32, smallest / len(pieces), top_value / len(pieces)))
        loudness = loudness * jnp.repeat(heights, shape[axis_at] // blocks).reshape([-1 if axis == axis_at else 1 for axis in range(len(shape))])
    return loudness


def scatter_about(stream_key, extent, spread, limit, pieces=(), kind=jnp.bfloat16):
    loudness = levels(stream_key, extent, pieces, -0.22, 0.18) if pieces else 1.0
    array = jax.random.normal(stream_key, extent, jnp.float32) * spread * loudness
    return jnp.minimum(jnp.maximum(array, -limit), limit).astype(kind)


def setup_inputs(seed: int = 0, part: int = 0) -> dict:
    splits = jax.random.split(jax.random.key(seed), 4)
    own_keys = jax.random.split(jax.random.fold_in(splits[3], part), 4)
    return {
        "spectra": scatter_about(own_keys[0], (DAYS, W, CHANNELS, 2, F), 1.0, 6.0, ((0, 2), (1, 2), (2, 4))),
        "tile_offset": draw_tile_offset(jax.random.fold_in(splits[3], 71), part),
        "pair_reach": draw_pair_reach(jax.random.fold_in(splits[3], 71), part),
    }


EPSILON = 1e-06

def whiten(spectra_in):
    values = spectra_in.astype(jnp.float32)
    power_sum = values[..., 0, :] ** 2 + values[..., 1, :] ** 2
    power_shape = power_sum.shape
    banded = power_sum.reshape(power_shape[:-1] + (power_shape[-1] // BAND, BAND))
    band_scale = lax.rsqrt(lax.optimization_barrier(jnp.mean(banded, axis=-1, keepdims=True)) + EPSILON)
    band_scale = jnp.broadcast_to(band_scale, banded.shape).reshape(power_shape)
    return (values * band_scale[..., None, :]).astype(jnp.bfloat16)

def lag_table(bin_count, lag_count):
    bin_index = jnp.arange(bin_count, dtype=jnp.float32)
    lag_index = jnp.arange(lag_count, dtype=jnp.float32) - lag_count // 2
    angle_table = math.pi * bin_index[:, None] * lag_index[None, :] / bin_count
    return jnp.concatenate([jnp.cos(angle_table), -jnp.sin(angle_table)], axis=0)

def reference(spectra, tile_offset, pair_reach):
    white = whiten(spectra)
    table = lag_table(F, LAGS)
    norm_scale = 1.0 / math.sqrt(F * DAYS * W)
    row_index = jnp.arange(CB, dtype=jnp.int32)

    def one_block(block_id):
        own_rows = lax.dynamic_slice_in_dim(white, block_id * CB, CB, 2).astype(jnp.float32)
        own_turned = jnp.stack([own_rows[:, :, :, 1, :], -own_rows[:, :, :, 0, :]], axis=3)
        results = []
        for slot_index in range(MAXT):
            offset = tile_offset[block_id, slot_index]
            reach_now = pair_reach[block_id, slot_index]
            begin = ((block_id + jnp.maximum(offset, 0)) * CB).astype(jnp.int32)
            partner = lax.dynamic_slice_in_dim(white, begin, CB, 2).astype(jnp.float32)
            real_part = jnp.einsum('dwicf,dwjcf->ijf', own_rows, partner, precision=lax.Precision.HIGHEST)
            imag_part = jnp.einsum('dwicf,dwjcf->ijf', own_turned, partner, precision=lax.Precision.HIGHEST)
            joined = jnp.concatenate([real_part, imag_part], axis=2).reshape(CB * CB, 2 * F)
            lagged = jnp.dot(joined, table, precision=lax.Precision.HIGHEST, preferred_element_type=jnp.float32)
            lagged = lagged.reshape(CB, CB, LAGS) * norm_scale
            distance = offset * CB + row_index[None, :] - row_index[:, None]
            distance_abs = jnp.abs(distance)
            keep_mask = (offset >= 0) & (distance_abs > 0) & (distance_abs < reach_now)
            results.append(jnp.where(keep_mask[:, :, None], lagged, jnp.float32(0.0)))
        return jnp.stack(results, axis=0)
    return lax.map(one_block, jnp.arange(BLOCKS, dtype=jnp.int32))
```

```python
import functools
import math

import jax
import jax.numpy as jnp
import ml_dtypes
import numpy as np
from jax import lax
from jax.experimental import pallas as pl
from jax.experimental.pallas import tpu as pltpu
from jax.sharding import PartitionSpec as P

BAND = 32
LAGS = 256
MAX_STEPS = 4
EPSILON = 1e-06
LANES = 128
ROWS = 16
OWN = 4
VMEM_LIMIT = 40 << 20


def lag_table(bin_count):
    bins = np.arange(bin_count, dtype=np.float64)[:, None]
    lags = np.arange(LAGS, dtype=np.float64)[None, :] - LAGS // 2
    angle = np.pi * bins * lags / bin_count
    table = np.concatenate([np.cos(angle), -np.sin(angle)], axis=0).astype(np.float32)
    return table.astype(ml_dtypes.bfloat16)


def whiten_into(source, target, as_row):
    source_ref, begin = source
    _, windows, channels, bins = source_ref.shape
    width = 2 * LANES
    row = lax.broadcasted_iota(jnp.int32, (width, width), 0) // BAND
    col = lax.broadcasted_iota(jnp.int32, (width, width), 1) // BAND
    mean_matrix = jnp.where(row == col, 1.0 / BAND, 0.0).astype(jnp.bfloat16)
    for at in range(0, bins, width):
        lanes = pl.ds(at, width)
        real = source_ref[0, :, :, lanes].astype(jnp.float32).reshape(windows * channels, width)
        imag = source_ref[1, :, :, lanes].astype(jnp.float32).reshape(windows * channels, width)
        rest = real * real + imag * imag
        mean = jnp.zeros_like(rest)
        for _ in range(3):
            piece = rest.astype(jnp.bfloat16)
            mean += jnp.dot(piece, mean_matrix, preferred_element_type=jnp.float32)
            rest = rest - piece.astype(jnp.float32)
        scale = lax.rsqrt(mean + EPSILON)
        real = (real * scale).astype(jnp.bfloat16).astype(jnp.float32)
        imag = (imag * scale).astype(jnp.bfloat16).astype(jnp.float32)
        if as_row:
            factors = (real + imag, real, imag)
        else:
            factors = (real, -(real + imag), real - imag)
        for k, factor in enumerate(factors):
            target[k, :, pl.ds(begin, channels), lanes] = factor.reshape(windows, channels, width)


def tile_kernel(part_count, can_swap, scalars, own, *refs):
    parts = refs[:part_count]
    table, keep, send, rows, cols, cross = refs[part_count:]
    _, windows, row_count, bins = own.shape
    col_count = cols.shape[2]
    owners, share = keep.shape[0], keep.shape[1]
    begins = [sum(p.shape[2] for p in parts[:k]) for k in range(part_count)]

    def straight():
        whiten_into((own, 0), rows, True)
        for part, begin in zip(parts, begins):
            whiten_into((part, begin), cols, False)

    def swapped():
        whiten_into((own, 0), cols, False)
        for part, begin in zip(parts, begins):
            whiten_into((part, begin), rows, True)

    if can_swap:
        pl.when(scalars[1] == 0)(straight)
        pl.when(scalars[1] != 0)(swapped)
    else:
        straight()

    groups = col_count // ROWS

    def body(step, carry):
        row_at = pl.multiple_of((step // groups) * 8, 8)
        col_at = pl.multiple_of((step % groups) * ROWS, ROWS)
        for at in range(0, bins, LANES):
            lanes = pl.ds(at, LANES)
            for first in range(0, 8, OWN):
                sums = [[None] * 3 for _ in range(OWN)]
                for w in range(windows):
                    for k in range(3):
                        right = cols[k, w, pl.ds(col_at, ROWS), lanes]
                        left = rows.at[k, w, pl.ds(row_at, 8), lanes]
                        for i in range(OWN):
                            product = right * left[pl.ds(first + i, 1)]
                            sums[i][k] = product if w == 0 else sums[i][k] + product
                for i in range(OWN):
                    k1, k2, k3 = sums[i]
                    at_row = (row_at + first + i) * col_count + col_at
                    place = pl.ds(pl.multiple_of(at_row, ROWS), ROWS)
                    cross[place, pl.ds(at, LANES)] = (k1 - k3).astype(jnp.bfloat16)
                    cross[place, pl.ds(bins + at, LANES)] = (k1 + k2).astype(jnp.bfloat16)
        return carry

    lax.fori_loop(0, (row_count // 8) * groups, body, 0)
    for owner in range(owners):
        lags = jnp.dot(
            cross[pl.ds(owner * 2 * share, 2 * share)], table[...], preferred_element_type=jnp.float32
        )
        low, high = lags[:share], lags[share:]

        @pl.when(scalars[0] == 0)
        def _():
            keep[owner] = low
            send[owner] = high.astype(send.dtype)

        @pl.when(scalars[0] != 0)
        def _():
            keep[owner] = high
            send[owner] = low.astype(send.dtype)


def lag_tile(scalars, own, parts, table, owners, can_swap):
    _, windows, row_count, bins = own.shape
    col_count = sum(part.shape[2] for part in parts)
    share = row_count * col_count // (2 * owners)
    vmem = pl.BlockSpec(memory_space=pltpu.VMEM)
    return pl.pallas_call(
        functools.partial(tile_kernel, len(parts), can_swap),
        out_shape=(
            jax.ShapeDtypeStruct((owners, share, LAGS), jnp.float32),
            jax.ShapeDtypeStruct((owners, share, LAGS), jnp.bfloat16),
        ),
        in_specs=[pl.BlockSpec(memory_space=pltpu.SMEM)] + [vmem] * (len(parts) + 2),
        out_specs=(vmem, vmem),
        scratch_shapes=[
            pltpu.VMEM((3, windows, row_count, bins), jnp.float32),
            pltpu.VMEM((3, windows, col_count, bins), jnp.float32),
            pltpu.VMEM((row_count * col_count, 2 * bins), jnp.bfloat16),
        ],
        compiler_params=pltpu.CompilerParams(vmem_limit_bytes=VMEM_LIMIT),
        cost_estimate=pl.CostEstimate(
            flops=5 * 10**6 * row_count * col_count, bytes_accessed=2 << 20, transcendentals=0
        ),
    )(scalars, own, *parts, table)


def final_kernel(shapes, norm_scale, scalars, *refs):
    out = refs[-1]
    row_count, width = out.shape[1], out.shape[2]
    slot = pl.program_id(0)
    slots = pl.num_programs(0)
    offset, reach = scalars[slot], scalars[slots + slot]
    row_begin = scalars[2 * slots] * row_count
    out[...] = jnp.zeros_like(out)
    at = 0
    for step, parts in enumerate(shapes):
        begin = 0
        for term_count, columns in parts:
            terms = refs[at : at + term_count]
            at += term_count

            @pl.when(offset == step)
            def _(terms=terms, begin=begin, columns=columns, step=step):
                value = functools.reduce(
                    lambda x, y: x + y, [t[0].astype(jnp.float32) for t in terms]
                )
                value = value.reshape(row_count, columns, LAGS)
                row = lax.broadcasted_iota(jnp.int32, value.shape, 0) + row_begin
                col = lax.broadcasted_iota(jnp.int32, value.shape, 1) + begin
                distance = jnp.abs(step * width + col - row)
                kept = (distance > 0) & (distance < reach)
                out[0, :, pl.ds(begin, columns), :] = jnp.where(kept, value * norm_scale, 0.0)

            begin += columns


def assemble(scalars, values, slots, row_count, width, norm_scale):
    shapes = [[(len(terms), columns) for columns, terms in parts] for parts in values]
    operands = [term for parts in values for _, terms in parts for term in terms]

    def spec(term):
        if term.shape[0] == 1:
            return pl.BlockSpec((1,) + term.shape[1:], lambda t, sc: (0, 0, 0))
        return pl.BlockSpec((1,) + term.shape[1:], lambda t, sc: (sc[2 * slots + 1], 0, 0))

    return pl.pallas_call(
        functools.partial(final_kernel, shapes, norm_scale),
        out_shape=jax.ShapeDtypeStruct((slots, row_count, width, LAGS), jnp.float32),
        grid_spec=pltpu.PrefetchScalarGridSpec(
            num_scalar_prefetch=1,
            grid=(slots,),
            in_specs=[spec(term) for term in operands],
            out_specs=pl.BlockSpec((1, row_count, width, LAGS), lambda t, sc: (t, 0, 0, 0)),
        ),
        compiler_params=pltpu.CompilerParams(vmem_limit_bytes=VMEM_LIMIT),
    )(scalars, *operands)


def on_device(spectra, tile_offset, pair_reach):
    blocks = lax.axis_size("chan")
    days, cores = lax.axis_size("day"), lax.axis_size("sub")
    steps = min(MAX_STEPS, blocks - 1)
    wraps = blocks >= 3 and steps == blocks - 1
    local_days, local_windows, width, _, bins = spectra.shape
    norm_scale = 1.0 / math.sqrt(bins * local_days * days * local_windows * cores)
    row_count = width // (days * cores)
    slots = tile_offset.shape[1]
    day, core, block = lax.axis_index("day"), lax.axis_index("sub"), lax.axis_index("chan")
    table = jnp.asarray(lag_table(bins))

    own = jnp.transpose(spectra, (3, 0, 1, 2, 4)).reshape(2, -1, width, bins)
    half = width // 2
    halves = [own[:, :, :half], own[:, :, half:]]

    is_last = (block == blocks - 1).astype(jnp.int32) if wraps else jnp.int32(0)
    scalars = jnp.stack([core, is_last]).astype(jnp.int32)

    def over_cores(value):
        return lax.ppermute(value, "sub", [(k, (k + 1) % cores) for k in range(cores)])

    def reduce_tile(parts, can_swap=False):
        keep, send = lag_tile(scalars, own, parts, table, days, can_swap)
        got = over_cores(send)
        terms = [keep, got]
        for shift in range(1, days):
            to = (day + shift) % days
            piece = lax.dynamic_index_in_dim(keep, to, 0) + lax.dynamic_index_in_dim(got, to, 0).astype(
                jnp.float32
            )
            terms.append(
                lax.ppermute(
                    piece.astype(jnp.bfloat16), "day", [(k, (k + shift) % days) for k in range(days)]
                )
            )
        return terms

    def total(terms):
        return functools.reduce(
            lambda x, y: x + y,
            [
                (lax.dynamic_index_in_dim(t, day, 0) if t.shape[0] > 1 else t).astype(jnp.float32)
                for t in terms
            ],
        )

    values = [[(width, [total(reduce_tile(halves))])]]
    moving = halves
    wrapped = None
    for step in range(1, steps + 1):
        if wraps and step == steps:
            back = lax.ppermute(wrapped.astype(jnp.bfloat16), "chan", [(blocks - 1, 0)])
            values.append([(width, [back])])
            break
        pairs = [(a + 1, a) for a in range(blocks - step)]
        if wraps and step == 1:
            pairs.append((0, blocks - 1))
        moving = [lax.ppermute(part, "chan", pairs) for part in moving]
        if step == 1:
            wrapped = total(reduce_tile(moving, can_swap=wraps))
            values.append([(width, [wrapped])])
        else:
            values.append([(half, reduce_tile([part])) for part in moving])

    place = jnp.stack([day * cores + core, day]).astype(jnp.int32)
    last_scalars = jnp.concatenate([tile_offset[0], pair_reach[0], place])
    return assemble(last_scalars, values, slots, row_count, width, norm_scale)[None]


def solution(mesh):
    in_specs = (P(("groups", "day"), "sub", "chan", None, None), P("chan", None), P("chan", None))
    out_specs = P(("groups", "chan"), None, ("day", "sub"), None, None)
    return jax.shard_map(
        on_device, mesh=mesh, in_specs=in_specs, out_specs=out_specs, check_vma=False
    )
```

```python
import functools
import math

import jax
import jax.numpy as jnp
import ml_dtypes
import numpy as np
from jax import lax
from jax.experimental import pallas as pl
from jax.experimental.pallas import tpu as pltpu
from jax.sharding import PartitionSpec as P

BAND = 32
LAGS = 256
MAX_STEPS = 4
EPSILON = 1e-06
LANES = 128
ROWS = 16
OWN = 4
VMEM_LIMIT = 40 << 20


def lag_table(bin_count):
    bins = np.arange(bin_count, dtype=np.float64)[:, None]
    lags = np.arange(LAGS, dtype=np.float64)[None, :] - LAGS // 2
    angle = np.pi * bins * lags / bin_count
    table = np.concatenate([np.cos(angle), -np.sin(angle)], axis=0).astype(np.float32)
    return table.astype(ml_dtypes.bfloat16)


def whiten(source):
    _, windows, channels, bins = source.shape
    width = 2 * LANES
    row = lax.broadcasted_iota(jnp.int32, (width, width), 0) // BAND
    col = lax.broadcasted_iota(jnp.int32, (width, width), 1) // BAND
    mean_matrix = jnp.where(row == col, 1.0 / BAND, 0.0).astype(jnp.bfloat16)
    for at in range(0, bins, width):
        lanes = pl.ds(at, width)
        real = source[0, :, :, lanes].astype(jnp.float32).reshape(windows * channels, width)
        imag = source[1, :, :, lanes].astype(jnp.float32).reshape(windows * channels, width)
        rest = real * real + imag * imag
        mean = jnp.zeros_like(rest)
        for _ in range(3):
            piece = rest.astype(jnp.bfloat16)
            mean += jnp.dot(piece, mean_matrix, preferred_element_type=jnp.float32)
            rest = rest - piece.astype(jnp.float32)
        scale = lax.rsqrt(mean + EPSILON)
        shape = (windows, channels, width)
        yield (
            lanes,
            (real * scale).astype(jnp.bfloat16).astype(jnp.float32).reshape(shape),
            (imag * scale).astype(jnp.bfloat16).astype(jnp.float32).reshape(shape),
        )


def row_factors(real, imag):
    return real + imag, real, imag


def col_factors(real, imag):
    return real, -(real + imag), real - imag


def store_factors(source, target, begin, factors):
    for lanes, real, imag in whiten(source):
        for k, value in enumerate(factors(real, imag)):
            target[k, :, pl.ds(begin, source.shape[2]), lanes] = value


def cross_tile(rows, cols, cross):
    _, windows, row_count, bins = rows.shape
    col_count = cols.shape[2]
    groups = col_count // ROWS

    def body(step, carry):
        row_at = pl.multiple_of((step // groups) * 8, 8)
        col_at = pl.multiple_of((step % groups) * ROWS, ROWS)
        for at in range(0, bins, LANES):
            lanes = pl.ds(at, LANES)
            for first in range(0, 8, OWN):
                sums = [[None] * 3 for _ in range(OWN)]
                for w in range(windows):
                    for k in range(3):
                        right = cols[k, w, pl.ds(col_at, ROWS), lanes]
                        left = rows.at[k, w, pl.ds(row_at, 8), lanes]
                        for i in range(OWN):
                            product = right * left[pl.ds(first + i, 1)]
                            sums[i][k] = product if w == 0 else sums[i][k] + product
                for i in range(OWN):
                    k1, k2, k3 = sums[i]
                    at_row = (row_at + first + i) * col_count + col_at
                    place = pl.ds(pl.multiple_of(at_row, ROWS), ROWS)
                    cross[place, pl.ds(at, LANES)] = (k1 - k3).astype(jnp.bfloat16)
                    cross[place, pl.ds(bins + at, LANES)] = (k1 + k2).astype(jnp.bfloat16)
        return carry

    lax.fori_loop(0, (row_count // 8) * groups, body, 0)


def lag_sums(scalars, cross, table, keep, sends):
    owners, share = keep.shape[0], keep.shape[1]
    core, day = scalars[0], scalars[1]
    for shift in range(owners):
        owner = lax.rem(day + shift, owners)
        place = pl.ds(pl.multiple_of(owner * (2 * share), 2 * share), 2 * share)
        lags = jnp.dot(cross[place], table[...], preferred_element_type=jnp.float32)
        low, high = lags[:share], lags[share:]
        send = sends[shift]

        @pl.when(core == 0)
        def _():
            keep[shift] = low
            send[0] = high.astype(send.dtype)

        @pl.when(core != 0)
        def _():
            keep[shift] = high
            send[0] = low.astype(send.dtype)


def begins_of(parts):
    return [sum(p.shape[2] for p in parts[:k]) for k in range(len(parts))]


def own_kernel(part_count, scalars, table, *refs):
    parts = refs[:part_count]
    keep, *sends, rows, cols, cross = refs[part_count:]
    for part, begin in zip(parts, begins_of(parts)):
        for lanes, real, imag in whiten(part):
            for k in range(3):
                rows[k, :, pl.ds(begin, part.shape[2]), lanes] = row_factors(real, imag)[k]
                cols[k, :, pl.ds(begin, part.shape[2]), lanes] = col_factors(real, imag)[k]
    cross_tile(rows, cols, cross)
    lag_sums(scalars, cross, table, keep, sends)


def partner_kernel(part_count, after_count, can_swap, scalars, own_rows, table, *refs):
    parts = refs[:part_count]
    keep, *sends = refs[part_count + after_count : -2 - can_swap]
    cols, cross = refs[-2 - can_swap :][:2]
    begins = begins_of(parts)

    def straight():
        for part, begin in zip(parts, begins):
            store_factors(part, cols, begin, col_factors)
        cross_tile(own_rows, cols, cross)

    def swapped():
        rows = refs[-1]
        for at in range(0, cols.shape[3], LANES):
            lanes = pl.ds(at, LANES)
            real, imag = own_rows[1, :, :, lanes], own_rows[2, :, :, lanes]
            for k, value in enumerate(col_factors(real, imag)):
                cols[k, :, :, lanes] = value
        for part, begin in zip(parts, begins):
            store_factors(part, rows, begin, row_factors)
        cross_tile(rows, cols, cross)

    if can_swap:
        pl.when(scalars[2] == 0)(straight)
        pl.when(scalars[2] != 0)(swapped)
    else:
        straight()
    lag_sums(scalars, cross, table, keep, sends)


VMEM = pl.BlockSpec(memory_space=pltpu.VMEM)
SMEM = pl.BlockSpec(memory_space=pltpu.SMEM)
ANY = pl.BlockSpec(memory_space=pl.ANY)
FREE = pl.CostEstimate(flops=0, bytes_accessed=0, transcendentals=0)
PARAMS = pltpu.CompilerParams(vmem_limit_bytes=VMEM_LIMIT)


def sums_shapes(owners, pairs):
    share = pairs // (2 * owners)
    return [jax.ShapeDtypeStruct((owners, share, LAGS), jnp.float32)] + [
        jax.ShapeDtypeStruct((1, share, LAGS), jnp.bfloat16)
    ] * owners


def own_tile(scalars, parts, table, owners):
    _, windows, _, bins = parts[0].shape
    width = sum(part.shape[2] for part in parts)
    factors = (3, windows, width, bins)
    keep, *sends, rows = pl.pallas_call(
        functools.partial(own_kernel, len(parts)),
        out_shape=sums_shapes(owners, width * width) + [jax.ShapeDtypeStruct(factors, jnp.float32)],
        in_specs=[SMEM] + [VMEM] * (1 + len(parts)),
        out_specs=[VMEM] * (owners + 2),
        scratch_shapes=[
            pltpu.VMEM(factors, jnp.float32),
            pltpu.VMEM((width * width, 2 * bins), jnp.bfloat16),
        ],
        compiler_params=PARAMS,
        cost_estimate=FREE,
    )(scalars, table, *parts)
    return keep, sends, rows


def partner_tile(scalars, own_rows, parts, table, owners, can_swap, after):
    _, windows, width, bins = own_rows.shape
    col_count = sum(part.shape[2] for part in parts)
    keep, *sends = pl.pallas_call(
        functools.partial(partner_kernel, len(parts), len(after), can_swap),
        out_shape=sums_shapes(owners, width * col_count),
        in_specs=[SMEM] + [VMEM] * (2 + len(parts)) + [ANY] * len(after),
        out_specs=[VMEM] * (owners + 1),
        scratch_shapes=[
            pltpu.VMEM((3, windows, col_count, bins), jnp.float32),
            pltpu.VMEM((width * col_count, 2 * bins), jnp.bfloat16),
        ]
        + [pltpu.VMEM((3, windows, width, bins), jnp.float32)] * can_swap,
        compiler_params=PARAMS,
        cost_estimate=FREE,
    )(scalars, own_rows, table, *parts, *after)
    return keep, sends


def add_kernel(term_count, *refs):
    total = functools.reduce(
        lambda x, y: x + y, [t[...].astype(jnp.float32) for t in refs[:term_count]]
    )
    for out in refs[term_count:]:
        out[...] = total.astype(out.dtype)


def add_terms(terms, dtypes):
    shape = (1,) + terms[0][0].shape[1:]
    return pl.pallas_call(
        functools.partial(add_kernel, len(terms)),
        out_shape=[jax.ShapeDtypeStruct(shape, dtype) for dtype in dtypes],
        grid=(1,),
        in_specs=[pl.BlockSpec(shape, lambda t, k=k: (k, 0, 0)) for _, k in terms],
        out_specs=[pl.BlockSpec(shape, lambda t: (0, 0, 0)) for _ in dtypes],
        compiler_params=PARAMS,
        cost_estimate=FREE,
    )(*[array for array, _ in terms])


def masked(value, step, begin, row_begin, reach, width, norm_scale):
    row = lax.broadcasted_iota(jnp.int32, value.shape, 0) + row_begin
    col = lax.broadcasted_iota(jnp.int32, value.shape, 1) + begin
    distance = jnp.abs(step * width + col - row)
    return jnp.where((distance > 0) & (distance < reach), value * norm_scale, 0.0)


def add_up(terms, row_count, columns):
    value = functools.reduce(lambda x, y: x + y, [t[0].astype(jnp.float32) for t in terms])
    return value.reshape(row_count, columns, LAGS)


def early_kernel(norm_scale, scalars, *refs):
    terms, out = refs[:-1], refs[-1]
    _, row_count, width, _ = out.shape
    slots = pl.num_programs(0)
    slot = pl.program_id(0)
    out[...] = jnp.zeros_like(out)

    @pl.when(scalars[slot] == 0)
    def _():
        value = add_up(terms, row_count, width)
        row_begin = scalars[2 * slots] * row_count
        out[0] = masked(value, 0, 0, row_begin, scalars[slots + slot], width, norm_scale)


def late_kernel(shapes, slots, norm_scale, scalars, *refs):
    out, tiles, sems = refs[-3:]
    _, row_count, width, _ = out.shape
    row_begin = scalars[2 * slots] * row_count
    at = 0
    copies = []
    for place, (step, parts) in enumerate(shapes):
        slot, found = jnp.int32(0), jnp.int32(0)
        for k in range(slots):
            here = (scalars[k] == step).astype(jnp.int32)
            slot, found = slot + k * here, found + here
        reach = scalars[slots + slot]
        copy = pltpu.make_async_copy(tiles.at[place], out.at[slot], sems.at[place])
        listed = []
        begin = 0
        for term_count, columns in parts:
            listed.append((refs[at : at + term_count], begin, columns))
            at += term_count
            begin += columns

        @pl.when(found > 0)
        def _(listed=listed, step=step, reach=reach, place=place, copy=copy):
            for terms, begin, columns in listed:
                value = add_up(terms, row_count, columns)
                tiles[place, :, pl.ds(begin, columns), :] = masked(
                    value, step, begin, row_begin, reach, width, norm_scale
                )
            copy.start()

        copies.append((found, copy))
    for found, copy in copies:
        pl.when(found > 0)(copy.wait)


def owner_spec(term):
    return pl.BlockSpec((1,) + term.shape[1:], lambda t, sc: (0, 0, 0))


def write_early(scalars, terms, slots, row_count, width, norm_scale):
    return pl.pallas_call(
        functools.partial(early_kernel, norm_scale),
        out_shape=jax.ShapeDtypeStruct((slots, row_count, width, LAGS), jnp.float32),
        grid_spec=pltpu.PrefetchScalarGridSpec(
            num_scalar_prefetch=1,
            grid=(slots,),
            in_specs=[owner_spec(term) for term in terms],
            out_specs=pl.BlockSpec((1, row_count, width, LAGS), lambda t, sc: (t, 0, 0, 0)),
        ),
        compiler_params=PARAMS,
        cost_estimate=FREE,
    )(scalars, *terms)


def write_late(scalars, values, out, norm_scale):
    slots, row_count, width, _ = out.shape
    shapes = [(step, [(len(terms), columns) for columns, terms in parts]) for step, parts in values]
    operands = [term for _, parts in values for _, terms in parts for term in terms]
    return pl.pallas_call(
        functools.partial(late_kernel, shapes, slots, norm_scale),
        out_shape=jax.ShapeDtypeStruct(out.shape, out.dtype),
        grid_spec=pltpu.PrefetchScalarGridSpec(
            num_scalar_prefetch=1,
            grid=(1,),
            in_specs=[owner_spec(term) for term in operands] + [ANY],
            out_specs=ANY,
            scratch_shapes=[
                pltpu.VMEM((len(values), row_count, width, LAGS), jnp.float32),
                pltpu.SemaphoreType.DMA((len(values),)),
            ],
        ),
        input_output_aliases={len(operands) + 1: 0},
        compiler_params=PARAMS,
        cost_estimate=FREE,
    )(scalars, *operands, out)


def on_device(spectra, tile_offset, pair_reach):
    blocks = lax.axis_size("chan")
    days, cores = lax.axis_size("day"), lax.axis_size("sub")
    steps = min(MAX_STEPS, blocks - 1)
    wraps = blocks >= 3 and steps == blocks - 1
    local_days, local_windows, width, _, bins = spectra.shape
    norm_scale = 1.0 / math.sqrt(bins * local_days * days * local_windows * cores)
    row_count = width // (days * cores)
    slots = tile_offset.shape[1]
    day, core, block = lax.axis_index("day"), lax.axis_index("sub"), lax.axis_index("chan")
    table = jnp.asarray(lag_table(bins))

    half = width // 2
    halves = [
        jnp.transpose(spectra[:, :, at : at + half], (3, 0, 1, 2, 4)).reshape(2, -1, half, bins)
        for at in (0, half)
    ]

    is_last = (block == blocks - 1).astype(jnp.int32) if wraps else jnp.int32(0)
    scalars = jnp.stack([core, day, is_last]).astype(jnp.int32)
    slot_scalars = jnp.concatenate([tile_offset[0], pair_reach[0], (day * cores + core).reshape(1)])

    def reduce_tile(keep, sends):
        got = [lax.ppermute(send, "sub", [(k, (k + 1) % cores) for k in range(cores)]) for send in sends]
        terms, pieces = [(keep, 0), (got[0], 0)], []
        for shift in range(1, days):
            (piece,) = add_terms([(keep, shift), (got[shift], 0)], [jnp.bfloat16])
            pieces.append(piece)
            moved = lax.ppermute(piece, "day", [(k, (k + shift) % days) for k in range(days)])
            terms.append((moved, 0))
        return terms, pieces

    keep, sends, own_rows = own_tile(scalars, halves, table, days)
    own_terms, _ = reduce_tile(keep, sends)
    out = write_early(slot_scalars, [a for a, _ in own_terms], slots, row_count, width, norm_scale)

    values = []
    moving = halves
    for step in range(1, steps + 1 - wraps):
        pairs = [(a + 1, a) for a in range(blocks - step)]
        if wraps and step == 1:
            pairs.append((0, blocks - 1))
        if step == 2:
            moving = [lax.optimization_barrier((part, sends[0]))[0] for part in moving]
        moving = [lax.ppermute(part, "chan", pairs) for part in moving]
        if step == 1:
            keep, sends1 = partner_tile(scalars, own_rows, moving, table, days, wraps, [])
            terms, pieces = reduce_tile(keep, sends1)
            if wraps:
                total, narrow = add_terms(terms, [jnp.float32, jnp.bfloat16])
                terms = [(total, 0)]
                back = lax.ppermute(narrow, "chan", [(blocks - 1, 0)])
            values.append((step, [(width, [a for a, _ in terms])]))
        else:
            listed = []
            for at, part in enumerate(moving):
                after = pieces if at else []
                keep, sends2 = partner_tile(scalars, own_rows, [part], table, days, False, after)
                terms, _ = reduce_tile(keep, sends2)
                listed.append((half, [a for a, _ in terms]))
            values.append((step, listed))
    if wraps:
        values.append((steps, [(width, [back])]))
    return write_late(slot_scalars, values, out, norm_scale)[None]


def solution(mesh):
    in_specs = (P(("groups", "day"), "sub", "chan", None, None), P("chan", None), P("chan", None))
    out_specs = P(("groups", "chan"), None, ("day", "sub"), None, None)
    return jax.shard_map(
        on_device, mesh=mesh, in_specs=in_specs, out_specs=out_specs, check_vma=False
    )
```

```python
import functools
import math

import jax
import jax.numpy as jnp
import ml_dtypes
import numpy as np
from jax import lax
from jax.experimental import pallas as pl
from jax.experimental.pallas import tpu as pltpu
from jax.sharding import PartitionSpec as P

BAND = 32
LAGS = 256
MAX_STEPS = 4
EPSILON = 1e-06
LANES = 128
ROWS = 16
OWN = 4
VMEM_LIMIT = 40 << 20
FAR = 1 << 20
HALVES = 2
SLOT_AT = 4


def lag_table(bin_count):
    bins = np.arange(bin_count, dtype=np.float64)[:, None]
    lags = np.arange(LAGS, dtype=np.float64)[None, :] - LAGS // 2
    angle = np.pi * bins * lags / bin_count
    table = np.concatenate([np.cos(angle), -np.sin(angle)], axis=0).astype(np.float32)
    return table.astype(ml_dtypes.bfloat16)


def whiten(source):
    _, windows, channels, bins = source.shape
    width = 2 * LANES
    row = lax.broadcasted_iota(jnp.int32, (width, width), 0) // BAND
    col = lax.broadcasted_iota(jnp.int32, (width, width), 1) // BAND
    mean_matrix = jnp.where(row == col, 1.0 / BAND, 0.0).astype(jnp.bfloat16)
    for at in range(0, bins, width):
        lanes = pl.ds(at, width)
        real = source[0, :, :, lanes].astype(jnp.float32).reshape(windows * channels, width)
        imag = source[1, :, :, lanes].astype(jnp.float32).reshape(windows * channels, width)
        rest = real * real + imag * imag
        mean = jnp.zeros_like(rest)
        for _ in range(3):
            piece = rest.astype(jnp.bfloat16)
            mean += jnp.dot(piece, mean_matrix, preferred_element_type=jnp.float32)
            rest = rest - piece.astype(jnp.float32)
        scale = lax.rsqrt(mean + EPSILON)
        shape = (windows, channels, width)
        yield (
            lanes,
            (real * scale).astype(jnp.bfloat16).astype(jnp.float32).reshape(shape),
            (imag * scale).astype(jnp.bfloat16).astype(jnp.float32).reshape(shape),
        )


def row_factors(real, imag):
    return real + imag, real, imag


def col_factors(real, imag):
    return real, -(real + imag), real - imag


def store_factors(source, target, begin, factors):
    for lanes, real, imag in whiten(source):
        for k, value in enumerate(factors(real, imag)):
            target[k, :, pl.ds(begin, source.shape[2]), lanes] = value


def reach_of(scalars, step):
    slots = (scalars.shape[0] - SLOT_AT) // 2
    picked = [
        jnp.where(scalars[SLOT_AT + k] == step, scalars[SLOT_AT + slots + k], 0) for k in range(slots)
    ]
    return functools.reduce(lambda x, y: x + y, picked)


def cross_tile(rows, cols, cross, reach, first_distance):
    _, windows, row_count, bins = rows.shape
    groups = cols.shape[2] // ROWS

    def body(step, carry):
        row_at = pl.multiple_of((step // groups) * 8, 8)
        group = step % groups
        col_at = pl.multiple_of(group * ROWS, ROWS)
        nearest = first_distance + col_at - row_at
        active = (nearest - 7 < reach) & (-(nearest + ROWS - 1) < reach)

        @pl.when(active)
        def _():
            for at in range(0, bins, LANES):
                lanes = pl.ds(at, LANES)
                for first in range(0, 8, OWN):
                    sums = [[None] * 3 for _ in range(OWN)]
                    for w in range(windows):
                        for k in range(3):
                            right = cols[k, w, pl.ds(col_at, ROWS), lanes]
                            left = rows.at[k, w, pl.ds(row_at, 8), lanes]
                            for i in range(OWN):
                                product = right * left[pl.ds(first + i, 1)]
                                sums[i][k] = product if w == 0 else sums[i][k] + product
                    for i in range(OWN):
                        k1, k2, k3 = sums[i]
                        at_row = (group * row_count + row_at + first + i) * ROWS
                        place = pl.ds(pl.multiple_of(at_row, ROWS), ROWS)
                        cross[place, pl.ds(at, LANES)] = (k1 - k3).astype(jnp.bfloat16)
                        cross[place, pl.ds(bins + at, LANES)] = (k1 + k2).astype(jnp.bfloat16)

        return carry

    lax.fori_loop(0, (row_count // 8) * groups, body, 0)


def lag_block(core, cross, begin, table, size, store):
    place = pl.ds(pl.multiple_of(begin, 2 * size), 2 * size)
    lags = jnp.dot(cross[place], table[...], preferred_element_type=jnp.float32)
    low, high = lags[:size], lags[size:]
    pl.when(core == 0)(lambda: store(low, high.astype(jnp.bfloat16)))
    pl.when(core != 0)(lambda: store(high, low.astype(jnp.bfloat16)))


def store_at(keep, sends, shift, half):
    def store(kept, sent):
        size = sent.shape[0]
        keep[shift, pl.ds(half * size, size)] = kept
        sends[shift * HALVES + half][0] = sent

    return store


def lag_sums(scalars, cross, table, keep, sends):
    owners, size = keep.shape[0], keep.shape[1] // HALVES
    core, day = scalars[0], scalars[1]
    for shift in range(owners):
        owner = lax.rem(day + shift, owners)
        for half in range(HALVES):
            begin = (half * owners + owner) * (2 * size)
            lag_block(core, cross, begin, table, size, store_at(keep, sends, shift, half))


def begins_of(parts):
    return [sum(p.shape[2] for p in parts[:k]) for k in range(len(parts))]


def own_kernel(part_count, scalars, table, *refs):
    parts = refs[:part_count]
    keep, *sends, rows, cols, cross = refs[part_count:]
    for part, begin in zip(parts, begins_of(parts)):
        for lanes, real, imag in whiten(part):
            for k in range(3):
                rows[k, :, pl.ds(begin, part.shape[2]), lanes] = row_factors(real, imag)[k]
                cols[k, :, pl.ds(begin, part.shape[2]), lanes] = col_factors(real, imag)[k]
    cross_tile(rows, cols, cross, reach_of(scalars, 0), 0)
    lag_sums(scalars, cross, table, keep, sends)


def partner_kernel(part_count, after_count, step, scalars, own_rows, table, *refs):
    parts = refs[:part_count]
    keep, *sends, cols, cross = refs[part_count + after_count :]
    reach = reach_of(scalars, step)

    @pl.when(reach > 0)
    def _():
        for part, begin in zip(parts, begins_of(parts)):
            store_factors(part, cols, begin, col_factors)
        cross_tile(own_rows, cols, cross, reach, step * own_rows.shape[2])
        lag_sums(scalars, cross, table, keep, sends)


def half_cross(can_swap, step, half, scalars, own_rows, part, cols, cross, swap_refs, finish):
    width, count = own_rows.shape[2], part.shape[2]
    reach = reach_of(scalars, step)

    @pl.when(reach > 0)
    def _():
        store_factors(part, cols, 0, col_factors)
        cross_tile(own_rows, cols, cross, reach, step * width + half * count)
        finish(False)

    if can_swap:
        rows, wide_cols = swap_refs

        @pl.when(scalars[2] != 0)
        def _():
            for at in range(0, own_rows.shape[3], LANES):
                lanes = pl.ds(at, LANES)
                real, imag = own_rows[1, :, :, lanes], own_rows[2, :, :, lanes]
                for k, value in enumerate(col_factors(real, imag)):
                    wide_cols[k, :, :, lanes] = value
            store_factors(part, rows, 0, row_factors)
            cross_tile(rows, wide_cols, cross, FAR, 0)
            finish(True)


def first_half_kernel(can_swap, step, scalars, own_rows, table, part, keep, send, cols, cross, *swap_refs):
    owners, size = keep.shape[0], keep.shape[1]

    def finish(swapped):
        for k in range(owners):

            def store(kept, sent, k=k):
                keep[k] = kept
                send[k] = sent

            lag_block(scalars[0], cross, k * 2 * size, table, size, store)

    half_cross(can_swap, step, 0, scalars, own_rows, part, cols, cross, swap_refs, finish)


def second_half_kernel(
    can_swap, step, after_count, scalars, own_rows, table, part, first_keep, first_send, *refs
):
    keep, *refs = refs[after_count:]
    sends = refs[: keep.shape[0] * HALVES]
    cols, cross, *swap_refs = refs[keep.shape[0] * HALVES :]
    owners, size = keep.shape[0], keep.shape[1] // HALVES
    core, day = scalars[0], scalars[1]

    def finish(swapped):
        for shift in range(owners):
            owner = lax.rem(day + shift, owners)
            if not swapped:
                store_at(keep, sends, shift, 0)(first_keep[owner], first_send[owner])
                lag_block(core, cross, owner * 2 * size, table, size, store_at(keep, sends, shift, 1))
                continue
            for half in range(HALVES):
                store = store_at(keep, sends, shift, half)
                pl.when(owner == 0)(lambda store=store, half=half: store(first_keep[half], first_send[half]))
                pl.when(owner != 0)(
                    lambda store=store, half=half: lag_block(
                        core, cross, half * 2 * size, table, size, store
                    )
                )

    half_cross(can_swap, step, 1, scalars, own_rows, part, cols, cross, swap_refs, finish)


VMEM = pl.BlockSpec(memory_space=pltpu.VMEM)
SMEM = pl.BlockSpec(memory_space=pltpu.SMEM)
ANY = pl.BlockSpec(memory_space=pl.ANY)
FREE = pl.CostEstimate(flops=0, bytes_accessed=0, transcendentals=0)
PARAMS = pltpu.CompilerParams(vmem_limit_bytes=VMEM_LIMIT)


def sums_shapes(owners, width):
    size = width * width // (2 * owners * HALVES)
    return [jax.ShapeDtypeStruct((owners, HALVES * size, LAGS), jnp.float32)] + [
        jax.ShapeDtypeStruct((1, size, LAGS), jnp.bfloat16)
    ] * (owners * HALVES)


def own_tile(scalars, parts, table, owners):
    _, windows, _, bins = parts[0].shape
    width = sum(part.shape[2] for part in parts)
    factors = (3, windows, width, bins)
    keep, *sends, rows = pl.pallas_call(
        functools.partial(own_kernel, len(parts)),
        out_shape=sums_shapes(owners, width) + [jax.ShapeDtypeStruct(factors, jnp.float32)],
        in_specs=[SMEM] + [VMEM] * (1 + len(parts)),
        out_specs=[VMEM] * (owners * HALVES + 2),
        scratch_shapes=[
            pltpu.VMEM(factors, jnp.float32),
            pltpu.VMEM((width * width, 2 * bins), jnp.bfloat16),
        ],
        compiler_params=PARAMS,
        cost_estimate=FREE,
    )(scalars, table, *parts)
    return keep, sends, rows


def partner_tile(scalars, own_rows, parts, table, owners, step, after):
    _, windows, width, bins = own_rows.shape
    keep, *sends = pl.pallas_call(
        functools.partial(partner_kernel, len(parts), len(after), step),
        out_shape=sums_shapes(owners, width),
        in_specs=[SMEM] + [VMEM] * (2 + len(parts)) + [ANY] * len(after),
        out_specs=[VMEM] * (owners * HALVES + 1),
        scratch_shapes=[
            pltpu.VMEM((3, windows, width, bins), jnp.float32),
            pltpu.VMEM((width * width, 2 * bins), jnp.bfloat16),
        ],
        compiler_params=PARAMS,
        cost_estimate=FREE,
    )(scalars, own_rows, table, *parts, *after)
    return keep, sends


def half_scratch(own_rows, can_swap):
    _, windows, width, bins = own_rows.shape
    half = width // HALVES
    wide, narrow = (3, windows, width, bins), (3, windows, half, bins)
    scratch = [pltpu.VMEM(narrow, jnp.float32), pltpu.VMEM((width * half, 2 * bins), jnp.bfloat16)]
    if can_swap:
        scratch += [pltpu.VMEM(narrow, jnp.float32), pltpu.VMEM(wide, jnp.float32)]
    return scratch


def first_half_tile(scalars, own_rows, part, table, owners, step, can_swap):
    width = own_rows.shape[2]
    size = width * width // (2 * owners * HALVES)
    return pl.pallas_call(
        functools.partial(first_half_kernel, can_swap, step),
        out_shape=[
            jax.ShapeDtypeStruct((owners, size, LAGS), jnp.float32),
            jax.ShapeDtypeStruct((owners, size, LAGS), jnp.bfloat16),
        ],
        in_specs=[SMEM, VMEM, VMEM, VMEM],
        out_specs=[VMEM, VMEM],
        scratch_shapes=half_scratch(own_rows, can_swap),
        compiler_params=PARAMS,
        cost_estimate=FREE,
    )(scalars, own_rows, table, part)


def second_half_tile(scalars, own_rows, part, first, table, owners, step, can_swap, after):
    keep, *sends = pl.pallas_call(
        functools.partial(second_half_kernel, can_swap, step, len(after)),
        out_shape=sums_shapes(owners, own_rows.shape[2]),
        in_specs=[SMEM] + [VMEM] * 5 + [ANY] * len(after),
        out_specs=[VMEM] * (owners * HALVES + 1),
        scratch_shapes=half_scratch(own_rows, can_swap),
        compiler_params=PARAMS,
        cost_estimate=FREE,
    )(scalars, own_rows, table, part, *first, *after)
    return keep, sends


def add_kernel(tiles, shift, *refs):
    out = refs[-1]
    for tile in range(tiles):
        keep, *got = refs[tile * (1 + HALVES) : (tile + 1) * (1 + HALVES)]
        for half, sent in enumerate(got):
            place = pl.ds(half * sent.shape[1], sent.shape[1])
            out[tile, place] = (keep[shift, place] + sent[0].astype(jnp.float32)).astype(out.dtype)


def add_cores(tiles, shift, after=()):
    operands = [term for keep, got in tiles for term in [keep] + got[shift]]
    rows = tiles[0][0].shape[1]
    return pl.pallas_call(
        functools.partial(add_kernel, len(tiles), shift),
        out_shape=jax.ShapeDtypeStruct((len(tiles), rows, LAGS), jnp.bfloat16),
        in_specs=[VMEM] * len(operands) + [ANY] * len(after),
        out_specs=VMEM,
        compiler_params=PARAMS,
        cost_estimate=FREE,
    )(*operands, *after)


def write_tile(scalars, step, terms, tile, norm_scale):
    row_count, width, _ = tile.shape
    slots = (scalars.shape[0] - SLOT_AT) // 2
    reach = reach_of(scalars, step)
    half_width = width // HALVES
    size = row_count * half_width
    for half in range(HALVES):
        value = None
        for term in terms:
            if isinstance(term, list):
                part = term[half][0]
            else:
                array, at = term
                part = array[at, pl.ds(half * size, size)]
            part = part.astype(jnp.float32)
            value = part if value is None else value + part
        value = value.reshape(row_count, half_width, LAGS)
        row = lax.broadcasted_iota(jnp.int32, value.shape, 0) + scalars[3] * row_count
        col = lax.broadcasted_iota(jnp.int32, value.shape, 1) + half * half_width
        distance = jnp.abs(step * width + col - row)
        kept = (distance > 0) & (distance < reach)
        tile[:, pl.ds(half * half_width, half_width), :] = jnp.where(kept, value * norm_scale, 0.0)


def grouped(refs, counts):
    terms = []
    for at, count in counts:
        if at is not None:
            terms.append((refs.pop(0), at))
        else:
            terms.append([refs.pop(0) for _ in range(count)])
    return terms


def tile_kernel(step, counts, norm_scale, scalars, *refs):
    *terms, tile = refs
    write_tile(scalars, step, grouped(terms, counts), tile, norm_scale)


def flat(terms):
    operands, counts = [], []
    for term in terms:
        listed = isinstance(term, list)
        operands += term if listed else [term[0]]
        counts.append((None, len(term)) if listed else (term[1], 1))
    return operands, counts


def finished_tile(scalars, step, terms, row_count, width, norm_scale):
    operands, counts = flat(terms)
    return pl.pallas_call(
        functools.partial(tile_kernel, step, counts, norm_scale),
        out_shape=jax.ShapeDtypeStruct((row_count, width, LAGS), jnp.float32),
        in_specs=[SMEM] + [VMEM] * len(operands),
        out_specs=VMEM,
        compiler_params=PARAMS,
        cost_estimate=FREE,
    )(scalars, *operands)


def output_kernel(ready_steps, late, norm_scale, scalars, *refs):
    out, tiles, zeros, sems = refs[-4:]
    slots = out.shape[0]
    ready, rest = refs[: len(ready_steps)], list(refs[len(ready_steps) : -4])

    def copies(slot, source):
        return pltpu.make_async_copy(source, out.at[slot], sems.at[slot])

    def start(step, source):
        for slot in range(slots):
            pl.when(scalars[SLOT_AT + slot] == step)(copies(slot, source).start)

    for step, tile in zip(ready_steps, ready):
        start(step, tile)
    zeros[...] = jnp.zeros_like(zeros)
    start(-1, zeros)
    for place, (step, counts) in enumerate(late):
        terms = grouped(rest, counts)

        @pl.when(reach_of(scalars, step) > 0)
        def _(step=step, terms=terms, place=place):
            write_tile(scalars, step, terms, tiles.at[place], norm_scale)

        start(step, tiles.at[place])
    for slot in range(slots):
        copies(slot, zeros).wait()


def write_output(scalars, ready, late, slots, norm_scale):
    tile_shape = ready[0][1].shape
    operands, listed = [tile for _, tile in ready], []
    for step, terms in late:
        more, counts = flat(terms)
        operands += more
        listed.append((step, counts))
    return pl.pallas_call(
        functools.partial(output_kernel, [step for step, _ in ready], listed, norm_scale),
        out_shape=jax.ShapeDtypeStruct((slots,) + tile_shape, jnp.float32),
        in_specs=[SMEM] + [VMEM] * len(operands),
        out_specs=ANY,
        scratch_shapes=[
            pltpu.VMEM((len(late),) + tile_shape, jnp.float32),
            pltpu.VMEM(tile_shape, jnp.float32),
            pltpu.SemaphoreType.DMA((slots,)),
        ],
        compiler_params=PARAMS,
        cost_estimate=FREE,
    )(scalars, *operands)


def on_device(spectra, tile_offset, pair_reach):
    blocks = lax.axis_size("chan")
    days, cores = lax.axis_size("day"), lax.axis_size("sub")
    steps = min(MAX_STEPS, blocks - 1)
    wraps = blocks >= 3 and steps == blocks - 1 and days == 2
    local_days, local_windows, width, _, bins = spectra.shape
    norm_scale = 1.0 / math.sqrt(bins * local_days * days * local_windows * cores)
    row_count = width // (days * cores)
    slots = tile_offset.shape[1]
    day, core, block = lax.axis_index("day"), lax.axis_index("sub"), lax.axis_index("chan")
    table = jnp.asarray(lag_table(bins))

    half = width // HALVES
    halves = [
        jnp.transpose(spectra[:, :, at : at + half], (3, 0, 1, 2, 4)).reshape(2, -1, half, bins)
        for at in range(0, width, half)
    ]
    is_last = (block == blocks - 1).astype(jnp.int32) if wraps else jnp.int32(0)
    scalars = jnp.stack([core, day, is_last, day * cores + core]).astype(jnp.int32)
    scalars = jnp.concatenate([scalars, tile_offset[0], pair_reach[0]])

    def over_cores(sends):
        got = [lax.ppermute(send, "sub", [(k, (k + 1) % cores) for k in range(cores)]) for send in sends]
        return [got[k * HALVES : (k + 1) * HALVES] for k in range(days)]

    def over_days(pieces):
        return [
            lax.ppermute(piece, "day", [(k, (k + shift) % days) for k in range(days)])
            for shift, piece in enumerate(pieces, 1)
        ]

    def to_first(piece, shift):
        pairs = [((blocks - 1) * days + k, (k + shift) % days) for k in range(days)]
        return lax.ppermute(piece, ("chan", "day"), pairs)

    keep, sends, own_rows = own_tile(scalars, halves, table, days)
    own_sums = (keep, over_cores(sends))
    ready, late, back = [], [], []

    pairs = [(a + 1, a) for a in range(blocks - 1)] + [(0, blocks - 1)] * wraps
    moving = [lax.ppermute(part, "chan", pairs) for part in halves]
    first = first_half_tile(scalars, own_rows, moving[0], table, days, 1, wraps)
    ahead = moving
    after = [x for pair in own_sums[1] for x in pair] if 0 else []
    keep, sends1 = second_half_tile(scalars, own_rows, moving[1], first, table, days, 1, wraps, after)
    sums = (keep, over_cores(sends1))
    pieces = [add_cores([sums, own_sums], shift) for shift in range(1, days)]
    if wraps:
        back = [to_first(add_cores([sums], shift), shift) for shift in range(days)]
    moved = over_days(pieces)
    for step, (keep, got) in enumerate([own_sums, sums]):
        terms = [(keep, 0), got[0]] + [(piece, 1 - step) for piece in moved]
        ready.append((step, finished_tile(scalars, step, terms, row_count, width, norm_scale)))

    waits = [sends[0], first[0]]
    for step in range(2, steps + 1 - wraps):
        pairs = [(a + 1, a) for a in range(blocks - step)]
        ahead = [
            lax.ppermute(lax.optimization_barrier((part, wait))[0], "chan", pairs)
            for part, wait in zip(ahead, waits)
        ]
        keep, sends2 = partner_tile(scalars, own_rows, ahead, table, days, step, pieces)
        sums = (keep, over_cores(sends2))
        last = [add_cores([sums], shift, back) for shift in range(1, days)]
        terms = [(keep, 0), sums[1][0]] + [(piece, 0) for piece in over_days(last)]
        late.append((step, terms))
    if wraps:
        late.append((steps, [(piece, 0) for piece in back]))
    return write_output(scalars, ready, late, slots, norm_scale)[None]


def solution(mesh):
    in_specs = (P(("groups", "day"), "sub", "chan", None, None), P("chan", None), P("chan", None))
    out_specs = P(("groups", "chan"), None, ("day", "sub"), None, None)
    return jax.shard_map(
        on_device, mesh=mesh, in_specs=in_specs, out_specs=out_specs, check_vma=False
    )
```

```python
import functools
import math

import jax
import jax.numpy as jnp
import ml_dtypes
import numpy as np
from jax import lax
from jax.experimental import pallas as pl
from jax.experimental.pallas import tpu as pltpu
from jax.sharding import PartitionSpec as P

BAND = 32
LAGS = 256
MAX_STEPS = 4
EPSILON = 1e-06
LANES = 128
ROWS = 16
OWN = 4
VMEM_LIMIT = 40 << 20
FAR = 1 << 20
HALVES = 2
SETTLED = 144
SLOT_AT = 4


def lag_table(bin_count):
    bins = np.arange(bin_count, dtype=np.float64)[:, None]
    lags = np.arange(LAGS, dtype=np.float64)[None, :] - LAGS // 2
    angle = np.pi * bins * lags / bin_count
    table = np.concatenate([np.cos(angle), -np.sin(angle)], axis=0).astype(np.float32)
    return table.astype(ml_dtypes.bfloat16)


def whiten(source):
    _, windows, channels, bins = source.shape
    width = 2 * LANES
    row = lax.broadcasted_iota(jnp.int32, (width, width), 0) // BAND
    col = lax.broadcasted_iota(jnp.int32, (width, width), 1) // BAND
    mean_matrix = jnp.where(row == col, 1.0 / BAND, 0.0).astype(jnp.bfloat16)
    for at in range(0, bins, width):
        lanes = pl.ds(at, width)
        real = source[0, :, :, lanes].astype(jnp.float32).reshape(windows * channels, width)
        imag = source[1, :, :, lanes].astype(jnp.float32).reshape(windows * channels, width)
        rest = real * real + imag * imag
        mean = jnp.zeros_like(rest)
        for _ in range(3):
            piece = rest.astype(jnp.bfloat16)
            mean += jnp.dot(piece, mean_matrix, preferred_element_type=jnp.float32)
            rest = rest - piece.astype(jnp.float32)
        scale = lax.rsqrt(mean + EPSILON)
        shape = (windows, channels, width)
        yield (
            lanes,
            (real * scale).astype(jnp.bfloat16).astype(jnp.float32).reshape(shape),
            (imag * scale).astype(jnp.bfloat16).astype(jnp.float32).reshape(shape),
        )


def row_factors(real, imag):
    return real + imag, real, imag


def col_factors(real, imag):
    return real, -(real + imag), real - imag


def store_factors(source, target, begin, factors):
    for lanes, real, imag in whiten(source):
        for k, value in enumerate(factors(real, imag)):
            target[k, :, pl.ds(begin, source.shape[2]), lanes] = value


def reach_of(scalars, step):
    slots = (scalars.shape[1] - SLOT_AT) // 2
    picked = [
        jnp.where(scalars[0, SLOT_AT + k] == step, scalars[0, SLOT_AT + slots + k], 0) for k in range(slots)
    ]
    return functools.reduce(lambda x, y: x + y, picked)


def cross_tile(rows, cols, cross, reach, first_distance):
    _, windows, row_count, bins = rows.shape
    groups = cols.shape[2] // ROWS

    def body(step, carry):
        row_at = pl.multiple_of((step // groups) * 8, 8)
        group = step % groups
        col_at = pl.multiple_of(group * ROWS, ROWS)
        nearest = first_distance + col_at - row_at
        active = (nearest - 7 < reach) & (-(nearest + ROWS - 1) < reach)

        @pl.when(active)
        def _():
            for at in range(0, bins, LANES):
                lanes = pl.ds(at, LANES)
                for first in range(0, 8, OWN):
                    sums = [[None] * 3 for _ in range(OWN)]
                    for w in range(windows):
                        for k in range(3):
                            right = cols[k, w, pl.ds(col_at, ROWS), lanes]
                            left = rows.at[k, w, pl.ds(row_at, 8), lanes]
                            for i in range(OWN):
                                product = right * left[pl.ds(first + i, 1)]
                                sums[i][k] = product if w == 0 else sums[i][k] + product
                    for i in range(OWN):
                        k1, k2, k3 = sums[i]
                        at_row = (group * row_count + row_at + first + i) * ROWS
                        place = pl.ds(pl.multiple_of(at_row, ROWS), ROWS)
                        cross[place, pl.ds(at, LANES)] = (k1 - k3).astype(jnp.bfloat16)
                        cross[place, pl.ds(bins + at, LANES)] = (k1 + k2).astype(jnp.bfloat16)

        return carry

    lax.fori_loop(0, (row_count // 8) * groups, body, 0)


def lag_block(core, cross, begin, table, size, store):
    place = pl.ds(pl.multiple_of(begin, 2 * size), 2 * size)
    lags = jnp.dot(cross[place], table[...], preferred_element_type=jnp.float32)
    low, high = lags[:size], lags[size:]
    pl.when(core == 0)(lambda: store(low, high.astype(jnp.bfloat16)))
    pl.when(core != 0)(lambda: store(high, low.astype(jnp.bfloat16)))


def store_at(keep, sends, shift, half):
    def store(kept, sent):
        size = sent.shape[0]
        keep[shift, pl.ds(half * size, size)] = kept
        sends[shift * HALVES + half][0] = sent

    return store


def lag_sums(scalars, cross, table, keep, sends):
    owners, size = keep.shape[0], keep.shape[1] // HALVES
    core, day = scalars[0, 0], scalars[0, 1]
    for shift in range(owners):
        owner = lax.rem(day + shift, owners)
        for half in range(HALVES):
            begin = (half * owners + owner) * (2 * size)
            lag_block(core, cross, begin, table, size, store_at(keep, sends, shift, half))


def begins_of(parts):
    return [sum(p.shape[2] for p in parts[:k]) for k in range(len(parts))]


def own_kernel(part_count, scalars, table, *refs):
    parts = refs[:part_count]
    keep, *sends, rows, cols, cross = refs[part_count:]
    for part, begin in zip(parts, begins_of(parts)):
        for lanes, real, imag in whiten(part):
            for k in range(3):
                rows[k, :, pl.ds(begin, part.shape[2]), lanes] = row_factors(real, imag)[k]
                cols[k, :, pl.ds(begin, part.shape[2]), lanes] = col_factors(real, imag)[k]
    cross_tile(rows, cols, cross, reach_of(scalars, 0), 0)
    lag_sums(scalars, cross, table, keep, sends)


def partner_kernel(part_count, after_count, step, scalars, own_rows, table, *refs):
    parts = refs[:part_count]
    keep, *sends, cols, cross = refs[part_count + after_count :]
    reach = reach_of(scalars, step)

    @pl.when(reach > 0)
    def _():
        for part, begin in zip(parts, begins_of(parts)):
            store_factors(part, cols, begin, col_factors)
        cross_tile(own_rows, cols, cross, reach, step * own_rows.shape[2])
        lag_sums(scalars, cross, table, keep, sends)


def half_cross(can_swap, step, half, scalars, own_rows, part, cols, cross, swap_refs, finish):
    width, count = own_rows.shape[2], part.shape[2]
    reach = reach_of(scalars, step)

    @pl.when(reach > 0)
    def _():
        store_factors(part, cols, 0, col_factors)
        cross_tile(own_rows, cols, cross, reach, step * width + half * count)
        finish(False)

    if can_swap:
        rows, wide_cols = swap_refs

        @pl.when(scalars[0, 2] != 0)
        def _():
            for at in range(0, own_rows.shape[3], LANES):
                lanes = pl.ds(at, LANES)
                real, imag = own_rows[1, :, :, lanes], own_rows[2, :, :, lanes]
                for k, value in enumerate(col_factors(real, imag)):
                    wide_cols[k, :, :, lanes] = value
            store_factors(part, rows, 0, row_factors)
            cross_tile(rows, wide_cols, cross, FAR, 0)
            finish(True)


def first_half_kernel(can_swap, step, scalars, own_rows, table, part, keep, send, cols, cross, *swap_refs):
    owners, size = keep.shape[0], keep.shape[1]

    def finish(swapped):
        for k in range(owners):

            def store(kept, sent, k=k):
                keep[k] = kept
                send[k] = sent

            lag_block(scalars[0, 0], cross, k * 2 * size, table, size, store)

    half_cross(can_swap, step, 0, scalars, own_rows, part, cols, cross, swap_refs, finish)


def second_half_kernel(
    can_swap, step, after_count, scalars, own_rows, table, part, first_keep, first_send, *refs
):
    keep, *refs = refs[after_count:]
    sends = refs[: keep.shape[0] * HALVES]
    cols, cross, *swap_refs = refs[keep.shape[0] * HALVES :]
    owners, size = keep.shape[0], keep.shape[1] // HALVES
    core, day = scalars[0, 0], scalars[0, 1]

    def finish(swapped):
        for shift in range(owners):
            owner = lax.rem(day + shift, owners)
            if not swapped:
                store_at(keep, sends, shift, 0)(first_keep[owner], first_send[owner])
                lag_block(core, cross, owner * 2 * size, table, size, store_at(keep, sends, shift, 1))
                continue
            for half in range(HALVES):
                store = store_at(keep, sends, shift, half)
                pl.when(owner == 0)(lambda store=store, half=half: store(first_keep[half], first_send[half]))
                pl.when(owner != 0)(
                    lambda store=store, half=half: lag_block(
                        core, cross, half * 2 * size, table, size, store
                    )
                )

    half_cross(can_swap, step, 1, scalars, own_rows, part, cols, cross, swap_refs, finish)


VMEM = pl.BlockSpec(memory_space=pltpu.VMEM)
ANY = pl.BlockSpec(memory_space=pl.ANY)
FREE = pl.CostEstimate(flops=0, bytes_accessed=0, transcendentals=0)
PARAMS = pltpu.CompilerParams(vmem_limit_bytes=VMEM_LIMIT)


def sums_shapes(owners, width):
    size = width * width // (2 * owners * HALVES)
    return [jax.ShapeDtypeStruct((owners, HALVES * size, LAGS), jnp.float32)] + [
        jax.ShapeDtypeStruct((1, size, LAGS), jnp.bfloat16)
    ] * (owners * HALVES)


def own_tile(scalars, parts, table, owners):
    _, windows, _, bins = parts[0].shape
    width = sum(part.shape[2] for part in parts)
    factors = (3, windows, width, bins)
    keep, *sends, rows = pl.pallas_call(
        functools.partial(own_kernel, len(parts)),
        out_shape=sums_shapes(owners, width) + [jax.ShapeDtypeStruct(factors, jnp.float32)],
        in_specs=[VMEM] + [VMEM] * (1 + len(parts)),
        out_specs=[VMEM] * (owners * HALVES + 2),
        scratch_shapes=[
            pltpu.VMEM(factors, jnp.float32),
            pltpu.VMEM((width * width, 2 * bins), jnp.bfloat16),
        ],
        compiler_params=PARAMS,
        cost_estimate=FREE,
    )(scalars, table, *parts)
    return keep, sends, rows


def partner_tile(scalars, own_rows, parts, table, owners, step, after):
    _, windows, width, bins = own_rows.shape
    keep, *sends = pl.pallas_call(
        functools.partial(partner_kernel, len(parts), len(after), step),
        out_shape=sums_shapes(owners, width),
        in_specs=[VMEM] + [VMEM] * (2 + len(parts)) + [ANY] * len(after),
        out_specs=[VMEM] * (owners * HALVES + 1),
        scratch_shapes=[
            pltpu.VMEM((3, windows, width, bins), jnp.float32),
            pltpu.VMEM((width * width, 2 * bins), jnp.bfloat16),
        ],
        compiler_params=PARAMS,
        cost_estimate=FREE,
    )(scalars, own_rows, table, *parts, *after)
    return keep, sends


def half_scratch(own_rows, can_swap):
    _, windows, width, bins = own_rows.shape
    half = width // HALVES
    wide, narrow = (3, windows, width, bins), (3, windows, half, bins)
    scratch = [pltpu.VMEM(narrow, jnp.float32), pltpu.VMEM((width * half, 2 * bins), jnp.bfloat16)]
    if can_swap:
        scratch += [pltpu.VMEM(narrow, jnp.float32), pltpu.VMEM(wide, jnp.float32)]
    return scratch


def first_half_tile(scalars, own_rows, part, table, owners, step, can_swap):
    width = own_rows.shape[2]
    size = width * width // (2 * owners * HALVES)
    return pl.pallas_call(
        functools.partial(first_half_kernel, can_swap, step),
        out_shape=[
            jax.ShapeDtypeStruct((owners, size, LAGS), jnp.float32),
            jax.ShapeDtypeStruct((owners, size, LAGS), jnp.bfloat16),
        ],
        in_specs=[VMEM, VMEM, VMEM, VMEM],
        out_specs=[VMEM, VMEM],
        scratch_shapes=half_scratch(own_rows, can_swap),
        compiler_params=PARAMS,
        cost_estimate=FREE,
    )(scalars, own_rows, table, part)


def second_half_tile(scalars, own_rows, part, first, table, owners, step, can_swap, after):
    keep, *sends = pl.pallas_call(
        functools.partial(second_half_kernel, can_swap, step, len(after)),
        out_shape=sums_shapes(owners, own_rows.shape[2]),
        in_specs=[VMEM] + [VMEM] * 5 + [ANY] * len(after),
        out_specs=[VMEM] * (owners * HALVES + 1),
        scratch_shapes=half_scratch(own_rows, can_swap),
        compiler_params=PARAMS,
        cost_estimate=FREE,
    )(scalars, own_rows, table, part, *first, *after)
    return keep, sends


def add_kernel(tiles, shift, *refs):
    out = refs[-1]
    for tile in range(tiles):
        keep, *got = refs[tile * (1 + HALVES) : (tile + 1) * (1 + HALVES)]
        for half, sent in enumerate(got):
            place = pl.ds(half * sent.shape[1], sent.shape[1])
            out[tile, place] = (keep[shift, place] + sent[0].astype(jnp.float32)).astype(out.dtype)


def add_cores(tiles, shift, after=()):
    operands = [term for keep, got in tiles for term in [keep] + got[shift]]
    rows = tiles[0][0].shape[1]
    return pl.pallas_call(
        functools.partial(add_kernel, len(tiles), shift),
        out_shape=jax.ShapeDtypeStruct((len(tiles), rows, LAGS), jnp.bfloat16),
        in_specs=[VMEM] * len(operands) + [ANY] * len(after),
        out_specs=VMEM,
        compiler_params=PARAMS,
        cost_estimate=FREE,
    )(*operands, *after)


def write_tile(scalars, step, terms, tile, norm_scale):
    row_count, width, _ = tile.shape
    slots = (scalars.shape[1] - SLOT_AT) // 2
    reach = reach_of(scalars, step)
    half_width = width // HALVES
    size = row_count * half_width
    for half in range(HALVES):
        value = None
        for term in terms:
            if isinstance(term, list):
                part = term[half][0]
            else:
                array, at = term
                part = array[at, pl.ds(half * size, size)]
            part = part.astype(jnp.float32)
            value = part if value is None else value + part
        value = value.reshape(row_count, half_width, LAGS)
        row = lax.broadcasted_iota(jnp.int32, value.shape, 0) + scalars[0, 3] * row_count
        col = lax.broadcasted_iota(jnp.int32, value.shape, 1) + half * half_width
        distance = jnp.abs(step * width + col - row)
        kept = (distance > 0) & (distance < reach)
        tile[:, pl.ds(half * half_width, half_width), :] = jnp.where(kept, value * norm_scale, 0.0)


def grouped(refs, counts):
    terms = []
    for at, count in counts:
        if at is not None:
            terms.append((refs.pop(0), at))
        else:
            terms.append([refs.pop(0) for _ in range(count)])
    return terms


def tile_kernel(step, counts, norm_scale, scalars, *refs):
    *terms, tile = refs
    write_tile(scalars, step, grouped(terms, counts), tile, norm_scale)


def flat(terms):
    operands, counts = [], []
    for term in terms:
        listed = isinstance(term, list)
        operands += term if listed else [term[0]]
        counts.append((None, len(term)) if listed else (term[1], 1))
    return operands, counts


def finished_tile(scalars, step, terms, row_count, width, norm_scale):
    operands, counts = flat(terms)
    return pl.pallas_call(
        functools.partial(tile_kernel, step, counts, norm_scale),
        out_shape=jax.ShapeDtypeStruct((row_count, width, LAGS), jnp.float32),
        in_specs=[VMEM] + [VMEM] * len(operands),
        out_specs=VMEM,
        compiler_params=PARAMS,
        cost_estimate=FREE,
    )(scalars, *operands)


def output_kernel(ready_steps, late, after_count, norm_scale, scalars, *refs):
    out, tiles, zeros, sems = refs[-4:]
    slots = out.shape[0]
    ready, rest = refs[: len(ready_steps)], list(refs[len(ready_steps) : -4])

    def copies(slot, source):
        return pltpu.make_async_copy(source, out.at[slot], sems.at[slot])

    def start(step, source):
        for slot in range(slots):
            pl.when(scalars[0, SLOT_AT + slot] == step)(copies(slot, source).start)

    for step, tile in zip(ready_steps, ready):
        start(step, tile)
    zeros[...] = jnp.zeros_like(zeros)
    start(-1, zeros)
    for place, (step, counts) in enumerate(late):
        terms = grouped(rest, counts)

        @pl.when(reach_of(scalars, step) > 0)
        def _(step=step, terms=terms, place=place):
            write_tile(scalars, step, terms, tiles.at[place], norm_scale)

        start(step, tiles.at[place])
    for slot in range(slots):
        copies(slot, zeros).wait()


def write_output(scalars, ready, late, slots, norm_scale, after):
    tile_shape = ready[0][1].shape
    operands, listed = [tile for _, tile in ready], []
    for step, terms in late:
        more, counts = flat(terms)
        operands += more
        listed.append((step, counts))
    return pl.pallas_call(
        functools.partial(output_kernel, [step for step, _ in ready], listed, len(after), norm_scale),
        out_shape=jax.ShapeDtypeStruct((slots,) + tile_shape, jnp.float32),
        in_specs=[VMEM] + [VMEM] * len(operands) + [ANY] * len(after),
        out_specs=ANY,
        scratch_shapes=[
            pltpu.VMEM((len(late),) + tile_shape, jnp.float32),
            pltpu.VMEM(tile_shape, jnp.float32),
            pltpu.SemaphoreType.DMA((slots,)),
        ],
        compiler_params=PARAMS,
        cost_estimate=FREE,
    )(scalars, *operands, *after)


def on_device(spectra, tile_offset, pair_reach):
    blocks = lax.axis_size("chan")
    days, cores = lax.axis_size("day"), lax.axis_size("sub")
    steps = min(MAX_STEPS, blocks - 1)
    wraps = blocks >= 3 and steps == blocks - 1 and days == 2
    local_days, local_windows, width, _, bins = spectra.shape
    norm_scale = 1.0 / math.sqrt(bins * local_days * days * local_windows * cores)
    row_count = width // (days * cores)
    slots = tile_offset.shape[1]
    day, core, block = lax.axis_index("day"), lax.axis_index("sub"), lax.axis_index("chan")
    table = jnp.asarray(lag_table(bins))

    half = width // HALVES
    halves = [
        jnp.transpose(spectra[:, :, at : at + half], (3, 0, 1, 2, 4)).reshape(2, -1, half, bins)
        for at in range(0, width, half)
    ]
    is_last = (block == blocks - 1).astype(jnp.int32) if wraps else jnp.int32(0)
    scalars = jnp.stack([core, day, is_last, day * cores + core]).astype(jnp.int32)
    scalars = jnp.concatenate([scalars, tile_offset[0], pair_reach[0]])[None]

    def over_cores(sends):
        got = [lax.ppermute(send, "sub", [(k, (k + 1) % cores) for k in range(cores)]) for send in sends]
        return [got[k * HALVES : (k + 1) * HALVES] for k in range(days)]

    def over_days(pieces):
        return [
            lax.ppermute(piece, "day", [(k, (k + shift) % days) for k in range(days)])
            for shift, piece in enumerate(pieces, 1)
        ]

    def to_first(piece, shift):
        pairs = [((blocks - 1) * days + k, (k + shift) % days) for k in range(days)]
        return lax.ppermute(piece, ("chan", "day"), pairs)

    keep, sends, own_rows = own_tile(scalars, halves, table, days)
    own_sums = (keep, over_cores(sends))
    ready, late, back, settled = [], [], [], []

    pairs = [(a + 1, a) for a in range(blocks - 1)] + [(0, blocks - 1)] * wraps
    moving = [lax.ppermute(part, "chan", pairs) for part in halves]
    first = first_half_tile(scalars, own_rows, moving[0], table, days, 1, wraps)
    ahead = moving
    after = [x for pair in own_sums[1] for x in pair] if 0 else []
    keep, sends1 = second_half_tile(scalars, own_rows, moving[1], first, table, days, 1, wraps, after)
    sums = (keep, over_cores(sends1))
    pieces = [add_cores([sums, own_sums], shift) for shift in range(1, days)]
    if wraps:
        back = [to_first(add_cores([sums], shift), shift) for shift in range(days)]
    moved = over_days(pieces)
    for step, (keep, got) in enumerate([own_sums, sums]):
        terms = [(keep, 0), got[0]] + [(piece, 1 - step) for piece in moved]
        ready.append((step, finished_tile(scalars, step, terms, row_count, width, norm_scale)))

    waits = [sends[0], first[0]]
    for step in range(2, steps + 1 - wraps):
        pairs = [(a + 1, a) for a in range(blocks - step)]
        ahead = [
            lax.ppermute(lax.optimization_barrier((part, wait))[0], "chan", pairs)
            for part, wait in zip(ahead, waits)
        ]
        keep, sends2 = partner_tile(scalars, own_rows, ahead, table, days, step, pieces)
        sums = (keep, over_cores(sends2))
        last = [add_cores([sums], shift) for shift in range(1, days)]
        terms = [(keep, 0), sums[1][0]] + [(piece, 0) for piece in over_days(last)]
        late.append((step, terms))
    if wraps:
        terms = [(piece, 0) for piece in back]
        ready.append((steps, finished_tile(scalars, steps, terms, row_count, width, norm_scale)))
        pairs = [(c, (c + 1) % cores) for c in range(cores)]
        settled = [lax.ppermute(piece[:, :SETTLED], "sub", pairs) for piece in back]
    return write_output(scalars, ready, late, slots, norm_scale, settled)[None]


def solution(mesh):
    in_specs = (P(("groups", "day"), "sub", "chan", None, None), P("chan", None), P("chan", None))
    out_specs = P(("groups", "chan"), None, ("day", "sub"), None, None)
    return jax.shard_map(
        on_device, mesh=mesh, in_specs=in_specs, out_specs=out_specs, check_vma=False
    )
```

```python
import functools
import math

import jax
import jax.numpy as jnp
import ml_dtypes
import numpy as np
from jax import lax
from jax.experimental import pallas as pl
from jax.experimental.pallas import tpu as pltpu
from jax.sharding import PartitionSpec as P

BAND = 32
LAGS = 256
MAX_STEPS = 4
EPSILON = 1e-06
LANES = 128
ROWS = 16
OWN = 4
VMEM_LIMIT = 40 << 20
FAR = 1 << 20
HALVES = 2
SETTLED = 144
SLOT_AT = 4


def lag_table(bin_count):
    bins = np.arange(bin_count, dtype=np.float64)[:, None]
    lags = np.arange(LAGS, dtype=np.float64)[None, :] - LAGS // 2
    angle = np.pi * bins * lags / bin_count
    table = np.concatenate([np.cos(angle), -np.sin(angle)], axis=0).astype(np.float32)
    return table.astype(ml_dtypes.bfloat16)


def whiten(source):
    _, windows, channels, bins = source.shape
    width = 2 * LANES
    row = lax.broadcasted_iota(jnp.int32, (width, width), 0) // BAND
    col = lax.broadcasted_iota(jnp.int32, (width, width), 1) // BAND
    mean_matrix = jnp.where(row == col, 1.0 / BAND, 0.0).astype(jnp.bfloat16)
    for at in range(0, bins, width):
        lanes = pl.ds(at, width)
        real = source[0, :, :, lanes].astype(jnp.float32).reshape(windows * channels, width)
        imag = source[1, :, :, lanes].astype(jnp.float32).reshape(windows * channels, width)
        rest = real * real + imag * imag
        mean = jnp.zeros_like(rest)
        for _ in range(3):
            piece = rest.astype(jnp.bfloat16)
            mean += jnp.dot(piece, mean_matrix, preferred_element_type=jnp.float32)
            rest = rest - piece.astype(jnp.float32)
        scale = lax.rsqrt(mean + EPSILON)
        shape = (windows, channels, width)
        yield (
            lanes,
            (real * scale).astype(jnp.bfloat16).astype(jnp.float32).reshape(shape),
            (imag * scale).astype(jnp.bfloat16).astype(jnp.float32).reshape(shape),
        )


def row_factors(real, imag):
    return real + imag, real, imag


def col_factors(real, imag):
    return real, -(real + imag), real - imag


def store_factors(source, target, begin, factors):
    for lanes, real, imag in whiten(source):
        for k, value in enumerate(factors(real, imag)):
            target[k, :, pl.ds(begin, source.shape[2]), lanes] = value


def reach_of(scalars, step):
    slots = (scalars.shape[1] - SLOT_AT) // 2
    picked = [
        jnp.where(scalars[0, SLOT_AT + k] == step, scalars[0, SLOT_AT + slots + k], 0) for k in range(slots)
    ]
    return functools.reduce(lambda x, y: x + y, picked)


def cross_tile(rows, cols, cross, reach, first_distance, begin=0, row_count=None):
    _, windows, all_rows, bins = rows.shape
    row_count = row_count or all_rows
    groups = cols.shape[2] // ROWS

    def body(step, carry):
        row_to = pl.multiple_of((step // groups) * 8, 8)
        row_at = pl.multiple_of(begin + row_to, 8)
        group = step % groups
        col_at = pl.multiple_of(group * ROWS, ROWS)
        nearest = first_distance + col_at - row_at
        active = (nearest - 7 < reach) & (-(nearest + ROWS - 1) < reach)

        @pl.when(active)
        def _():
            for at in range(0, bins, LANES):
                lanes = pl.ds(at, LANES)
                for first in range(0, 8, OWN):
                    sums = [[None] * 3 for _ in range(OWN)]
                    for w in range(windows):
                        for k in range(3):
                            right = cols[k, w, pl.ds(col_at, ROWS), lanes]
                            left = rows.at[k, w, pl.ds(row_at, 8), lanes]
                            for i in range(OWN):
                                product = right * left[pl.ds(first + i, 1)]
                                sums[i][k] = product if w == 0 else sums[i][k] + product
                    for i in range(OWN):
                        k1, k2, k3 = sums[i]
                        at_row = (group * row_count + row_to + first + i) * ROWS
                        place = pl.ds(pl.multiple_of(at_row, ROWS), ROWS)
                        cross[place, pl.ds(at, LANES)] = (k1 - k3).astype(jnp.bfloat16)
                        cross[place, pl.ds(bins + at, LANES)] = (k1 + k2).astype(jnp.bfloat16)

        return carry

    lax.fori_loop(0, (row_count // 8) * groups, body, 0)


def lag_block(core, cross, begin, table, size, store):
    place = pl.ds(pl.multiple_of(begin, 2 * size), 2 * size)
    lags = jnp.dot(cross[place], table[...], preferred_element_type=jnp.float32)
    low, high = lags[:size], lags[size:]
    pl.when(core == 0)(lambda: store(low, high.astype(jnp.bfloat16)))
    pl.when(core != 0)(lambda: store(high, low.astype(jnp.bfloat16)))


def store_at(keep, sends, shift, half):
    def store(kept, sent):
        size = sent.shape[0]
        keep[shift, pl.ds(half * size, size)] = kept
        sends[shift * HALVES + half][0] = sent

    return store


def lag_sums(scalars, cross, table, keep, sends):
    owners, size = keep.shape[0], keep.shape[1] // HALVES
    core, day = scalars[0, 0], scalars[0, 1]
    for shift in range(owners):
        owner = lax.rem(day + shift, owners)
        for half in range(HALVES):
            begin = (half * owners + owner) * (2 * size)
            lag_block(core, cross, begin, table, size, store_at(keep, sends, shift, half))


def begins_of(parts):
    return [sum(p.shape[2] for p in parts[:k]) for k in range(len(parts))]


def own_kernel(part_count, scalars, table, *refs):
    parts = refs[:part_count]
    keep, *sends, rows, cols, cross = refs[part_count:]
    for part, begin in zip(parts, begins_of(parts)):
        for lanes, real, imag in whiten(part):
            for k in range(3):
                rows[k, :, pl.ds(begin, part.shape[2]), lanes] = row_factors(real, imag)[k]
                cols[k, :, pl.ds(begin, part.shape[2]), lanes] = col_factors(real, imag)[k]
    cross_tile(rows, cols, cross, reach_of(scalars, 0), 0)
    lag_sums(scalars, cross, table, keep, sends)


def days_kernel(shifts, owners, part_count, after_count, step, scalars, own_rows, table, *refs):
    parts, refs = refs[:part_count], refs[part_count:]
    if not parts:
        cols, *refs = refs
    keep, *sends, cross = refs[after_count:]
    if parts:
        *sends, cols = sends
    per = len(sends) // len(shifts)
    width = own_rows.shape[2]
    count = width // owners
    size = count * ROWS // 2
    core, day = scalars[0, 0], scalars[0, 1]
    reach = reach_of(scalars, step)

    def store_at(k, half):
        def store(kept, sent):
            keep[k, pl.ds(half * size, size)] = kept
            begin = 0
            for send in sends[k * per : (k + 1) * per]:
                low = max(begin, half * size)
                high = min(begin + send.shape[1], (half + 1) * size)
                if low < high:
                    send[0, pl.ds(low - begin, high - low)] = sent[low - half * size : high - half * size]
                begin += send.shape[1]

        return store

    @pl.when(reach > 0)
    def _():
        for part, begin in zip(parts, begins_of(parts)):
            store_factors(part, cols, begin, col_factors)
        for k, shift in enumerate(shifts):
            begin = lax.rem(day + shift, owners) * count
            cross_tile(own_rows, cols, cross, reach, step * width, begin, count)
            for half in range(HALVES):
                lag_block(core, cross, half * 2 * size, table, size, store_at(k, half))


def half_cross(can_swap, step, half, scalars, own_rows, part, cols, cross, swap_refs, finish):
    width, count = own_rows.shape[2], part.shape[2]
    reach = reach_of(scalars, step)

    @pl.when(reach > 0)
    def _():
        store_factors(part, cols, 0, col_factors)
        cross_tile(own_rows, cols, cross, reach, step * width + half * count)
        finish(False)

    if can_swap:
        rows, wide_cols = swap_refs

        @pl.when(scalars[0, 2] != 0)
        def _():
            for at in range(0, own_rows.shape[3], LANES):
                lanes = pl.ds(at, LANES)
                real, imag = own_rows[1, :, :, lanes], own_rows[2, :, :, lanes]
                for k, value in enumerate(col_factors(real, imag)):
                    wide_cols[k, :, :, lanes] = value
            store_factors(part, rows, 0, row_factors)
            cross_tile(rows, wide_cols, cross, FAR, 0)
            finish(True)


def first_half_kernel(can_swap, step, scalars, own_rows, table, part, keep, send, cols, cross, *swap_refs):
    owners, size = keep.shape[0], keep.shape[1]

    def finish(swapped):
        for k in range(owners):

            def store(kept, sent, k=k):
                keep[k] = kept
                send[k] = sent

            lag_block(scalars[0, 0], cross, k * 2 * size, table, size, store)

    half_cross(can_swap, step, 0, scalars, own_rows, part, cols, cross, swap_refs, finish)


def second_half_kernel(
    can_swap, step, after_count, scalars, own_rows, table, part, first_keep, first_send, *refs
):
    keep, *refs = refs[after_count:]
    sends = refs[: keep.shape[0] * HALVES]
    cols, cross, *swap_refs = refs[keep.shape[0] * HALVES :]
    owners, size = keep.shape[0], keep.shape[1] // HALVES
    core, day = scalars[0, 0], scalars[0, 1]

    def finish(swapped):
        for shift in range(owners):
            owner = lax.rem(day + shift, owners)
            if not swapped:
                store_at(keep, sends, shift, 0)(first_keep[owner], first_send[owner])
                lag_block(core, cross, owner * 2 * size, table, size, store_at(keep, sends, shift, 1))
                continue
            for half in range(HALVES):
                store = store_at(keep, sends, shift, half)
                pl.when(owner == 0)(lambda store=store, half=half: store(first_keep[half], first_send[half]))
                pl.when(owner != 0)(
                    lambda store=store, half=half: lag_block(
                        core, cross, half * 2 * size, table, size, store
                    )
                )

    half_cross(can_swap, step, 1, scalars, own_rows, part, cols, cross, swap_refs, finish)


VMEM = pl.BlockSpec(memory_space=pltpu.VMEM)
ANY = pl.BlockSpec(memory_space=pl.ANY)
FREE = pl.CostEstimate(flops=0, bytes_accessed=0, transcendentals=0)
PARAMS = pltpu.CompilerParams(vmem_limit_bytes=VMEM_LIMIT)


def sums_shapes(owners, width):
    size = width * width // (2 * owners * HALVES)
    return [jax.ShapeDtypeStruct((owners, HALVES * size, LAGS), jnp.float32)] + [
        jax.ShapeDtypeStruct((1, size, LAGS), jnp.bfloat16)
    ] * (owners * HALVES)


def fetch_kernel(source, *refs):
    *parts, sems = refs
    half = parts[0].shape[2]
    copies = [
        pltpu.make_async_copy(source.at[:, :, pl.ds(k * half, half)], part, sems.at[k])
        for k, part in enumerate(parts)
    ]
    for copy in copies:
        copy.start()
    for copy in copies:
        copy.wait()


def fetch_halves(spectra):
    days, windows, width, parts, bins = spectra.shape
    shape = jax.ShapeDtypeStruct((days, windows, width // HALVES, parts, bins), spectra.dtype)
    return pl.pallas_call(
        fetch_kernel,
        out_shape=[shape] * HALVES,
        in_specs=[ANY],
        out_specs=[VMEM] * HALVES,
        scratch_shapes=[pltpu.SemaphoreType.DMA((HALVES,))],
        compiler_params=PARAMS,
        cost_estimate=FREE,
    )(spectra)


def own_tile(scalars, parts, table, owners):
    _, windows, _, bins = parts[0].shape
    width = sum(part.shape[2] for part in parts)
    factors = (3, windows, width, bins)
    keep, *sends, rows = pl.pallas_call(
        functools.partial(own_kernel, len(parts)),
        out_shape=sums_shapes(owners, width) + [jax.ShapeDtypeStruct(factors, jnp.float32)],
        in_specs=[VMEM] + [VMEM] * (1 + len(parts)),
        out_specs=[VMEM] * (owners * HALVES + 2),
        scratch_shapes=[
            pltpu.VMEM(factors, jnp.float32),
            pltpu.VMEM((width * width, 2 * bins), jnp.bfloat16),
        ],
        compiler_params=PARAMS,
        cost_estimate=FREE,
    )(scalars, table, *parts)
    return keep, sends, rows


def days_tile(scalars, own_rows, table, owners, step, shifts, splits, parts=(), cols=None, after=()):
    _, windows, width, bins = own_rows.shape
    col_shape = (3, windows, width, bins)
    shapes = [jax.ShapeDtypeStruct((len(shifts), sum(splits), LAGS), jnp.float32)]
    shapes += [jax.ShapeDtypeStruct((1, rows, LAGS), jnp.bfloat16) for rows in splits] * len(shifts)
    if cols is None:
        shapes.append(jax.ShapeDtypeStruct(col_shape, jnp.float32))
    operands = list(parts) if cols is None else [cols]
    keep, *sends = pl.pallas_call(
        functools.partial(days_kernel, shifts, owners, len(parts), len(after), step),
        out_shape=shapes,
        in_specs=[VMEM] * (3 + len(operands)) + [ANY] * len(after),
        out_specs=[VMEM] * len(shapes),
        scratch_shapes=[pltpu.VMEM((width // owners * width, 2 * bins), jnp.bfloat16)],
        compiler_params=PARAMS,
        cost_estimate=FREE,
    )(scalars, own_rows, table, *operands, *after)
    if cols is None:
        *sends, cols = sends
    return keep, sends, cols


def half_scratch(own_rows, can_swap):
    _, windows, width, bins = own_rows.shape
    half = width // HALVES
    wide, narrow = (3, windows, width, bins), (3, windows, half, bins)
    scratch = [pltpu.VMEM(narrow, jnp.float32), pltpu.VMEM((width * half, 2 * bins), jnp.bfloat16)]
    if can_swap:
        scratch += [pltpu.VMEM(narrow, jnp.float32), pltpu.VMEM(wide, jnp.float32)]
    return scratch


def first_half_tile(scalars, own_rows, part, table, owners, step, can_swap):
    width = own_rows.shape[2]
    size = width * width // (2 * owners * HALVES)
    return pl.pallas_call(
        functools.partial(first_half_kernel, can_swap, step),
        out_shape=[
            jax.ShapeDtypeStruct((owners, size, LAGS), jnp.float32),
            jax.ShapeDtypeStruct((owners, size, LAGS), jnp.bfloat16),
        ],
        in_specs=[VMEM, VMEM, VMEM, VMEM],
        out_specs=[VMEM, VMEM],
        scratch_shapes=half_scratch(own_rows, can_swap),
        compiler_params=PARAMS,
        cost_estimate=FREE,
    )(scalars, own_rows, table, part)


def second_half_tile(scalars, own_rows, part, first, table, owners, step, can_swap, after):
    keep, *sends = pl.pallas_call(
        functools.partial(second_half_kernel, can_swap, step, len(after)),
        out_shape=sums_shapes(owners, own_rows.shape[2]),
        in_specs=[VMEM] + [VMEM] * 5 + [ANY] * len(after),
        out_specs=[VMEM] * (owners * HALVES + 1),
        scratch_shapes=half_scratch(own_rows, can_swap),
        compiler_params=PARAMS,
        cost_estimate=FREE,
    )(scalars, own_rows, table, part, *first, *after)
    return keep, sends


def add_kernel(tiles, shift, *refs):
    out = refs[-1]
    for tile in range(tiles):
        keep, *got = refs[tile * (1 + HALVES) : (tile + 1) * (1 + HALVES)]
        for half, sent in enumerate(got):
            place = pl.ds(half * sent.shape[1], sent.shape[1])
            out[tile, place] = (keep[shift, place] + sent[0].astype(jnp.float32)).astype(out.dtype)


def add_cores(tiles, shift, after=()):
    operands = [term for keep, got in tiles for term in [keep] + got[shift]]
    rows = tiles[0][0].shape[1]
    return pl.pallas_call(
        functools.partial(add_kernel, len(tiles), shift),
        out_shape=jax.ShapeDtypeStruct((len(tiles), rows, LAGS), jnp.bfloat16),
        in_specs=[VMEM] * len(operands) + [ANY] * len(after),
        out_specs=VMEM,
        compiler_params=PARAMS,
        cost_estimate=FREE,
    )(*operands, *after)


def write_tile(scalars, step, terms, tile, norm_scale):
    row_count, width, _ = tile.shape
    slots = (scalars.shape[1] - SLOT_AT) // 2
    reach = reach_of(scalars, step)
    half_width = width // HALVES
    size = row_count * half_width
    for half in range(HALVES):
        value = None
        for term in terms:
            if isinstance(term, list):
                whole = jnp.concatenate([part[0].astype(jnp.float32) for part in term], axis=0)
                part = whole[half * size : (half + 1) * size]
            else:
                array, at = term
                part = array[at, pl.ds(half * size, size)]
            part = part.astype(jnp.float32)
            value = part if value is None else value + part
        value = value.reshape(row_count, half_width, LAGS)
        row = lax.broadcasted_iota(jnp.int32, value.shape, 0) + scalars[0, 3] * row_count
        col = lax.broadcasted_iota(jnp.int32, value.shape, 1) + half * half_width
        distance = jnp.abs(step * width + col - row)
        kept = (distance > 0) & (distance < reach)
        tile[:, pl.ds(half * half_width, half_width), :] = jnp.where(kept, value * norm_scale, 0.0)


def grouped(refs, counts):
    terms = []
    for at, count in counts:
        if at is not None:
            terms.append((refs.pop(0), at))
        else:
            terms.append([refs.pop(0) for _ in range(count)])
    return terms


def tile_kernel(step, counts, norm_scale, scalars, *refs):
    *terms, tile = refs
    write_tile(scalars, step, grouped(terms, counts), tile, norm_scale)


def flat(terms):
    operands, counts = [], []
    for term in terms:
        listed = isinstance(term, list)
        operands += term if listed else [term[0]]
        counts.append((None, len(term)) if listed else (term[1], 1))
    return operands, counts


def finished_tile(scalars, step, terms, row_count, width, norm_scale):
    operands, counts = flat(terms)
    return pl.pallas_call(
        functools.partial(tile_kernel, step, counts, norm_scale),
        out_shape=jax.ShapeDtypeStruct((row_count, width, LAGS), jnp.float32),
        in_specs=[VMEM] + [VMEM] * len(operands),
        out_specs=VMEM,
        compiler_params=PARAMS,
        cost_estimate=FREE,
    )(scalars, *operands)


def output_kernel(ready_steps, late, after_count, norm_scale, scalars, *refs):
    out, tiles, zeros, sems = refs[-4:]
    slots = out.shape[0]
    ready, rest = refs[: len(ready_steps)], list(refs[len(ready_steps) : -4])

    def copies(slot, source):
        return pltpu.make_async_copy(source, out.at[slot], sems.at[slot])

    def start(step, source):
        for slot in range(slots):
            pl.when(scalars[0, SLOT_AT + slot] == step)(copies(slot, source).start)

    for step, tile in zip(ready_steps, ready):
        start(step, tile)
    zeros[...] = jnp.zeros_like(zeros)
    start(-1, zeros)
    for place, (step, counts) in enumerate(late):
        terms = grouped(rest, counts)

        @pl.when(reach_of(scalars, step) > 0)
        def _(step=step, terms=terms, place=place):
            write_tile(scalars, step, terms, tiles.at[place], norm_scale)

        start(step, tiles.at[place])
    for slot in range(slots):
        copies(slot, zeros).wait()


def write_output(scalars, ready, late, slots, norm_scale, after):
    tile_shape = ready[0][1].shape
    operands, listed = [tile for _, tile in ready], []
    for step, terms in late:
        more, counts = flat(terms)
        operands += more
        listed.append((step, counts))
    return pl.pallas_call(
        functools.partial(output_kernel, [step for step, _ in ready], listed, len(after), norm_scale),
        out_shape=jax.ShapeDtypeStruct((slots,) + tile_shape, jnp.float32),
        in_specs=[VMEM] + [VMEM] * len(operands) + [ANY] * len(after),
        out_specs=ANY,
        scratch_shapes=[
            pltpu.VMEM((len(late),) + tile_shape, jnp.float32),
            pltpu.VMEM(tile_shape, jnp.float32),
            pltpu.SemaphoreType.DMA((slots,)),
        ],
        compiler_params=PARAMS,
        cost_estimate=FREE,
    )(scalars, *operands, *after)


def on_device(spectra, tile_offset, pair_reach):
    blocks = lax.axis_size("chan")
    days, cores = lax.axis_size("day"), lax.axis_size("sub")
    steps = min(MAX_STEPS, blocks - 1)
    wraps = blocks >= 3 and steps == blocks - 1 and days == 2
    local_days, local_windows, width, _, bins = spectra.shape
    norm_scale = 1.0 / math.sqrt(bins * local_days * days * local_windows * cores)
    row_count = width // (days * cores)
    slots = tile_offset.shape[1]
    day, core, block = lax.axis_index("day"), lax.axis_index("sub"), lax.axis_index("chan")
    table = jnp.asarray(lag_table(bins))

    half = width // HALVES
    halves = [
        jnp.transpose(part, (3, 0, 1, 2, 4)).reshape(2, -1, half, bins) for part in fetch_halves(spectra)
    ]
    is_last = (block == blocks - 1).astype(jnp.int32) if wraps else jnp.int32(0)
    scalars = jnp.stack([core, day, is_last, day * cores + core]).astype(jnp.int32)
    scalars = jnp.concatenate([scalars, tile_offset[0], pair_reach[0]])[None]

    def over_cores(sends):
        got = [lax.ppermute(send, "sub", [(k, (k + 1) % cores) for k in range(cores)]) for send in sends]
        return [got[k : k + HALVES] for k in range(0, len(got), HALVES)]

    def over_days(pieces):
        return [
            lax.ppermute(piece, "day", [(k, (k + shift) % days) for k in range(days)])
            for shift, piece in enumerate(pieces, 1)
        ]

    def to_first(piece, shift):
        pairs = [((blocks - 1) * days + k, (k + shift) % days) for k in range(days)]
        return lax.ppermute(piece, ("chan", "day"), pairs)

    keep, sends, own_rows = own_tile(scalars, halves, table, days)
    own_sums = (keep, over_cores(sends))
    ready, late, back, settled = [], [], [], []

    pairs = [(a + 1, a) for a in range(blocks - 1)] + [(0, blocks - 1)] * wraps
    moving = [lax.ppermute(part, "chan", pairs) for part in halves]
    first = first_half_tile(scalars, own_rows, moving[0], table, days, 1, wraps)
    ahead = moving
    after = [x for pair in own_sums[1] for x in pair] if 0 else []
    keep, sends1 = second_half_tile(scalars, own_rows, moving[1], first, table, days, 1, wraps, after)
    sums = (keep, over_cores(sends1))
    pieces = [add_cores([sums, own_sums], shift) for shift in range(1, days)]
    if wraps:
        back = [to_first(add_cores([sums], shift), shift) for shift in range(days)]
    moved = over_days(pieces)
    for step, (keep, got) in enumerate([own_sums, sums]):
        terms = [(keep, 0), got[0]] + [(piece, 1 - step) for piece in moved]
        ready.append((step, finished_tile(scalars, step, terms, row_count, width, norm_scale)))

    waits = [sends[0], first[0]]
    for step in range(2, steps + 1 - wraps):
        pairs = [(a + 1, a) for a in range(blocks - step)]
        ahead = [
            lax.ppermute(lax.optimization_barrier((part, wait))[0], "chan", pairs)
            for part, wait in zip(ahead, waits)
        ]
        rows = row_count * width
        arrived, block = [], {"parts": ahead}
        if days > 1:
            keep, sends2, cols = days_tile(
                scalars, own_rows, table, days, step, range(1, days), (rows // 2, rows // 2), ahead, None, pieces
            )
            sums = (keep, over_cores(sends2))
            arrived = over_days([add_cores([sums], k) for k in range(days - 1)])
            block = {"cols": cols}
        splits = (rows * 3 // 4, rows // 4)
        keep, sends2, _ = days_tile(scalars, own_rows, table, days, step, [0], splits, **block)
        got = [array for arrays in over_cores(sends2) for array in arrays]
        late.append((step, [(keep, 0), got] + [(piece, 0) for piece in arrived]))
    if wraps:
        terms = [(piece, 0) for piece in back]
        hosted = finished_tile(scalars, steps, terms, row_count, width, norm_scale)
        ready.append((steps, hosted))
        pairs = [(c, (c + 1) % cores) for c in range(cores)]
        settled = [lax.ppermute(hosted[:3, :24], "sub", pairs)]
    return write_output(scalars, ready, late, slots, norm_scale, settled)[None]


def solution(mesh):
    in_specs = (P(("groups", "day"), "sub", "chan", None, None), P("chan", None), P("chan", None))
    out_specs = P(("groups", "chan"), None, ("day", "sub"), None, None)
    return jax.shard_map(
        on_device, mesh=mesh, in_specs=in_specs, out_specs=out_specs, check_vma=False
    )
```

```python
import functools
import math

import jax
import jax.numpy as jnp
import ml_dtypes
import numpy as np
from jax import lax
from jax.experimental import pallas as pl
from jax.experimental.pallas import tpu as pltpu
from jax.sharding import PartitionSpec as P

BAND = 32
LAGS = 256
MAX_STEPS = 4
EPSILON = 1e-06
LANES = 128
ROWS = 16
OWN = 4
VMEM_LIMIT = 40 << 20
FAR = 1 << 20
HALVES = 2
SETTLED = 144
SLOT_AT = 4


def lag_table(bin_count):
    bins = np.arange(bin_count, dtype=np.float64)[:, None]
    lags = np.arange(LAGS, dtype=np.float64)[None, :] - LAGS // 2
    angle = np.pi * bins * lags / bin_count
    table = np.concatenate([np.cos(angle), -np.sin(angle)], axis=0).astype(np.float32)
    return table.astype(ml_dtypes.bfloat16)


def whiten(source):
    _, windows, channels, bins = source.shape
    width = 2 * LANES
    row = lax.broadcasted_iota(jnp.int32, (width, width), 0) // BAND
    col = lax.broadcasted_iota(jnp.int32, (width, width), 1) // BAND
    mean_matrix = jnp.where(row == col, 1.0 / BAND, 0.0).astype(jnp.bfloat16)
    for at in range(0, bins, width):
        lanes = pl.ds(at, width)
        real = source[0, :, :, lanes].astype(jnp.float32).reshape(windows * channels, width)
        imag = source[1, :, :, lanes].astype(jnp.float32).reshape(windows * channels, width)
        rest = real * real + imag * imag
        mean = jnp.zeros_like(rest)
        for _ in range(3):
            piece = rest.astype(jnp.bfloat16)
            mean += jnp.dot(piece, mean_matrix, preferred_element_type=jnp.float32)
            rest = rest - piece.astype(jnp.float32)
        scale = lax.rsqrt(mean + EPSILON)
        shape = (windows, channels, width)
        yield (
            lanes,
            (real * scale).astype(jnp.bfloat16).astype(jnp.float32).reshape(shape),
            (imag * scale).astype(jnp.bfloat16).astype(jnp.float32).reshape(shape),
        )


def row_factors(real, imag):
    return real + imag, real, imag


def col_factors(real, imag):
    return real, -(real + imag), real - imag


def store_factors(source, target, begin, factors):
    for lanes, real, imag in whiten(source):
        for k, value in enumerate(factors(real, imag)):
            target[k, :, pl.ds(begin, source.shape[2]), lanes] = value


def reach_of(scalars, step):
    slots = (scalars.shape[1] - SLOT_AT) // 2
    picked = [
        jnp.where(scalars[0, SLOT_AT + k] == step, scalars[0, SLOT_AT + slots + k], 0) for k in range(slots)
    ]
    return functools.reduce(lambda x, y: x + y, picked)


def cross_tile(rows, cols, cross, reach, first_distance, begin=0, row_count=None):
    _, windows, all_rows, bins = rows.shape
    row_count = row_count or all_rows
    groups = cols.shape[2] // ROWS

    def body(step, carry):
        row_to = pl.multiple_of((step // groups) * 8, 8)
        row_at = pl.multiple_of(begin + row_to, 8)
        group = step % groups
        col_at = pl.multiple_of(group * ROWS, ROWS)
        nearest = first_distance + col_at - row_at
        active = (nearest - 7 < reach) & (-(nearest + ROWS - 1) < reach)

        @pl.when(active)
        def _():
            for at in range(0, bins, LANES):
                lanes = pl.ds(at, LANES)
                for first in range(0, 8, OWN):
                    sums = [[None] * 3 for _ in range(OWN)]
                    for w in range(windows):
                        for k in range(3):
                            right = cols[k, w, pl.ds(col_at, ROWS), lanes]
                            left = rows.at[k, w, pl.ds(row_at, 8), lanes]
                            for i in range(OWN):
                                product = right * left[pl.ds(first + i, 1)]
                                sums[i][k] = product if w == 0 else sums[i][k] + product
                    for i in range(OWN):
                        k1, k2, k3 = sums[i]
                        at_row = (group * row_count + row_to + first + i) * ROWS
                        place = pl.ds(pl.multiple_of(at_row, ROWS), ROWS)
                        cross[place, pl.ds(at, LANES)] = (k1 - k3).astype(jnp.bfloat16)
                        cross[place, pl.ds(bins + at, LANES)] = (k1 + k2).astype(jnp.bfloat16)

        return carry

    lax.fori_loop(0, (row_count // 8) * groups, body, 0)


def lag_block(core, cross, begin, table, size, store):
    place = pl.ds(pl.multiple_of(begin, 2 * size), 2 * size)
    lags = jnp.dot(cross[place], table[...], preferred_element_type=jnp.float32)
    low, high = lags[:size], lags[size:]
    pl.when(core == 0)(lambda: store(low, high.astype(jnp.bfloat16)))
    pl.when(core != 0)(lambda: store(high, low.astype(jnp.bfloat16)))


def lag_blocks(core, cross, blocks, table, size, store):
    lags = jnp.dot(cross[: blocks * 2 * size], table[...], preferred_element_type=jnp.float32)
    parts = [(lags[k * 2 * size :][:size], lags[(k * 2 + 1) * size :][:size]) for k in range(blocks)]

    @pl.when(core == 0)
    def _():
        for k, (low, high) in enumerate(parts):
            store(k, low, high.astype(jnp.bfloat16))

    @pl.when(core != 0)
    def _():
        for k, (low, high) in enumerate(parts):
            store(k, high, low.astype(jnp.bfloat16))


def store_at(keep, sends, shift, half):
    def store(kept, sent):
        size = sent.shape[0]
        keep[shift, pl.ds(half * size, size)] = kept
        sends[shift * HALVES + half][0] = sent

    return store


def lag_sums(scalars, cross, table, keep, sends):
    owners, size = keep.shape[0], keep.shape[1] // HALVES
    core, day = scalars[0, 0], scalars[0, 1]
    for shift in range(owners):
        owner = lax.rem(day + shift, owners)
        for half in range(HALVES):
            begin = (half * owners + owner) * (2 * size)
            lag_block(core, cross, begin, table, size, store_at(keep, sends, shift, half))


def begins_of(parts):
    return [sum(p.shape[2] for p in parts[:k]) for k in range(len(parts))]


def own_kernel(part_count, scalars, table, *refs):
    parts = refs[:part_count]
    keep, *sends, rows, cols, cross = refs[part_count:]
    for part, begin in zip(parts, begins_of(parts)):
        for lanes, real, imag in whiten(part):
            for k in range(3):
                rows[k, :, pl.ds(begin, part.shape[2]), lanes] = row_factors(real, imag)[k]
                cols[k, :, pl.ds(begin, part.shape[2]), lanes] = col_factors(real, imag)[k]
    cross_tile(rows, cols, cross, reach_of(scalars, 0), 0)
    lag_sums(scalars, cross, table, keep, sends)


def days_kernel(shifts, owners, part_count, after_count, step, scalars, own_rows, table, *refs):
    parts, refs = refs[:part_count], refs[part_count:]
    if not parts:
        cols, *refs = refs
    keep, *sends, cross = refs[after_count:]
    if parts:
        *sends, cols = sends
    per = len(sends) // len(shifts)
    width = own_rows.shape[2]
    count = width // owners
    size = count * ROWS // 2
    core, day = scalars[0, 0], scalars[0, 1]
    reach = reach_of(scalars, step)

    def store(k, half, kept, sent):
        keep[k, pl.ds(half * size, size)] = kept
        begin = 0
        for send in sends[k * per : (k + 1) * per]:
            low = max(begin, half * size)
            high = min(begin + send.shape[1], (half + 1) * size)
            if low < high:
                send[0, pl.ds(low - begin, high - low)] = sent[low - half * size : high - half * size]
            begin += send.shape[1]

    @pl.when(reach > 0)
    def _():
        for part, begin in zip(parts, begins_of(parts)):
            store_factors(part, cols, begin, col_factors)
        for k, shift in enumerate(shifts):
            begin = lax.rem(day + shift, owners) * count
            cross_tile(own_rows, cols, cross, reach, step * width, begin, count)
            lag_blocks(core, cross, HALVES, table, size, functools.partial(store, k))


def half_cross(can_swap, step, half, scalars, own_rows, part, cols, cross, swap_refs, finish):
    width, count = own_rows.shape[2], part.shape[2]
    reach = reach_of(scalars, step)

    @pl.when(reach > 0)
    def _():
        store_factors(part, cols, 0, col_factors)
        cross_tile(own_rows, cols, cross, reach, step * width + half * count)
        finish(False)

    if can_swap:
        rows, wide_cols = swap_refs

        @pl.when(scalars[0, 2] != 0)
        def _():
            for at in range(0, own_rows.shape[3], LANES):
                lanes = pl.ds(at, LANES)
                real, imag = own_rows[1, :, :, lanes], own_rows[2, :, :, lanes]
                for k, value in enumerate(col_factors(real, imag)):
                    wide_cols[k, :, :, lanes] = value
            store_factors(part, rows, 0, row_factors)
            cross_tile(rows, wide_cols, cross, FAR, 0)
            finish(True)


def first_half_kernel(can_swap, step, scalars, own_rows, table, part, keep, send, cols, cross, *swap_refs):
    owners, size = keep.shape[0], keep.shape[1]

    def finish(swapped):
        def store(k, kept, sent):
            keep[k] = kept
            send[k] = sent

        lag_blocks(scalars[0, 0], cross, owners, table, size, store)

    half_cross(can_swap, step, 0, scalars, own_rows, part, cols, cross, swap_refs, finish)


def second_half_kernel(
    can_swap, step, after_count, scalars, own_rows, table, part, first_keep, first_send, *refs
):
    keep, *refs = refs[after_count:]
    sends = refs[: keep.shape[0] * HALVES]
    cols, cross, *swap_refs = refs[keep.shape[0] * HALVES :]
    owners, size = keep.shape[0], keep.shape[1] // HALVES
    core, day = scalars[0, 0], scalars[0, 1]

    def finish(swapped):
        def store(block, kept, sent):
            for shift in range(owners):
                owner = lax.rem(day + shift, owners)
                half = block if swapped else 1
                here = owner != 0 if swapped else owner == block
                pl.when(here)(lambda: store_at(keep, sends, shift, half)(kept, sent))

        for shift in range(owners):
            owner = lax.rem(day + shift, owners)
            if swapped:
                for half in range(HALVES):
                    copy = functools.partial(
                        store_at(keep, sends, shift, half), first_keep[half], first_send[half]
                    )
                    pl.when(owner == 0)(copy)
            else:
                store_at(keep, sends, shift, 0)(first_keep[owner], first_send[owner])
        lag_blocks(core, cross, HALVES if swapped else owners, table, size, store)

    half_cross(can_swap, step, 1, scalars, own_rows, part, cols, cross, swap_refs, finish)


VMEM = pl.BlockSpec(memory_space=pltpu.VMEM)
ANY = pl.BlockSpec(memory_space=pl.ANY)
FREE = pl.CostEstimate(flops=0, bytes_accessed=0, transcendentals=0)
PARAMS = pltpu.CompilerParams(vmem_limit_bytes=VMEM_LIMIT)


def sums_shapes(owners, width):
    size = width * width // (2 * owners * HALVES)
    return [jax.ShapeDtypeStruct((owners, HALVES * size, LAGS), jnp.float32)] + [
        jax.ShapeDtypeStruct((1, size, LAGS), jnp.bfloat16)
    ] * (owners * HALVES)


def fetch_kernel(source, *refs):
    *parts, sems = refs
    half = parts[0].shape[2]
    copies = [
        pltpu.make_async_copy(source.at[:, :, pl.ds(k * half, half)], part, sems.at[k])
        for k, part in enumerate(parts)
    ]
    for copy in copies:
        copy.start()
    for copy in copies:
        copy.wait()


def fetch_halves(spectra):
    days, windows, width, parts, bins = spectra.shape
    shape = jax.ShapeDtypeStruct((days, windows, width // HALVES, parts, bins), spectra.dtype)
    return pl.pallas_call(
        fetch_kernel,
        out_shape=[shape] * HALVES,
        in_specs=[ANY],
        out_specs=[VMEM] * HALVES,
        scratch_shapes=[pltpu.SemaphoreType.DMA((HALVES,))],
        compiler_params=PARAMS,
        cost_estimate=FREE,
    )(spectra)


def own_tile(scalars, parts, table, owners):
    _, windows, _, bins = parts[0].shape
    width = sum(part.shape[2] for part in parts)
    factors = (3, windows, width, bins)
    keep, *sends, rows = pl.pallas_call(
        functools.partial(own_kernel, len(parts)),
        out_shape=sums_shapes(owners, width) + [jax.ShapeDtypeStruct(factors, jnp.float32)],
        in_specs=[VMEM] + [VMEM] * (1 + len(parts)),
        out_specs=[VMEM] * (owners * HALVES + 2),
        scratch_shapes=[
            pltpu.VMEM(factors, jnp.float32),
            pltpu.VMEM((width * width, 2 * bins), jnp.bfloat16),
        ],
        compiler_params=PARAMS,
        cost_estimate=FREE,
    )(scalars, table, *parts)
    return keep, sends, rows


def days_tile(scalars, own_rows, table, owners, step, shifts, splits, parts=(), cols=None, after=()):
    _, windows, width, bins = own_rows.shape
    col_shape = (3, windows, width, bins)
    shapes = [jax.ShapeDtypeStruct((len(shifts), sum(splits), LAGS), jnp.float32)]
    shapes += [jax.ShapeDtypeStruct((1, rows, LAGS), jnp.bfloat16) for rows in splits] * len(shifts)
    if cols is None:
        shapes.append(jax.ShapeDtypeStruct(col_shape, jnp.float32))
    operands = list(parts) if cols is None else [cols]
    keep, *sends = pl.pallas_call(
        functools.partial(days_kernel, shifts, owners, len(parts), len(after), step),
        out_shape=shapes,
        in_specs=[VMEM] * (3 + len(operands)) + [ANY] * len(after),
        out_specs=[VMEM] * len(shapes),
        scratch_shapes=[pltpu.VMEM((width // owners * width, 2 * bins), jnp.bfloat16)],
        compiler_params=PARAMS,
        cost_estimate=FREE,
    )(scalars, own_rows, table, *operands, *after)
    if cols is None:
        *sends, cols = sends
    return keep, sends, cols


def half_scratch(own_rows, can_swap):
    _, windows, width, bins = own_rows.shape
    half = width // HALVES
    wide, narrow = (3, windows, width, bins), (3, windows, half, bins)
    scratch = [pltpu.VMEM(narrow, jnp.float32), pltpu.VMEM((width * half, 2 * bins), jnp.bfloat16)]
    if can_swap:
        scratch += [pltpu.VMEM(narrow, jnp.float32), pltpu.VMEM(wide, jnp.float32)]
    return scratch


def first_half_tile(scalars, own_rows, part, table, owners, step, can_swap):
    width = own_rows.shape[2]
    size = width * width // (2 * owners * HALVES)
    return pl.pallas_call(
        functools.partial(first_half_kernel, can_swap, step),
        out_shape=[
            jax.ShapeDtypeStruct((owners, size, LAGS), jnp.float32),
            jax.ShapeDtypeStruct((owners, size, LAGS), jnp.bfloat16),
        ],
        in_specs=[VMEM, VMEM, VMEM, VMEM],
        out_specs=[VMEM, VMEM],
        scratch_shapes=half_scratch(own_rows, can_swap),
        compiler_params=PARAMS,
        cost_estimate=FREE,
    )(scalars, own_rows, table, part)


def second_half_tile(scalars, own_rows, part, first, table, owners, step, can_swap, after):
    keep, *sends = pl.pallas_call(
        functools.partial(second_half_kernel, can_swap, step, len(after)),
        out_shape=sums_shapes(owners, own_rows.shape[2]),
        in_specs=[VMEM] + [VMEM] * 5 + [ANY] * len(after),
        out_specs=[VMEM] * (owners * HALVES + 1),
        scratch_shapes=half_scratch(own_rows, can_swap),
        compiler_params=PARAMS,
        cost_estimate=FREE,
    )(scalars, own_rows, table, part, *first, *after)
    return keep, sends


def add_kernel(tiles, shift, *refs):
    out = refs[-1]
    for tile in range(tiles):
        keep, *got = refs[tile * (1 + HALVES) : (tile + 1) * (1 + HALVES)]
        for half, sent in enumerate(got):
            place = pl.ds(half * sent.shape[1], sent.shape[1])
            out[tile, place] = (keep[shift, place] + sent[0].astype(jnp.float32)).astype(out.dtype)


def add_cores(tiles, shift, after=()):
    operands = [term for keep, got in tiles for term in [keep] + got[shift]]
    rows = tiles[0][0].shape[1]
    return pl.pallas_call(
        functools.partial(add_kernel, len(tiles), shift),
        out_shape=jax.ShapeDtypeStruct((len(tiles), rows, LAGS), jnp.bfloat16),
        in_specs=[VMEM] * len(operands) + [ANY] * len(after),
        out_specs=VMEM,
        compiler_params=PARAMS,
        cost_estimate=FREE,
    )(*operands, *after)


def write_tile(scalars, step, terms, tile, norm_scale):
    row_count, width, _ = tile.shape
    slots = (scalars.shape[1] - SLOT_AT) // 2
    reach = reach_of(scalars, step)
    half_width = width // HALVES
    size = row_count * half_width
    for half in range(HALVES):
        value = None
        for term in terms:
            if isinstance(term, list):
                whole = jnp.concatenate([part[0].astype(jnp.float32) for part in term], axis=0)
                part = whole[half * size : (half + 1) * size]
            else:
                array, at = term
                part = array[at, pl.ds(half * size, size)]
            part = part.astype(jnp.float32)
            value = part if value is None else value + part
        value = value.reshape(row_count, half_width, LAGS)
        row = lax.broadcasted_iota(jnp.int32, value.shape, 0) + scalars[0, 3] * row_count
        col = lax.broadcasted_iota(jnp.int32, value.shape, 1) + half * half_width
        distance = jnp.abs(step * width + col - row)
        kept = (distance > 0) & (distance < reach)
        tile[:, pl.ds(half * half_width, half_width), :] = jnp.where(kept, value * norm_scale, 0.0)


def grouped(refs, counts):
    terms = []
    for at, count in counts:
        if at is not None:
            terms.append((refs.pop(0), at))
        else:
            terms.append([refs.pop(0) for _ in range(count)])
    return terms


def tile_kernel(step, counts, norm_scale, scalars, *refs):
    *terms, tile = refs
    write_tile(scalars, step, grouped(terms, counts), tile, norm_scale)


def flat(terms):
    operands, counts = [], []
    for term in terms:
        listed = isinstance(term, list)
        operands += term if listed else [term[0]]
        counts.append((None, len(term)) if listed else (term[1], 1))
    return operands, counts


def finished_tile(scalars, step, terms, row_count, width, norm_scale):
    operands, counts = flat(terms)
    return pl.pallas_call(
        functools.partial(tile_kernel, step, counts, norm_scale),
        out_shape=jax.ShapeDtypeStruct((row_count, width, LAGS), jnp.float32),
        in_specs=[VMEM] + [VMEM] * len(operands),
        out_specs=VMEM,
        compiler_params=PARAMS,
        cost_estimate=FREE,
    )(scalars, *operands)


def output_kernel(ready_steps, late, after_count, norm_scale, scalars, *refs):
    out, tiles, zeros, sems = refs[-4:]
    slots = out.shape[0]
    ready, rest = refs[: len(ready_steps)], list(refs[len(ready_steps) : -4])

    def copies(slot, source):
        return pltpu.make_async_copy(source, out.at[slot], sems.at[slot])

    def start(step, source):
        for slot in range(slots):
            pl.when(scalars[0, SLOT_AT + slot] == step)(copies(slot, source).start)

    for step, tile in zip(ready_steps, ready):
        start(step, tile)
    zeros[...] = jnp.zeros_like(zeros)
    start(-1, zeros)
    for place, (step, counts) in enumerate(late):
        terms = grouped(rest, counts)

        @pl.when(reach_of(scalars, step) > 0)
        def _(step=step, terms=terms, place=place):
            write_tile(scalars, step, terms, tiles.at[place], norm_scale)

        start(step, tiles.at[place])
    for slot in range(slots):
        copies(slot, zeros).wait()


def write_output(scalars, ready, late, slots, norm_scale, after):
    tile_shape = ready[0][1].shape
    operands, listed = [tile for _, tile in ready], []
    for step, terms in late:
        more, counts = flat(terms)
        operands += more
        listed.append((step, counts))
    return pl.pallas_call(
        functools.partial(output_kernel, [step for step, _ in ready], listed, len(after), norm_scale),
        out_shape=jax.ShapeDtypeStruct((slots,) + tile_shape, jnp.float32),
        in_specs=[VMEM] + [VMEM] * len(operands) + [ANY] * len(after),
        out_specs=ANY,
        scratch_shapes=[
            pltpu.VMEM((len(late),) + tile_shape, jnp.float32),
            pltpu.VMEM(tile_shape, jnp.float32),
            pltpu.SemaphoreType.DMA((slots,)),
        ],
        compiler_params=PARAMS,
        cost_estimate=FREE,
    )(scalars, *operands, *after)


def on_device(spectra, tile_offset, pair_reach):
    blocks = lax.axis_size("chan")
    days, cores = lax.axis_size("day"), lax.axis_size("sub")
    steps = min(MAX_STEPS, blocks - 1)
    wraps = blocks >= 3 and steps == blocks - 1 and days == 2
    local_days, local_windows, width, _, bins = spectra.shape
    norm_scale = 1.0 / math.sqrt(bins * local_days * days * local_windows * cores)
    row_count = width // (days * cores)
    slots = tile_offset.shape[1]
    day, core, block = lax.axis_index("day"), lax.axis_index("sub"), lax.axis_index("chan")
    table = jnp.asarray(lag_table(bins))

    half = width // HALVES
    halves = [
        jnp.transpose(part, (3, 0, 1, 2, 4)).reshape(2, -1, half, bins) for part in fetch_halves(spectra)
    ]
    is_last = (block == blocks - 1).astype(jnp.int32) if wraps else jnp.int32(0)
    scalars = jnp.stack([core, day, is_last, day * cores + core]).astype(jnp.int32)
    scalars = jnp.concatenate([scalars, tile_offset[0], pair_reach[0]])[None]

    def over_cores(sends):
        got = [lax.ppermute(send, "sub", [(k, (k + 1) % cores) for k in range(cores)]) for send in sends]
        return [got[k : k + HALVES] for k in range(0, len(got), HALVES)]

    def over_days(pieces):
        return [
            lax.ppermute(piece, "day", [(k, (k + shift) % days) for k in range(days)])
            for shift, piece in enumerate(pieces, 1)
        ]

    def to_first(piece, shift):
        pairs = [((blocks - 1) * days + k, (k + shift) % days) for k in range(days)]
        return lax.ppermute(piece, ("chan", "day"), pairs)

    keep, sends, own_rows = own_tile(scalars, halves, table, days)
    own_sums = (keep, over_cores(sends))
    ready, late, back, settled = [], [], [], []

    pairs = [(a + 1, a) for a in range(blocks - 1)] + [(0, blocks - 1)] * wraps
    moving = [lax.ppermute(part, "chan", pairs) for part in halves]
    first = first_half_tile(scalars, own_rows, moving[0], table, days, 1, wraps)
    ahead = moving
    after = [x for pair in own_sums[1] for x in pair] if 0 else []
    keep, sends1 = second_half_tile(scalars, own_rows, moving[1], first, table, days, 1, wraps, after)
    sums = (keep, over_cores(sends1))
    pieces = [add_cores([sums, own_sums], shift) for shift in range(1, days)]
    if wraps:
        back = [to_first(add_cores([sums], shift), shift) for shift in range(days)]
    moved = over_days(pieces)
    for step, (keep, got) in enumerate([own_sums, sums]):
        terms = [(keep, 0), got[0]] + [(piece, 1 - step) for piece in moved]
        ready.append((step, finished_tile(scalars, step, terms, row_count, width, norm_scale)))

    waits = [sends[0], first[0]]
    for step in range(2, steps + 1 - wraps):
        pairs = [(a + 1, a) for a in range(blocks - step)]
        ahead = [
            lax.ppermute(lax.optimization_barrier((part, wait))[0], "chan", pairs)
            for part, wait in zip(ahead, waits)
        ]
        rows = row_count * width
        arrived, block = [], {"parts": ahead}
        if days > 1:
            keep, sends2, cols = days_tile(
                scalars, own_rows, table, days, step, range(1, days), (rows // 2, rows // 2), ahead, None, pieces
            )
            sums = (keep, over_cores(sends2))
            arrived = over_days([add_cores([sums], k) for k in range(days - 1)])
            block = {"cols": cols}
        splits = (rows * 3 // 4, rows // 4)
        keep, sends2, _ = days_tile(scalars, own_rows, table, days, step, [0], splits, **block)
        got = [array for arrays in over_cores(sends2) for array in arrays]
        late.append((step, [(keep, 0), got] + [(piece, 0) for piece in arrived]))
    if wraps:
        terms = [(piece, 0) for piece in back]
        hosted = finished_tile(scalars, steps, terms, row_count, width, norm_scale)
        ready.append((steps, hosted))
        pairs = [(c, (c + 1) % cores) for c in range(cores)]
        settled = [lax.ppermute(hosted[:3, :24], "sub", pairs)]
    return write_output(scalars, ready, late, slots, norm_scale, settled)[None]


def solution(mesh):
    in_specs = (P(("groups", "day"), "sub", "chan", None, None), P("chan", None), P("chan", None))
    out_specs = P(("groups", "chan"), None, ("day", "sub"), None, None)
    return jax.shard_map(
        on_device, mesh=mesh, in_specs=in_specs, out_specs=out_specs, check_vma=False
    )
```

```python
import functools
import math

import jax
import jax.numpy as jnp
import ml_dtypes
import numpy as np
from jax import lax
from jax.experimental import pallas as pl
from jax.experimental.pallas import tpu as pltpu
from jax.sharding import PartitionSpec as P

BAND = 32
LAGS = 256
MAX_STEPS = 4
EPSILON = 1e-06
LANES = 128
ROWS = 16
OWN = 4
VMEM_LIMIT = 40 << 20
FAR = 1 << 20
HALVES = 2
SETTLED = 144
SLOT_AT = 4


def lag_table(bin_count):
    bins = np.arange(bin_count, dtype=np.float64)[:, None]
    lags = np.arange(LAGS, dtype=np.float64)[None, :] - LAGS // 2
    angle = np.pi * bins * lags / bin_count
    table = np.concatenate([np.cos(angle), -np.sin(angle)], axis=0).astype(np.float32)
    return table.astype(ml_dtypes.bfloat16)


def whiten(source):
    _, windows, channels, bins = source.shape
    width = 2 * LANES
    row = lax.broadcasted_iota(jnp.int32, (width, width), 0) // BAND
    col = lax.broadcasted_iota(jnp.int32, (width, width), 1) // BAND
    mean_matrix = jnp.where(row == col, 1.0 / BAND, 0.0).astype(jnp.bfloat16)
    for at in range(0, bins, width):
        lanes = pl.ds(at, width)
        real = source[0, :, :, lanes].astype(jnp.float32).reshape(windows * channels, width)
        imag = source[1, :, :, lanes].astype(jnp.float32).reshape(windows * channels, width)
        rest = real * real + imag * imag
        mean = jnp.zeros_like(rest)
        for _ in range(3):
            piece = rest.astype(jnp.bfloat16)
            mean += jnp.dot(piece, mean_matrix, preferred_element_type=jnp.float32)
            rest = rest - piece.astype(jnp.float32)
        scale = lax.rsqrt(mean + EPSILON)
        shape = (windows, channels, width)
        yield (
            lanes,
            (real * scale).astype(jnp.bfloat16).astype(jnp.float32).reshape(shape),
            (imag * scale).astype(jnp.bfloat16).astype(jnp.float32).reshape(shape),
        )


def row_factors(real, imag):
    return real + imag, real, imag


def col_factors(real, imag):
    return real, -(real + imag), real - imag


def store_factors(source, target, begin, factors):
    for lanes, real, imag in whiten(source):
        for k, value in enumerate(factors(real, imag)):
            target[k, :, pl.ds(begin, source.shape[2]), lanes] = value


def reach_of(scalars, step):
    slots = (scalars.shape[1] - SLOT_AT) // 2
    picked = [
        jnp.where(scalars[0, SLOT_AT + k] == step, scalars[0, SLOT_AT + slots + k], 0) for k in range(slots)
    ]
    return functools.reduce(lambda x, y: x + y, picked)


def cross_tile(rows, cols, cross, reach, first_distance, begin=0, row_count=None):
    _, windows, all_rows, bins = rows.shape
    row_count = row_count or all_rows
    groups = cols.shape[2] // ROWS

    def body(step, carry):
        row_to = pl.multiple_of((step // groups) * 8, 8)
        row_at = pl.multiple_of(begin + row_to, 8)
        group = step % groups
        col_at = pl.multiple_of(group * ROWS, ROWS)
        nearest = first_distance + col_at - row_at
        active = (nearest - 7 < reach) & (-(nearest + ROWS - 1) < reach)

        @pl.when(active)
        def _():
            for at in range(0, bins, LANES):
                lanes = pl.ds(at, LANES)
                for first in range(0, 8, OWN):
                    sums = [[None] * 3 for _ in range(OWN)]
                    for w in range(windows):
                        for k in range(3):
                            right = cols[k, w, pl.ds(col_at, ROWS), lanes]
                            left = rows.at[k, w, pl.ds(row_at, 8), lanes]
                            for i in range(OWN):
                                product = right * left[pl.ds(first + i, 1)]
                                sums[i][k] = product if w == 0 else sums[i][k] + product
                    for i in range(OWN):
                        k1, k2, k3 = sums[i]
                        at_row = (group * row_count + row_to + first + i) * ROWS
                        place = pl.ds(pl.multiple_of(at_row, ROWS), ROWS)
                        cross[place, pl.ds(at, LANES)] = (k1 - k3).astype(jnp.bfloat16)
                        cross[place, pl.ds(bins + at, LANES)] = (k1 + k2).astype(jnp.bfloat16)

        return carry

    lax.fori_loop(0, (row_count // 8) * groups, body, 0)


def lag_block(core, cross, begin, table, size, store):
    place = pl.ds(pl.multiple_of(begin, 2 * size), 2 * size)
    lags = jnp.dot(cross[place], table[...], preferred_element_type=jnp.float32)
    low, high = lags[:size], lags[size:]
    pl.when(core == 0)(lambda: store(low, high.astype(jnp.bfloat16)))
    pl.when(core != 0)(lambda: store(high, low.astype(jnp.bfloat16)))


def lag_blocks(core, cross, blocks, table, size, store):
    lags = jnp.dot(cross[: blocks * 2 * size], table[...], preferred_element_type=jnp.float32)
    parts = [(lags[k * 2 * size :][:size], lags[(k * 2 + 1) * size :][:size]) for k in range(blocks)]

    @pl.when(core == 0)
    def _():
        for k, (low, high) in enumerate(parts):
            store(k, low, high.astype(jnp.bfloat16))

    @pl.when(core != 0)
    def _():
        for k, (low, high) in enumerate(parts):
            store(k, high, low.astype(jnp.bfloat16))


def store_at(keep, sends, shift, half):
    def store(kept, sent):
        size = sent.shape[0]
        keep[shift, pl.ds(half * size, size)] = kept
        sends[shift * HALVES + half][0] = sent

    return store


def lag_sums(scalars, cross, table, keep, sends):
    owners, size = keep.shape[0], keep.shape[1] // HALVES
    core, day = scalars[0, 0], scalars[0, 1]
    for shift in range(owners):
        owner = lax.rem(day + shift, owners)
        for half in range(HALVES):
            begin = (half * owners + owner) * (2 * size)
            lag_block(core, cross, begin, table, size, store_at(keep, sends, shift, half))


def begins_of(parts):
    return [sum(p.shape[2] for p in parts[:k]) for k in range(len(parts))]


def own_kernel(part_count, scalars, table, *refs):
    parts = refs[:part_count]
    keep, send, rows, cols, cross = refs[part_count:]
    sends = [send.at[pl.ds(k, 1)] for k in range(send.shape[0])]
    for part, begin in zip(parts, begins_of(parts)):
        for lanes, real, imag in whiten(part):
            for k in range(3):
                rows[k, :, pl.ds(begin, part.shape[2]), lanes] = row_factors(real, imag)[k]
                cols[k, :, pl.ds(begin, part.shape[2]), lanes] = col_factors(real, imag)[k]
    cross_tile(rows, cols, cross, reach_of(scalars, 0), 0)
    lag_sums(scalars, cross, table, keep, sends)


def days_kernel(shifts, owners, part_count, after_count, step, scalars, own_rows, table, *refs):
    parts, refs = refs[:part_count], refs[part_count:]
    if not parts:
        cols, *refs = refs
    keep, *sends, cross = refs[after_count:]
    if parts:
        *sends, cols = sends
    per = len(sends) // len(shifts)
    width = own_rows.shape[2]
    count = width // owners
    size = count * ROWS // 2
    core, day = scalars[0, 0], scalars[0, 1]
    reach = reach_of(scalars, step)

    def store(k, half, kept, sent):
        keep[k, pl.ds(half * size, size)] = kept
        begin = 0
        for send in sends[k * per : (k + 1) * per]:
            low = max(begin, half * size)
            high = min(begin + send.shape[1], (half + 1) * size)
            if low < high:
                send[0, pl.ds(low - begin, high - low)] = sent[low - half * size : high - half * size]
            begin += send.shape[1]

    @pl.when(reach > 0)
    def _():
        for part, begin in zip(parts, begins_of(parts)):
            store_factors(part, cols, begin, col_factors)
        for k, shift in enumerate(shifts):
            begin = lax.rem(day + shift, owners) * count
            cross_tile(own_rows, cols, cross, reach, step * width, begin, count)
            lag_blocks(core, cross, HALVES, table, size, functools.partial(store, k))


def half_cross(can_swap, step, half, scalars, own_rows, part, cols, cross, swap_refs, finish):
    width, count = own_rows.shape[2], part.shape[2]
    reach = reach_of(scalars, step)

    @pl.when(reach > 0)
    def _():
        store_factors(part, cols, 0, col_factors)
        cross_tile(own_rows, cols, cross, reach, step * width + half * count)
        finish(False)

    if can_swap:
        rows, wide_cols = swap_refs

        @pl.when(scalars[0, 2] != 0)
        def _():
            for at in range(0, own_rows.shape[3], LANES):
                lanes = pl.ds(at, LANES)
                real, imag = own_rows[1, :, :, lanes], own_rows[2, :, :, lanes]
                for k, value in enumerate(col_factors(real, imag)):
                    wide_cols[k, :, :, lanes] = value
            store_factors(part, rows, 0, row_factors)
            cross_tile(rows, wide_cols, cross, FAR, 0)
            finish(True)


def first_half_kernel(can_swap, step, scalars, own_rows, table, part, keep, send, cols, cross, *swap_refs):
    owners, size = keep.shape[0], keep.shape[1]

    def finish(swapped):
        def store(k, kept, sent):
            keep[k] = kept
            send[k] = sent

        lag_blocks(scalars[0, 0], cross, owners, table, size, store)

    half_cross(can_swap, step, 0, scalars, own_rows, part, cols, cross, swap_refs, finish)


def second_half_kernel(
    can_swap, step, after_count, scalars, own_rows, table, part, first_keep, first_send, *refs
):
    keep, *refs = refs[after_count:]
    sends = refs[: keep.shape[0] * HALVES]
    cols, cross, *swap_refs = refs[keep.shape[0] * HALVES :]
    owners, size = keep.shape[0], keep.shape[1] // HALVES
    core, day = scalars[0, 0], scalars[0, 1]

    def finish(swapped):
        def store(block, kept, sent):
            for shift in range(owners):
                owner = lax.rem(day + shift, owners)
                half = block if swapped else 1
                here = owner != 0 if swapped else owner == block
                pl.when(here)(lambda: store_at(keep, sends, shift, half)(kept, sent))

        for shift in range(owners):
            owner = lax.rem(day + shift, owners)
            if swapped:
                for half in range(HALVES):
                    copy = functools.partial(
                        store_at(keep, sends, shift, half), first_keep[half], first_send[half]
                    )
                    pl.when(owner == 0)(copy)
            else:
                store_at(keep, sends, shift, 0)(first_keep[owner], first_send[owner])
        lag_blocks(core, cross, HALVES if swapped else owners, table, size, store)

    half_cross(can_swap, step, 1, scalars, own_rows, part, cols, cross, swap_refs, finish)


VMEM = pl.BlockSpec(memory_space=pltpu.VMEM)
ANY = pl.BlockSpec(memory_space=pl.ANY)
FREE = pl.CostEstimate(flops=0, bytes_accessed=0, transcendentals=0)
PARAMS = pltpu.CompilerParams(vmem_limit_bytes=VMEM_LIMIT)


def sums_shapes(owners, width):
    size = width * width // (2 * owners * HALVES)
    return [jax.ShapeDtypeStruct((owners, HALVES * size, LAGS), jnp.float32)] + [
        jax.ShapeDtypeStruct((1, size, LAGS), jnp.bfloat16)
    ] * (owners * HALVES)


def fetch_kernel(source, *refs):
    *parts, sems = refs
    half = parts[0].shape[2]
    copies = [
        pltpu.make_async_copy(source.at[:, :, pl.ds(k * half, half)], part, sems.at[k])
        for k, part in enumerate(parts)
    ]
    for copy in copies:
        copy.start()
    for copy in copies:
        copy.wait()


def fetch_halves(spectra):
    days, windows, width, parts, bins = spectra.shape
    shape = jax.ShapeDtypeStruct((days, windows, width // HALVES, parts, bins), spectra.dtype)
    return pl.pallas_call(
        fetch_kernel,
        out_shape=[shape] * HALVES,
        in_specs=[ANY],
        out_specs=[VMEM] * HALVES,
        scratch_shapes=[pltpu.SemaphoreType.DMA((HALVES,))],
        compiler_params=PARAMS,
        cost_estimate=FREE,
    )(spectra)


def own_tile(scalars, parts, table, owners):
    _, windows, _, bins = parts[0].shape
    width = sum(part.shape[2] for part in parts)
    factors = (3, windows, width, bins)
    keep_shape, *send_shapes = sums_shapes(owners, width)
    sent = jax.ShapeDtypeStruct((len(send_shapes),) + send_shapes[0].shape[1:], send_shapes[0].dtype)
    keep, send, rows = pl.pallas_call(
        functools.partial(own_kernel, len(parts)),
        out_shape=[keep_shape, sent, jax.ShapeDtypeStruct(factors, jnp.float32)],
        in_specs=[VMEM] + [VMEM] * (1 + len(parts)),
        out_specs=[VMEM] * 3,
        scratch_shapes=[
            pltpu.VMEM(factors, jnp.float32),
            pltpu.VMEM((width * width, 2 * bins), jnp.bfloat16),
        ],
        compiler_params=PARAMS,
        cost_estimate=FREE,
    )(scalars, table, *parts)
    return keep, [send], rows


def days_tile(scalars, own_rows, table, owners, step, shifts, splits, parts=(), cols=None, after=()):
    _, windows, width, bins = own_rows.shape
    col_shape = (3, windows, width, bins)
    shapes = [jax.ShapeDtypeStruct((len(shifts), sum(splits), LAGS), jnp.float32)]
    shapes += [jax.ShapeDtypeStruct((1, rows, LAGS), jnp.bfloat16) for rows in splits] * len(shifts)
    if cols is None:
        shapes.append(jax.ShapeDtypeStruct(col_shape, jnp.float32))
    operands = list(parts) if cols is None else [cols]
    keep, *sends = pl.pallas_call(
        functools.partial(days_kernel, shifts, owners, len(parts), len(after), step),
        out_shape=shapes,
        in_specs=[VMEM] * (3 + len(operands)) + [ANY] * len(after),
        out_specs=[VMEM] * len(shapes),
        scratch_shapes=[pltpu.VMEM((width // owners * width, 2 * bins), jnp.bfloat16)],
        compiler_params=PARAMS,
        cost_estimate=FREE,
    )(scalars, own_rows, table, *operands, *after)
    if cols is None:
        *sends, cols = sends
    return keep, sends, cols


def half_scratch(own_rows, can_swap):
    _, windows, width, bins = own_rows.shape
    half = width // HALVES
    wide, narrow = (3, windows, width, bins), (3, windows, half, bins)
    scratch = [pltpu.VMEM(narrow, jnp.float32), pltpu.VMEM((width * half, 2 * bins), jnp.bfloat16)]
    if can_swap:
        scratch += [pltpu.VMEM(narrow, jnp.float32), pltpu.VMEM(wide, jnp.float32)]
    return scratch


def first_half_tile(scalars, own_rows, part, table, owners, step, can_swap):
    width = own_rows.shape[2]
    size = width * width // (2 * owners * HALVES)
    return pl.pallas_call(
        functools.partial(first_half_kernel, can_swap, step),
        out_shape=[
            jax.ShapeDtypeStruct((owners, size, LAGS), jnp.float32),
            jax.ShapeDtypeStruct((owners, size, LAGS), jnp.bfloat16),
        ],
        in_specs=[VMEM, VMEM, VMEM, VMEM],
        out_specs=[VMEM, VMEM],
        scratch_shapes=half_scratch(own_rows, can_swap),
        compiler_params=PARAMS,
        cost_estimate=FREE,
    )(scalars, own_rows, table, part)


def second_half_tile(scalars, own_rows, part, first, table, owners, step, can_swap, after):
    keep, *sends = pl.pallas_call(
        functools.partial(second_half_kernel, can_swap, step, len(after)),
        out_shape=sums_shapes(owners, own_rows.shape[2]),
        in_specs=[VMEM] + [VMEM] * 5 + [ANY] * len(after),
        out_specs=[VMEM] * (owners * HALVES + 1),
        scratch_shapes=half_scratch(own_rows, can_swap),
        compiler_params=PARAMS,
        cost_estimate=FREE,
    )(scalars, own_rows, table, part, *first, *after)
    return keep, sends


def add_kernel(tiles, shift, *refs):
    out = refs[-1]
    for tile, places in enumerate(tiles):
        keep, *got = refs[tile * (1 + HALVES) : (tile + 1) * (1 + HALVES)]
        for half, (sent, at) in enumerate(zip(got, places)):
            place = pl.ds(half * sent.shape[1], sent.shape[1])
            out[tile, place] = (keep[shift, place] + sent[at].astype(jnp.float32)).astype(out.dtype)


def add_cores(tiles, shift, after=()):
    operands = [term for keep, got in tiles for term in [keep] + [array for array, _ in got[shift]]]
    places = [[at for _, at in got[shift]] for _, got in tiles]
    rows = tiles[0][0].shape[1]
    return pl.pallas_call(
        functools.partial(add_kernel, places, shift),
        out_shape=jax.ShapeDtypeStruct((len(tiles), rows, LAGS), jnp.bfloat16),
        in_specs=[VMEM] * len(operands) + [ANY] * len(after),
        out_specs=VMEM,
        compiler_params=PARAMS,
        cost_estimate=FREE,
    )(*operands, *after)


def write_tile(scalars, step, terms, tile, norm_scale):
    row_count, width, _ = tile.shape
    slots = (scalars.shape[1] - SLOT_AT) // 2
    reach = reach_of(scalars, step)
    half_width = width // HALVES
    size = row_count * half_width
    for half in range(HALVES):
        value = None
        for term in terms:
            if isinstance(term, list):
                whole = jnp.concatenate([array[at].astype(jnp.float32) for array, at in term], axis=0)
                part = whole[half * size : (half + 1) * size]
            else:
                array, at = term
                part = array[at, pl.ds(half * size, size)]
            part = part.astype(jnp.float32)
            value = part if value is None else value + part
        value = value.reshape(row_count, half_width, LAGS)
        row = lax.broadcasted_iota(jnp.int32, value.shape, 0) + scalars[0, 3] * row_count
        col = lax.broadcasted_iota(jnp.int32, value.shape, 1) + half * half_width
        distance = jnp.abs(step * width + col - row)
        kept = (distance > 0) & (distance < reach)
        tile[:, pl.ds(half * half_width, half_width), :] = jnp.where(kept, value * norm_scale, 0.0)


def grouped(refs, places):
    terms = []
    for place in places:
        if isinstance(place, list):
            terms.append([(refs.pop(0), at) for at in place])
        else:
            terms.append((refs.pop(0), place))
    return terms


def tile_kernel(step, counts, norm_scale, scalars, *refs):
    *terms, tile = refs
    write_tile(scalars, step, grouped(terms, counts), tile, norm_scale)


def flat(terms):
    operands, places = [], []
    for term in terms:
        listed = isinstance(term, list)
        operands += [array for array, _ in term] if listed else [term[0]]
        places.append([at for _, at in term] if listed else term[1])
    return operands, places


def finished_tile(scalars, step, terms, row_count, width, norm_scale):
    operands, counts = flat(terms)
    return pl.pallas_call(
        functools.partial(tile_kernel, step, counts, norm_scale),
        out_shape=jax.ShapeDtypeStruct((row_count, width, LAGS), jnp.float32),
        in_specs=[VMEM] + [VMEM] * len(operands),
        out_specs=VMEM,
        compiler_params=PARAMS,
        cost_estimate=FREE,
    )(scalars, *operands)


def output_kernel(ready_steps, late, after_count, norm_scale, scalars, *refs):
    out, tiles, zeros, sems = refs[-4:]
    slots = out.shape[0]
    ready, rest = refs[: len(ready_steps)], list(refs[len(ready_steps) : -4])

    def copies(slot, source):
        return pltpu.make_async_copy(source, out.at[slot], sems.at[slot])

    def start(step, source):
        for slot in range(slots):
            pl.when(scalars[0, SLOT_AT + slot] == step)(copies(slot, source).start)

    for step, tile in zip(ready_steps, ready):
        start(step, tile)
    zeros[...] = jnp.zeros_like(zeros)
    start(-1, zeros)
    for place, (step, counts) in enumerate(late):
        terms = grouped(rest, counts)

        @pl.when(reach_of(scalars, step) > 0)
        def _(step=step, terms=terms, place=place):
            write_tile(scalars, step, terms, tiles.at[place], norm_scale)

        start(step, tiles.at[place])
    for slot in range(slots):
        copies(slot, zeros).wait()


def write_output(scalars, ready, late, slots, norm_scale, after):
    tile_shape = ready[0][1].shape
    operands, listed = [tile for _, tile in ready], []
    for step, terms in late:
        more, counts = flat(terms)
        operands += more
        listed.append((step, counts))
    return pl.pallas_call(
        functools.partial(output_kernel, [step for step, _ in ready], listed, len(after), norm_scale),
        out_shape=jax.ShapeDtypeStruct((slots,) + tile_shape, jnp.float32),
        in_specs=[VMEM] + [VMEM] * len(operands) + [ANY] * len(after),
        out_specs=ANY,
        scratch_shapes=[
            pltpu.VMEM((len(late),) + tile_shape, jnp.float32),
            pltpu.VMEM(tile_shape, jnp.float32),
            pltpu.SemaphoreType.DMA((slots,)),
        ],
        compiler_params=PARAMS,
        cost_estimate=FREE,
    )(scalars, *operands, *after)


def on_device(spectra, tile_offset, pair_reach):
    blocks = lax.axis_size("chan")
    days, cores = lax.axis_size("day"), lax.axis_size("sub")
    steps = min(MAX_STEPS, blocks - 1)
    wraps = blocks >= 3 and steps == blocks - 1 and days == 2
    local_days, local_windows, width, _, bins = spectra.shape
    norm_scale = 1.0 / math.sqrt(bins * local_days * days * local_windows * cores)
    row_count = width // (days * cores)
    slots = tile_offset.shape[1]
    day, core, block = lax.axis_index("day"), lax.axis_index("sub"), lax.axis_index("chan")
    table = jnp.asarray(lag_table(bins))

    half = width // HALVES
    halves = [
        jnp.transpose(part, (3, 0, 1, 2, 4)).reshape(2, -1, half, bins) for part in fetch_halves(spectra)
    ]
    is_last = (block == blocks - 1).astype(jnp.int32) if wraps else jnp.int32(0)
    scalars = jnp.stack([core, day, is_last, day * cores + core]).astype(jnp.int32)
    scalars = jnp.concatenate([scalars, tile_offset[0], pair_reach[0]])[None]

    def over_cores(sends):
        got = [lax.ppermute(send, "sub", [(k, (k + 1) % cores) for k in range(cores)]) for send in sends]
        got = [(array, at) for array in got for at in range(array.shape[0])]
        return [got[k : k + HALVES] for k in range(0, len(got), HALVES)]

    def over_days(pieces):
        return [
            lax.ppermute(piece, "day", [(k, (k + shift) % days) for k in range(days)])
            for shift, piece in enumerate(pieces, 1)
        ]

    def to_first(piece, shift):
        pairs = [((blocks - 1) * days + k, (k + shift) % days) for k in range(days)]
        return lax.ppermute(piece, ("chan", "day"), pairs)

    keep, sends, own_rows = own_tile(scalars, halves, table, days)
    own_sums = (keep, over_cores(sends))
    ready, late, back, settled = [], [], [], []

    pairs = [(a + 1, a) for a in range(blocks - 1)] + [(0, blocks - 1)] * wraps
    moving = [lax.ppermute(part, "chan", pairs) for part in halves]
    first = first_half_tile(scalars, own_rows, moving[0], table, days, 1, wraps)
    ahead = moving
    after = [x for pair in own_sums[1] for x in pair] if 0 else []
    keep, sends1 = second_half_tile(scalars, own_rows, moving[1], first, table, days, 1, wraps, after)
    sums = (keep, over_cores(sends1))
    pieces = [add_cores([sums, own_sums], shift) for shift in range(1, days)]
    if wraps:
        back = [to_first(add_cores([sums], shift), shift) for shift in range(days)]
    moved = over_days(pieces)
    for step, (keep, got) in enumerate([own_sums, sums]):
        terms = [(keep, 0), got[0]] + [(piece, 1 - step) for piece in moved]
        ready.append((step, finished_tile(scalars, step, terms, row_count, width, norm_scale)))

    waits = [sends[0], first[0]]
    for step in range(2, steps + 1 - wraps):
        pairs = [(a + 1, a) for a in range(blocks - step)]
        ahead = [
            lax.ppermute(lax.optimization_barrier((part, wait))[0], "chan", pairs)
            for part, wait in zip(ahead, waits)
        ]
        rows = row_count * width
        arrived, block = [], {"parts": ahead}
        if days > 1:
            keep, sends2, cols = days_tile(
                scalars, own_rows, table, days, step, range(1, days), (rows // 2, rows // 2), ahead, None, pieces
            )
            sums = (keep, over_cores(sends2))
            arrived = over_days([add_cores([sums], k) for k in range(days - 1)])
            block = {"cols": cols}
        splits = (rows * 3 // 4, rows // 4)
        keep, sends2, _ = days_tile(scalars, own_rows, table, days, step, [0], splits, **block)
        got = [part for parts in over_cores(sends2) for part in parts]
        late.append((step, [(keep, 0), got] + [(piece, 0) for piece in arrived]))
    if wraps:
        terms = [(piece, 0) for piece in back]
        hosted = finished_tile(scalars, steps, terms, row_count, width, norm_scale)
        ready.append((steps, hosted))
        pairs = [(c, (c + 1) % cores) for c in range(cores)]
        settled = [lax.ppermute(hosted[:3, :24], "sub", pairs)]
    return write_output(scalars, ready, late, slots, norm_scale, settled)[None]


def solution(mesh):
    in_specs = (P(("groups", "day"), "sub", "chan", None, None), P("chan", None), P("chan", None))
    out_specs = P(("groups", "chan"), None, ("day", "sub"), None, None)
    return jax.shard_map(
        on_device, mesh=mesh, in_specs=in_specs, out_specs=out_specs, check_vma=False
    )
```

```python
import functools
import math

import jax
import jax.numpy as jnp
import ml_dtypes
import numpy as np
from jax import lax
from jax.experimental import pallas as pl
from jax.experimental.pallas import tpu as pltpu
from jax.sharding import PartitionSpec as P

BAND = 32
LAGS = 256
MAX_STEPS = 4
EPSILON = 1e-06
LANES = 128
ROWS = 16
OWN = 4
VMEM_LIMIT = 40 << 20
FAR = 1 << 20
HALVES = 2
SETTLED = 144
SLOT_AT = 4


def lag_table(bin_count):
    bins = np.arange(bin_count, dtype=np.float64)[:, None]
    lags = np.arange(LAGS, dtype=np.float64)[None, :] - LAGS // 2
    angle = np.pi * bins * lags / bin_count
    table = np.concatenate([np.cos(angle), -np.sin(angle)], axis=0).astype(np.float32)
    return table.astype(ml_dtypes.bfloat16)


def whiten(source):
    _, windows, channels, bins = source.shape
    width = 2 * LANES
    row = lax.broadcasted_iota(jnp.int32, (width, width), 0) // BAND
    col = lax.broadcasted_iota(jnp.int32, (width, width), 1) // BAND
    mean_matrix = jnp.where(row == col, 1.0 / BAND, 0.0).astype(jnp.bfloat16)
    for at in range(0, bins, width):
        lanes = pl.ds(at, width)
        real = source[0, :, :, lanes].astype(jnp.float32).reshape(windows * channels, width)
        imag = source[1, :, :, lanes].astype(jnp.float32).reshape(windows * channels, width)
        rest = real * real + imag * imag
        mean = jnp.zeros_like(rest)
        for _ in range(3):
            piece = rest.astype(jnp.bfloat16)
            mean += jnp.dot(piece, mean_matrix, preferred_element_type=jnp.float32)
            rest = rest - piece.astype(jnp.float32)
        scale = lax.rsqrt(mean + EPSILON)
        shape = (windows, channels, width)
        yield (
            lanes,
            (real * scale).astype(jnp.bfloat16).astype(jnp.float32).reshape(shape),
            (imag * scale).astype(jnp.bfloat16).astype(jnp.float32).reshape(shape),
        )


def row_factors(real, imag):
    return real + imag, real, imag


def col_factors(real, imag):
    return real, -(real + imag), real - imag


def store_factors(source, target, begin, factors):
    for lanes, real, imag in whiten(source):
        for k, value in enumerate(factors(real, imag)):
            target[k, :, pl.ds(begin, source.shape[2]), lanes] = value


def reach_of(scalars, step):
    slots = (scalars.shape[1] - SLOT_AT) // 2
    picked = [
        jnp.where(scalars[0, SLOT_AT + k] == step, scalars[0, SLOT_AT + slots + k], 0) for k in range(slots)
    ]
    return functools.reduce(lambda x, y: x + y, picked)


def cross_tile(rows, cols, cross, reach, first_distance, begin=0, row_count=None):
    _, windows, all_rows, bins = rows.shape
    row_count = row_count or all_rows
    groups = cols.shape[2] // ROWS

    def body(step, carry):
        row_to = pl.multiple_of((step // groups) * 8, 8)
        row_at = pl.multiple_of(begin + row_to, 8)
        group = step % groups
        col_at = pl.multiple_of(group * ROWS, ROWS)
        nearest = first_distance + col_at - row_at
        active = (nearest - 7 < reach) & (-(nearest + ROWS - 1) < reach)

        @pl.when(active)
        def _():
            for at in range(0, bins, LANES):
                lanes = pl.ds(at, LANES)
                for first in range(0, 8, OWN):
                    sums = [[None] * 3 for _ in range(OWN)]
                    for w in range(windows):
                        for k in range(3):
                            right = cols[k, w, pl.ds(col_at, ROWS), lanes]
                            left = rows.at[k, w, pl.ds(row_at, 8), lanes]
                            for i in range(OWN):
                                product = right * left[pl.ds(first + i, 1)]
                                sums[i][k] = product if w == 0 else sums[i][k] + product
                    for i in range(OWN):
                        k1, k2, k3 = sums[i]
                        at_row = (group * row_count + row_to + first + i) * ROWS
                        place = pl.ds(pl.multiple_of(at_row, ROWS), ROWS)
                        cross[place, pl.ds(at, LANES)] = (k1 - k3).astype(jnp.bfloat16)
                        cross[place, pl.ds(bins + at, LANES)] = (k1 + k2).astype(jnp.bfloat16)

        return carry

    lax.fori_loop(0, (row_count // 8) * groups, body, 0)


def lag_block(core, cross, begin, table, size, store):
    place = pl.ds(pl.multiple_of(begin, 2 * size), 2 * size)
    lags = jnp.dot(cross[place], table[...], preferred_element_type=jnp.float32)
    low, high = lags[:size], lags[size:]
    pl.when(core == 0)(lambda: store(low, high.astype(jnp.bfloat16)))
    pl.when(core != 0)(lambda: store(high, low.astype(jnp.bfloat16)))


def lag_blocks(core, cross, blocks, table, size, store):
    lags = jnp.dot(cross[: blocks * 2 * size], table[...], preferred_element_type=jnp.float32)
    parts = [(lags[k * 2 * size :][:size], lags[(k * 2 + 1) * size :][:size]) for k in range(blocks)]

    @pl.when(core == 0)
    def _():
        for k, (low, high) in enumerate(parts):
            store(k, low, high.astype(jnp.bfloat16))

    @pl.when(core != 0)
    def _():
        for k, (low, high) in enumerate(parts):
            store(k, high, low.astype(jnp.bfloat16))


def store_at(keep, sends, shift, half):
    def store(kept, sent):
        size = sent.shape[0]
        keep[shift, pl.ds(half * size, size)] = kept
        sends[shift * HALVES + half][0] = sent

    return store


def lag_sums(scalars, cross, table, keep, sends):
    owners, size = keep.shape[0], keep.shape[1] // HALVES
    core, day = scalars[0, 0], scalars[0, 1]
    for shift in range(owners):
        owner = lax.rem(day + shift, owners)
        for half in range(HALVES):
            begin = (half * owners + owner) * (2 * size)
            lag_block(core, cross, begin, table, size, store_at(keep, sends, shift, half))


def begins_of(parts):
    return [sum(p.shape[2] for p in parts[:k]) for k in range(len(parts))]


def own_kernel(part_count, scalars, table, *refs):
    parts = refs[:part_count]
    keep, send, rows, cols, cross = refs[part_count:]
    sends = [send.at[pl.ds(k, 1)] for k in range(send.shape[0])]
    for part, begin in zip(parts, begins_of(parts)):
        for lanes, real, imag in whiten(part):
            for k in range(3):
                rows[k, :, pl.ds(begin, part.shape[2]), lanes] = row_factors(real, imag)[k]
                cols[k, :, pl.ds(begin, part.shape[2]), lanes] = col_factors(real, imag)[k]
    cross_tile(rows, cols, cross, reach_of(scalars, 0), 0)
    lag_sums(scalars, cross, table, keep, sends)


def days_kernel(shifts, owners, part_count, after_count, step, scalars, own_rows, table, *refs):
    parts, refs = refs[:part_count], refs[part_count:]
    if not parts:
        cols, *refs = refs
    keep, *sends, cross = refs[after_count:]
    if parts:
        *sends, cols = sends
    per = len(sends) // len(shifts)
    width = own_rows.shape[2]
    count = width // owners
    size = count * ROWS // 2
    core, day = scalars[0, 0], scalars[0, 1]
    reach = reach_of(scalars, step)

    def store(k, half, kept, sent):
        keep[k, pl.ds(half * size, size)] = kept
        begin = 0
        for send in sends[k * per : (k + 1) * per]:
            low = max(begin, half * size)
            high = min(begin + send.shape[1], (half + 1) * size)
            if low < high:
                send[0, pl.ds(low - begin, high - low)] = sent[low - half * size : high - half * size]
            begin += send.shape[1]

    @pl.when(reach > 0)
    def _():
        for part, begin in zip(parts, begins_of(parts)):
            store_factors(part, cols, begin, col_factors)
        for k, shift in enumerate(shifts):
            begin = lax.rem(day + shift, owners) * count
            cross_tile(own_rows, cols, cross, reach, step * width, begin, count)
            lag_blocks(core, cross, HALVES, table, size, functools.partial(store, k))


def half_cross(can_swap, step, half, scalars, own_rows, part, cols, cross, swap_refs, finish):
    width, count = own_rows.shape[2], part.shape[2]
    reach = reach_of(scalars, step)

    @pl.when(reach > 0)
    def _():
        store_factors(part, cols, 0, col_factors)
        cross_tile(own_rows, cols, cross, reach, step * width + half * count)
        finish(False)

    if can_swap:
        rows, wide_cols = swap_refs

        @pl.when(scalars[0, 2] != 0)
        def _():
            for at in range(0, own_rows.shape[3], LANES):
                lanes = pl.ds(at, LANES)
                real, imag = own_rows[1, :, :, lanes], own_rows[2, :, :, lanes]
                for k, value in enumerate(col_factors(real, imag)):
                    wide_cols[k, :, :, lanes] = value
            store_factors(part, rows, 0, row_factors)
            cross_tile(rows, wide_cols, cross, FAR, 0)
            finish(True)


def first_half_kernel(can_swap, step, scalars, own_rows, table, part, keep, send, cols, cross, *swap_refs):
    owners, size = keep.shape[0], keep.shape[1]

    def finish(swapped):
        def store(k, kept, sent):
            keep[k] = kept
            send[k] = sent

        lag_blocks(scalars[0, 0], cross, owners, table, size, store)

    half_cross(can_swap, step, 0, scalars, own_rows, part, cols, cross, swap_refs, finish)


def second_half_kernel(
    can_swap, step, after_count, scalars, own_rows, table, part, first_keep, first_send, *refs
):
    keep, *refs = refs[after_count:]
    sends = refs[: keep.shape[0] * HALVES]
    cols, cross, *swap_refs = refs[keep.shape[0] * HALVES :]
    owners, size = keep.shape[0], keep.shape[1] // HALVES
    core, day = scalars[0, 0], scalars[0, 1]

    def finish(swapped):
        def store(block, kept, sent):
            for shift in range(owners):
                owner = lax.rem(day + shift, owners)
                half = block if swapped else 1
                here = owner != 0 if swapped else owner == block
                pl.when(here)(lambda: store_at(keep, sends, shift, half)(kept, sent))

        for shift in range(owners):
            owner = lax.rem(day + shift, owners)
            if swapped:
                for half in range(HALVES):
                    copy = functools.partial(
                        store_at(keep, sends, shift, half), first_keep[half], first_send[half]
                    )
                    pl.when(owner == 0)(copy)
            else:
                store_at(keep, sends, shift, 0)(first_keep[owner], first_send[owner])
        lag_blocks(core, cross, HALVES if swapped else owners, table, size, store)

    half_cross(can_swap, step, 1, scalars, own_rows, part, cols, cross, swap_refs, finish)


VMEM = pl.BlockSpec(memory_space=pltpu.VMEM)
ANY = pl.BlockSpec(memory_space=pl.ANY)
FREE = pl.CostEstimate(flops=0, bytes_accessed=0, transcendentals=0)
PARAMS = pltpu.CompilerParams(vmem_limit_bytes=VMEM_LIMIT)


def sums_shapes(owners, width):
    size = width * width // (2 * owners * HALVES)
    return [jax.ShapeDtypeStruct((owners, HALVES * size, LAGS), jnp.float32)] + [
        jax.ShapeDtypeStruct((1, size, LAGS), jnp.bfloat16)
    ] * (owners * HALVES)


def fetch_kernel(source, *refs):
    *parts, sems = refs
    half = parts[0].shape[2]
    copies = [
        pltpu.make_async_copy(source.at[:, :, pl.ds(k * half, half)], part, sems.at[k])
        for k, part in enumerate(parts)
    ]
    for copy in copies:
        copy.start()
    for copy in copies:
        copy.wait()


def fetch_halves(spectra):
    days, windows, width, parts, bins = spectra.shape
    shape = jax.ShapeDtypeStruct((days, windows, width // HALVES, parts, bins), spectra.dtype)
    return pl.pallas_call(
        fetch_kernel,
        out_shape=[shape] * HALVES,
        in_specs=[ANY],
        out_specs=[VMEM] * HALVES,
        scratch_shapes=[pltpu.SemaphoreType.DMA((HALVES,))],
        compiler_params=PARAMS,
        cost_estimate=FREE,
    )(spectra)


def own_tile(scalars, parts, table, owners):
    _, windows, _, bins = parts[0].shape
    width = sum(part.shape[2] for part in parts)
    factors = (3, windows, width, bins)
    keep_shape, *send_shapes = sums_shapes(owners, width)
    sent = jax.ShapeDtypeStruct((len(send_shapes),) + send_shapes[0].shape[1:], send_shapes[0].dtype)
    keep, send, rows = pl.pallas_call(
        functools.partial(own_kernel, len(parts)),
        out_shape=[keep_shape, sent, jax.ShapeDtypeStruct(factors, jnp.float32)],
        in_specs=[VMEM] + [VMEM] * (1 + len(parts)),
        out_specs=[VMEM] * 3,
        scratch_shapes=[
            pltpu.VMEM(factors, jnp.float32),
            pltpu.VMEM((width * width, 2 * bins), jnp.bfloat16),
        ],
        compiler_params=PARAMS,
        cost_estimate=FREE,
    )(scalars, table, *parts)
    return keep, [send], rows


def days_tile(scalars, own_rows, table, owners, step, shifts, splits, parts=(), cols=None, after=()):
    _, windows, width, bins = own_rows.shape
    col_shape = (3, windows, width, bins)
    shapes = [jax.ShapeDtypeStruct((len(shifts), sum(splits), LAGS), jnp.float32)]
    shapes += [jax.ShapeDtypeStruct((1, rows, LAGS), jnp.bfloat16) for rows in splits] * len(shifts)
    if cols is None:
        shapes.append(jax.ShapeDtypeStruct(col_shape, jnp.float32))
    operands = list(parts) if cols is None else [cols]
    keep, *sends = pl.pallas_call(
        functools.partial(days_kernel, shifts, owners, len(parts), len(after), step),
        out_shape=shapes,
        in_specs=[VMEM] * (3 + len(operands)) + [ANY] * len(after),
        out_specs=[VMEM] * len(shapes),
        scratch_shapes=[pltpu.VMEM((width // owners * width, 2 * bins), jnp.bfloat16)],
        compiler_params=PARAMS,
        cost_estimate=FREE,
    )(scalars, own_rows, table, *operands, *after)
    if cols is None:
        *sends, cols = sends
    return keep, sends, cols


def half_scratch(own_rows, can_swap):
    _, windows, width, bins = own_rows.shape
    half = width // HALVES
    wide, narrow = (3, windows, width, bins), (3, windows, half, bins)
    scratch = [pltpu.VMEM(narrow, jnp.float32), pltpu.VMEM((width * half, 2 * bins), jnp.bfloat16)]
    if can_swap:
        scratch += [pltpu.VMEM(narrow, jnp.float32), pltpu.VMEM(wide, jnp.float32)]
    return scratch


def first_half_tile(scalars, own_rows, part, table, owners, step, can_swap):
    width = own_rows.shape[2]
    size = width * width // (2 * owners * HALVES)
    return pl.pallas_call(
        functools.partial(first_half_kernel, can_swap, step),
        out_shape=[
            jax.ShapeDtypeStruct((owners, size, LAGS), jnp.float32),
            jax.ShapeDtypeStruct((owners, size, LAGS), jnp.bfloat16),
        ],
        in_specs=[VMEM, VMEM, VMEM, VMEM],
        out_specs=[VMEM, VMEM],
        scratch_shapes=half_scratch(own_rows, can_swap),
        compiler_params=PARAMS,
        cost_estimate=FREE,
    )(scalars, own_rows, table, part)


def second_half_tile(scalars, own_rows, part, first, table, owners, step, can_swap, after):
    keep, *sends = pl.pallas_call(
        functools.partial(second_half_kernel, can_swap, step, len(after)),
        out_shape=sums_shapes(owners, own_rows.shape[2]),
        in_specs=[VMEM] + [VMEM] * 5 + [ANY] * len(after),
        out_specs=[VMEM] * (owners * HALVES + 1),
        scratch_shapes=half_scratch(own_rows, can_swap),
        compiler_params=PARAMS,
        cost_estimate=FREE,
    )(scalars, own_rows, table, part, *first, *after)
    return keep, sends


def add_kernel(tiles, shift, *refs):
    out = refs[-1]
    for tile, places in enumerate(tiles):
        keep, *got = refs[tile * (1 + HALVES) : (tile + 1) * (1 + HALVES)]
        for half, (sent, at) in enumerate(zip(got, places)):
            place = pl.ds(half * sent.shape[1], sent.shape[1])
            out[tile, place] = (keep[shift, place] + sent[at].astype(jnp.float32)).astype(out.dtype)


def add_cores(tiles, shift, after=()):
    operands = [term for keep, got in tiles for term in [keep] + [array for array, _ in got[shift]]]
    places = [[at for _, at in got[shift]] for _, got in tiles]
    rows = tiles[0][0].shape[1]
    return pl.pallas_call(
        functools.partial(add_kernel, places, shift),
        out_shape=jax.ShapeDtypeStruct((len(tiles), rows, LAGS), jnp.bfloat16),
        in_specs=[VMEM] * len(operands) + [ANY] * len(after),
        out_specs=VMEM,
        compiler_params=PARAMS,
        cost_estimate=FREE,
    )(*operands, *after)


def write_tile(scalars, step, terms, tile, norm_scale):
    row_count, width, _ = tile.shape
    slots = (scalars.shape[1] - SLOT_AT) // 2
    reach = reach_of(scalars, step)
    half_width = width // HALVES
    size = row_count * half_width
    for half in range(HALVES):
        value = None
        for term in terms:
            if isinstance(term, list):
                whole = jnp.concatenate([array[at].astype(jnp.float32) for array, at in term], axis=0)
                part = whole[half * size : (half + 1) * size]
            else:
                array, at = term
                part = array[at, pl.ds(half * size, size)]
            part = part.astype(jnp.float32)
            value = part if value is None else value + part
        value = value.reshape(row_count, half_width, LAGS)
        row = lax.broadcasted_iota(jnp.int32, value.shape, 0) + scalars[0, 3] * row_count
        col = lax.broadcasted_iota(jnp.int32, value.shape, 1) + half * half_width
        distance = jnp.abs(step * width + col - row)
        kept = (distance > 0) & (distance < reach)
        tile[:, pl.ds(half * half_width, half_width), :] = jnp.where(kept, value * norm_scale, 0.0)


def grouped(refs, places):
    terms = []
    for place in places:
        if isinstance(place, list):
            terms.append([(refs.pop(0), at) for at in place])
        else:
            terms.append((refs.pop(0), place))
    return terms


def tile_kernel(step, counts, norm_scale, scalars, *refs):
    *terms, tile = refs
    write_tile(scalars, step, grouped(terms, counts), tile, norm_scale)


def flat(terms):
    operands, places = [], []
    for term in terms:
        listed = isinstance(term, list)
        operands += [array for array, _ in term] if listed else [term[0]]
        places.append([at for _, at in term] if listed else term[1])
    return operands, places


def finished_tile(scalars, step, terms, row_count, width, norm_scale):
    operands, counts = flat(terms)
    return pl.pallas_call(
        functools.partial(tile_kernel, step, counts, norm_scale),
        out_shape=jax.ShapeDtypeStruct((row_count, width, LAGS), jnp.float32),
        in_specs=[VMEM] + [VMEM] * len(operands),
        out_specs=VMEM,
        compiler_params=PARAMS,
        cost_estimate=FREE,
    )(scalars, *operands)


def output_kernel(ready_steps, late, after_count, norm_scale, scalars, *refs):
    out, tiles, zeros, sems = refs[-4:]
    slots = out.shape[0]
    ready, rest = refs[: len(ready_steps)], list(refs[len(ready_steps) : -4])

    def copies(slot, source):
        return pltpu.make_async_copy(source, out.at[slot], sems.at[slot])

    def start(step, source):
        for slot in range(slots):
            pl.when(scalars[0, SLOT_AT + slot] == step)(copies(slot, source).start)

    for step, tile in zip(ready_steps, ready):
        start(step, tile)
    zeros[...] = jnp.zeros_like(zeros)
    start(-1, zeros)
    for place, (step, counts) in enumerate(late):
        terms = grouped(rest, counts)

        @pl.when(reach_of(scalars, step) > 0)
        def _(step=step, terms=terms, place=place):
            write_tile(scalars, step, terms, tiles.at[place], norm_scale)

        start(step, tiles.at[place])
    for slot in range(slots):
        copies(slot, zeros).wait()


def write_output(scalars, ready, late, slots, norm_scale, after):
    tile_shape = ready[0][1].shape
    operands, listed = [tile for _, tile in ready], []
    for step, terms in late:
        more, counts = flat(terms)
        operands += more
        listed.append((step, counts))
    return pl.pallas_call(
        functools.partial(output_kernel, [step for step, _ in ready], listed, len(after), norm_scale),
        out_shape=jax.ShapeDtypeStruct((slots,) + tile_shape, jnp.float32),
        in_specs=[VMEM] + [VMEM] * len(operands) + [ANY] * len(after),
        out_specs=ANY,
        scratch_shapes=[
            pltpu.VMEM((len(late),) + tile_shape, jnp.float32),
            pltpu.VMEM(tile_shape, jnp.float32),
            pltpu.SemaphoreType.DMA((slots,)),
        ],
        compiler_params=PARAMS,
        cost_estimate=FREE,
    )(scalars, *operands, *after)


def on_device(spectra, tile_offset, pair_reach):
    blocks = lax.axis_size("chan")
    days, cores = lax.axis_size("day"), lax.axis_size("sub")
    steps = min(MAX_STEPS, blocks - 1)
    wraps = blocks >= 3 and steps == blocks - 1 and days == 2
    local_days, local_windows, width, _, bins = spectra.shape
    norm_scale = 1.0 / math.sqrt(bins * local_days * days * local_windows * cores)
    row_count = width // (days * cores)
    slots = tile_offset.shape[1]
    day, core, block = lax.axis_index("day"), lax.axis_index("sub"), lax.axis_index("chan")
    table = jnp.asarray(lag_table(bins))

    half = width // HALVES
    halves = [
        jnp.transpose(part, (3, 0, 1, 2, 4)).reshape(2, -1, half, bins) for part in fetch_halves(spectra)
    ]
    is_last = (block == blocks - 1).astype(jnp.int32) if wraps else jnp.int32(0)
    scalars = jnp.stack([core, day, is_last, day * cores + core]).astype(jnp.int32)
    scalars = jnp.concatenate([scalars, tile_offset[0], pair_reach[0]])[None]

    def over_cores(sends):
        got = [lax.ppermute(send, "sub", [(k, (k + 1) % cores) for k in range(cores)]) for send in sends]
        got = [(array, at) for array in got for at in range(array.shape[0])]
        return [got[k : k + HALVES] for k in range(0, len(got), HALVES)]

    def over_days(pieces):
        return [
            lax.ppermute(piece, "day", [(k, (k + shift) % days) for k in range(days)])
            for shift, piece in enumerate(pieces, 1)
        ]

    def to_first(piece, shift):
        pairs = [((blocks - 1) * days + k, (k + shift) % days) for k in range(days)]
        return lax.ppermute(piece, ("chan", "day"), pairs)

    keep, sends, own_rows = own_tile(scalars, halves, table, days)
    own_sums = (keep, over_cores(sends))
    ready, late, back, settled = [], [], [], []

    pairs = [(a + 1, a) for a in range(blocks - 1)] + [(0, blocks - 1)] * wraps
    moving = [lax.ppermute(part, "chan", pairs) for part in halves]
    first = first_half_tile(scalars, own_rows, moving[0], table, days, 1, wraps)
    ahead = moving
    after = [x for pair in own_sums[1] for x in pair] if 0 else []
    keep, sends1 = second_half_tile(scalars, own_rows, moving[1], first, table, days, 1, wraps, after)
    sums = (keep, over_cores(sends1))
    pieces = [add_cores([sums, own_sums], shift) for shift in range(1, days)]
    if wraps:
        back = [to_first(add_cores([sums], shift), shift) for shift in reversed(range(days))]
    moved = over_days(pieces)
    for step, (keep, got) in enumerate([own_sums, sums]):
        terms = [(keep, 0), got[0]] + [(piece, 1 - step) for piece in moved]
        ready.append((step, finished_tile(scalars, step, terms, row_count, width, norm_scale)))

    waits = [sends[0], first[0]]
    for step in range(2, steps + 1 - wraps):
        pairs = [(a + 1, a) for a in range(blocks - step)]
        ahead = [
            lax.ppermute(lax.optimization_barrier((part, wait))[0], "chan", pairs)
            for part, wait in zip(ahead, waits)
        ]
        rows = row_count * width
        arrived, block = [], {"parts": ahead}
        if days > 1:
            keep, sends2, cols = days_tile(
                scalars, own_rows, table, days, step, range(1, days), (rows // 2, rows // 2), ahead, None, pieces
            )
            sums = (keep, over_cores(sends2))
            arrived = over_days([add_cores([sums], k) for k in range(days - 1)])
            block = {"cols": cols}
        splits = (rows * 3 // 4, rows // 4)
        keep, sends2, _ = days_tile(scalars, own_rows, table, days, step, [0], splits, **block)
        got = [part for parts in over_cores(sends2) for part in parts]
        late.append((step, [(keep, 0), got] + [(piece, 0) for piece in arrived]))
    if wraps:
        terms = [(piece, 0) for piece in back]
        hosted = finished_tile(scalars, steps, terms, row_count, width, norm_scale)
        ready.append((steps, hosted))
        pairs = [(c, (c + 1) % cores) for c in range(cores)]
        settled = [lax.ppermute(hosted[:3, :24], "sub", pairs)]
    return write_output(scalars, ready, late, slots, norm_scale, settled)[None]


def solution(mesh):
    in_specs = (P(("groups", "day"), "sub", "chan", None, None), P("chan", None), P("chan", None))
    out_specs = P(("groups", "chan"), None, ("day", "sub"), None, None)
    return jax.shard_map(
        on_device, mesh=mesh, in_specs=in_specs, out_specs=out_specs, check_vma=False
    )
```

```python
import functools
import math

import jax
import jax.numpy as jnp
import ml_dtypes
import numpy as np
from jax import lax
from jax.experimental import pallas as pl
from jax.experimental.pallas import tpu as pltpu
from jax.sharding import PartitionSpec as P

BAND = 32
LAGS = 256
MAX_STEPS = 4
EPSILON = 1e-06
LANES = 128
ROWS = 16
OWN = 4
VMEM_LIMIT = 40 << 20
FAR = 1 << 20
HALVES = 2
SETTLED = 144
SLOT_AT = 4


def lag_table(bin_count):
    bins = np.arange(bin_count, dtype=np.float64)[:, None]
    lags = np.arange(LAGS, dtype=np.float64)[None, :] - LAGS // 2
    angle = np.pi * bins * lags / bin_count
    table = np.concatenate([np.cos(angle), -np.sin(angle)], axis=0).astype(np.float32)
    return table.astype(ml_dtypes.bfloat16)


def whiten(source):
    _, windows, channels, bins = source.shape
    width = 2 * LANES
    row = lax.broadcasted_iota(jnp.int32, (width, width), 0) // BAND
    col = lax.broadcasted_iota(jnp.int32, (width, width), 1) // BAND
    mean_matrix = jnp.where(row == col, 1.0 / BAND, 0.0).astype(jnp.bfloat16)
    for at in range(0, bins, width):
        lanes = pl.ds(at, width)
        real = source[0, :, :, lanes].astype(jnp.float32).reshape(windows * channels, width)
        imag = source[1, :, :, lanes].astype(jnp.float32).reshape(windows * channels, width)
        rest = real * real + imag * imag
        mean = jnp.zeros_like(rest)
        for _ in range(3):
            piece = rest.astype(jnp.bfloat16)
            mean += jnp.dot(piece, mean_matrix, preferred_element_type=jnp.float32)
            rest = rest - piece.astype(jnp.float32)
        scale = lax.rsqrt(mean + EPSILON)
        shape = (windows, channels, width)
        yield (
            lanes,
            (real * scale).astype(jnp.bfloat16).astype(jnp.float32).reshape(shape),
            (imag * scale).astype(jnp.bfloat16).astype(jnp.float32).reshape(shape),
        )


def row_factors(real, imag):
    return real + imag, real, imag


def col_factors(real, imag):
    return real, -(real + imag), real - imag


def store_factors(source, target, begin, factors):
    for lanes, real, imag in whiten(source):
        for k, value in enumerate(factors(real, imag)):
            target[k, :, pl.ds(begin, source.shape[2]), lanes] = value


def reach_of(scalars, step):
    slots = (scalars.shape[1] - SLOT_AT) // 2
    picked = [
        jnp.where(scalars[0, SLOT_AT + k] == step, scalars[0, SLOT_AT + slots + k], 0) for k in range(slots)
    ]
    return functools.reduce(lambda x, y: x + y, picked)


def cross_tile(rows, cols, cross, reach, first_distance, begin=0, row_count=None):
    _, windows, all_rows, bins = rows.shape
    row_count = row_count or all_rows
    groups = cols.shape[2] // ROWS

    def body(step, carry):
        row_to = pl.multiple_of((step // groups) * 8, 8)
        row_at = pl.multiple_of(begin + row_to, 8)
        group = step % groups
        col_at = pl.multiple_of(group * ROWS, ROWS)
        nearest = first_distance + col_at - row_at
        active = (nearest - 7 < reach) & (-(nearest + ROWS - 1) < reach)

        @pl.when(active)
        def _():
            for at in range(0, bins, LANES):
                lanes = pl.ds(at, LANES)
                for first in range(0, 8, OWN):
                    sums = [[None] * 3 for _ in range(OWN)]
                    for w in range(windows):
                        for k in range(3):
                            right = cols[k, w, pl.ds(col_at, ROWS), lanes]
                            left = rows.at[k, w, pl.ds(row_at, 8), lanes]
                            for i in range(OWN):
                                product = right * left[pl.ds(first + i, 1)]
                                sums[i][k] = product if w == 0 else sums[i][k] + product
                    for i in range(OWN):
                        k1, k2, k3 = sums[i]
                        at_row = (group * row_count + row_to + first + i) * ROWS
                        place = pl.ds(pl.multiple_of(at_row, ROWS), ROWS)
                        cross[place, pl.ds(at, LANES)] = (k1 - k3).astype(jnp.bfloat16)
                        cross[place, pl.ds(bins + at, LANES)] = (k1 + k2).astype(jnp.bfloat16)

        return carry

    lax.fori_loop(0, (row_count // 8) * groups, body, 0)


def lag_block(core, cross, begin, table, size, store):
    place = pl.ds(pl.multiple_of(begin, 2 * size), 2 * size)
    lags = jnp.dot(cross[place], table[...], preferred_element_type=jnp.float32)
    low, high = lags[:size], lags[size:]
    pl.when(core == 0)(lambda: store(low, high.astype(jnp.bfloat16)))
    pl.when(core != 0)(lambda: store(high, low.astype(jnp.bfloat16)))


def lag_blocks(core, cross, blocks, table, size, store):
    lags = jnp.dot(cross[: blocks * 2 * size], table[...], preferred_element_type=jnp.float32)
    parts = [(lags[k * 2 * size :][:size], lags[(k * 2 + 1) * size :][:size]) for k in range(blocks)]

    @pl.when(core == 0)
    def _():
        for k, (low, high) in enumerate(parts):
            store(k, low, high.astype(jnp.bfloat16))

    @pl.when(core != 0)
    def _():
        for k, (low, high) in enumerate(parts):
            store(k, high, low.astype(jnp.bfloat16))


def store_at(keep, sends, shift, half):
    def store(kept, sent):
        size = sent.shape[0]
        keep[shift, pl.ds(half * size, size)] = kept
        sends[shift * HALVES + half][0] = sent

    return store


def lag_sums(scalars, cross, table, keep, sends):
    owners, size = keep.shape[0], keep.shape[1] // HALVES
    core, day = scalars[0, 0], scalars[0, 1]
    for shift in range(owners):
        owner = lax.rem(day + shift, owners)
        for half in range(HALVES):
            begin = (half * owners + owner) * (2 * size)
            lag_block(core, cross, begin, table, size, store_at(keep, sends, shift, half))


def begins_of(parts):
    return [sum(p.shape[2] for p in parts[:k]) for k in range(len(parts))]


def own_kernel(part_count, scalars, table, *refs):
    parts = refs[:part_count]
    keep, send, rows, cols, cross = refs[part_count:]
    sends = [send.at[pl.ds(k, 1)] for k in range(send.shape[0])]
    for part, begin in zip(parts, begins_of(parts)):
        for lanes, real, imag in whiten(part):
            for k in range(3):
                rows[k, :, pl.ds(begin, part.shape[2]), lanes] = row_factors(real, imag)[k]
                cols[k, :, pl.ds(begin, part.shape[2]), lanes] = col_factors(real, imag)[k]
    cross_tile(rows, cols, cross, reach_of(scalars, 0), 0)
    lag_sums(scalars, cross, table, keep, sends)


def days_kernel(shifts, owners, part_count, after_count, step, scalars, own_rows, table, *refs):
    parts, refs = refs[:part_count], refs[part_count:]
    if not parts:
        cols, *refs = refs
    keep, *sends, cross = refs[after_count:]
    if parts:
        *sends, cols = sends
    per = len(sends) // len(shifts)
    width = own_rows.shape[2]
    count = width // owners
    size = count * ROWS // 2
    core, day = scalars[0, 0], scalars[0, 1]
    reach = reach_of(scalars, step)

    def store(k, half, kept, sent):
        keep[k, pl.ds(half * size, size)] = kept
        begin = 0
        for send in sends[k * per : (k + 1) * per]:
            low = max(begin, half * size)
            high = min(begin + send.shape[1], (half + 1) * size)
            if low < high:
                send[0, pl.ds(low - begin, high - low)] = sent[low - half * size : high - half * size]
            begin += send.shape[1]

    @pl.when(reach > 0)
    def _():
        for part, begin in zip(parts, begins_of(parts)):
            store_factors(part, cols, begin, col_factors)
        for k, shift in enumerate(shifts):
            begin = lax.rem(day + shift, owners) * count
            cross_tile(own_rows, cols, cross, reach, step * width, begin, count)
            lag_blocks(core, cross, HALVES, table, size, functools.partial(store, k))


def half_cross(can_swap, step, half, scalars, own_rows, part, cols, cross, swap_refs, finish):
    width, count = own_rows.shape[2], part.shape[2]
    reach = reach_of(scalars, step)

    @pl.when(reach > 0)
    def _():
        store_factors(part, cols, 0, col_factors)
        cross_tile(own_rows, cols, cross, reach, step * width + half * count)
        finish(False)

    if can_swap:
        rows, wide_cols = swap_refs

        @pl.when(scalars[0, 2] != 0)
        def _():
            for at in range(0, own_rows.shape[3], LANES):
                lanes = pl.ds(at, LANES)
                real, imag = own_rows[1, :, :, lanes], own_rows[2, :, :, lanes]
                for k, value in enumerate(col_factors(real, imag)):
                    wide_cols[k, :, :, lanes] = value
            store_factors(part, rows, 0, row_factors)
            cross_tile(rows, wide_cols, cross, FAR, 0)
            finish(True)


def first_half_kernel(can_swap, step, scalars, own_rows, table, part, keep, send, cols, cross, *swap_refs):
    owners, size = keep.shape[0], keep.shape[1]

    def finish(swapped):
        def store(k, kept, sent):
            keep[k] = kept
            send[k] = sent

        lag_blocks(scalars[0, 0], cross, owners, table, size, store)

    half_cross(can_swap, step, 0, scalars, own_rows, part, cols, cross, swap_refs, finish)


def second_half_kernel(
    can_swap, step, after_count, scalars, own_rows, table, part, first_keep, first_send, *refs
):
    keep, *refs = refs[after_count:]
    sends = refs[: keep.shape[0] * HALVES]
    cols, cross, *swap_refs = refs[keep.shape[0] * HALVES :]
    owners, size = keep.shape[0], keep.shape[1] // HALVES
    core, day = scalars[0, 0], scalars[0, 1]

    def finish(swapped):
        def store(block, kept, sent):
            for shift in range(owners):
                owner = lax.rem(day + shift, owners)
                half = block if swapped else 1
                here = owner != 0 if swapped else owner == block
                pl.when(here)(lambda: store_at(keep, sends, shift, half)(kept, sent))

        for shift in range(owners):
            owner = lax.rem(day + shift, owners)
            if swapped:
                for half in range(HALVES):
                    copy = functools.partial(
                        store_at(keep, sends, shift, half), first_keep[half], first_send[half]
                    )
                    pl.when(owner == 0)(copy)
            else:
                store_at(keep, sends, shift, 0)(first_keep[owner], first_send[owner])
        lag_blocks(core, cross, HALVES if swapped else owners, table, size, store)

    half_cross(can_swap, step, 1, scalars, own_rows, part, cols, cross, swap_refs, finish)


VMEM = pl.BlockSpec(memory_space=pltpu.VMEM)
ANY = pl.BlockSpec(memory_space=pl.ANY)
FREE = pl.CostEstimate(flops=0, bytes_accessed=0, transcendentals=0)
PARAMS = pltpu.CompilerParams(vmem_limit_bytes=VMEM_LIMIT)


def sums_shapes(owners, width):
    size = width * width // (2 * owners * HALVES)
    return [jax.ShapeDtypeStruct((owners, HALVES * size, LAGS), jnp.float32)] + [
        jax.ShapeDtypeStruct((1, size, LAGS), jnp.bfloat16)
    ] * (owners * HALVES)


def fetch_kernel(source, *refs):
    *parts, sems = refs
    half = parts[0].shape[2]
    copies = [
        pltpu.make_async_copy(source.at[:, :, pl.ds(k * half, half)], part, sems.at[k])
        for k, part in enumerate(parts)
    ]
    for copy in copies:
        copy.start()
    for copy in copies:
        copy.wait()


def fetch_halves(spectra):
    days, windows, width, parts, bins = spectra.shape
    shape = jax.ShapeDtypeStruct((days, windows, width // HALVES, parts, bins), spectra.dtype)
    return pl.pallas_call(
        fetch_kernel,
        out_shape=[shape] * HALVES,
        in_specs=[ANY],
        out_specs=[VMEM] * HALVES,
        scratch_shapes=[pltpu.SemaphoreType.DMA((HALVES,))],
        compiler_params=PARAMS,
        cost_estimate=FREE,
    )(spectra)


def own_tile(scalars, parts, table, owners):
    _, windows, _, bins = parts[0].shape
    width = sum(part.shape[2] for part in parts)
    factors = (3, windows, width, bins)
    keep_shape, *send_shapes = sums_shapes(owners, width)
    sent = jax.ShapeDtypeStruct((len(send_shapes),) + send_shapes[0].shape[1:], send_shapes[0].dtype)
    keep, send, rows = pl.pallas_call(
        functools.partial(own_kernel, len(parts)),
        out_shape=[keep_shape, sent, jax.ShapeDtypeStruct(factors, jnp.float32)],
        in_specs=[VMEM] + [VMEM] * (1 + len(parts)),
        out_specs=[VMEM] * 3,
        scratch_shapes=[
            pltpu.VMEM(factors, jnp.float32),
            pltpu.VMEM((width * width, 2 * bins), jnp.bfloat16),
        ],
        compiler_params=PARAMS,
        cost_estimate=FREE,
    )(scalars, table, *parts)
    return keep, [send], rows


def days_tile(scalars, own_rows, table, owners, step, shifts, splits, parts=(), cols=None, after=()):
    _, windows, width, bins = own_rows.shape
    col_shape = (3, windows, width, bins)
    shapes = [jax.ShapeDtypeStruct((len(shifts), sum(splits), LAGS), jnp.float32)]
    shapes += [jax.ShapeDtypeStruct((1, rows, LAGS), jnp.bfloat16) for rows in splits] * len(shifts)
    if cols is None:
        shapes.append(jax.ShapeDtypeStruct(col_shape, jnp.float32))
    operands = list(parts) if cols is None else [cols]
    keep, *sends = pl.pallas_call(
        functools.partial(days_kernel, shifts, owners, len(parts), len(after), step),
        out_shape=shapes,
        in_specs=[VMEM] * (3 + len(operands)) + [ANY] * len(after),
        out_specs=[VMEM] * len(shapes),
        scratch_shapes=[pltpu.VMEM((width // owners * width, 2 * bins), jnp.bfloat16)],
        compiler_params=PARAMS,
        cost_estimate=FREE,
    )(scalars, own_rows, table, *operands, *after)
    if cols is None:
        *sends, cols = sends
    return keep, sends, cols


def half_scratch(own_rows, can_swap):
    _, windows, width, bins = own_rows.shape
    half = width // HALVES
    wide, narrow = (3, windows, width, bins), (3, windows, half, bins)
    scratch = [pltpu.VMEM(narrow, jnp.float32), pltpu.VMEM((width * half, 2 * bins), jnp.bfloat16)]
    if can_swap:
        scratch += [pltpu.VMEM(narrow, jnp.float32), pltpu.VMEM(wide, jnp.float32)]
    return scratch


def first_half_tile(scalars, own_rows, part, table, owners, step, can_swap):
    width = own_rows.shape[2]
    size = width * width // (2 * owners * HALVES)
    return pl.pallas_call(
        functools.partial(first_half_kernel, can_swap, step),
        out_shape=[
            jax.ShapeDtypeStruct((owners, size, LAGS), jnp.float32),
            jax.ShapeDtypeStruct((owners, size, LAGS), jnp.bfloat16),
        ],
        in_specs=[VMEM, VMEM, VMEM, VMEM],
        out_specs=[VMEM, VMEM],
        scratch_shapes=half_scratch(own_rows, can_swap),
        compiler_params=PARAMS,
        cost_estimate=FREE,
    )(scalars, own_rows, table, part)


def second_half_tile(scalars, own_rows, part, first, table, owners, step, can_swap, after):
    keep, *sends = pl.pallas_call(
        functools.partial(second_half_kernel, can_swap, step, len(after)),
        out_shape=sums_shapes(owners, own_rows.shape[2]),
        in_specs=[VMEM] + [VMEM] * 5 + [ANY] * len(after),
        out_specs=[VMEM] * (owners * HALVES + 1),
        scratch_shapes=half_scratch(own_rows, can_swap),
        compiler_params=PARAMS,
        cost_estimate=FREE,
    )(scalars, own_rows, table, part, *first, *after)
    return keep, sends


def add_kernel(tiles, shift, *refs):
    out = refs[-1]
    for tile, places in enumerate(tiles):
        keep, *got = refs[tile * (1 + HALVES) : (tile + 1) * (1 + HALVES)]
        for half, (sent, at) in enumerate(zip(got, places)):
            place = pl.ds(half * sent.shape[1], sent.shape[1])
            out[tile, place] = (keep[shift, place] + sent[at].astype(jnp.float32)).astype(out.dtype)


def add_cores(tiles, shift, after=()):
    operands = [term for keep, got in tiles for term in [keep] + [array for array, _ in got[shift]]]
    places = [[at for _, at in got[shift]] for _, got in tiles]
    rows = tiles[0][0].shape[1]
    return pl.pallas_call(
        functools.partial(add_kernel, places, shift),
        out_shape=jax.ShapeDtypeStruct((len(tiles), rows, LAGS), jnp.bfloat16),
        in_specs=[VMEM] * len(operands) + [ANY] * len(after),
        out_specs=VMEM,
        compiler_params=PARAMS,
        cost_estimate=FREE,
    )(*operands, *after)


def write_tile(scalars, step, terms, tile, norm_scale):
    row_count, width, _ = tile.shape
    slots = (scalars.shape[1] - SLOT_AT) // 2
    reach = reach_of(scalars, step)
    half_width = width // HALVES
    size = row_count * half_width
    for half in range(HALVES):
        value = None
        for term in terms:
            if isinstance(term, list):
                whole = jnp.concatenate([array[at].astype(jnp.float32) for array, at in term], axis=0)
                part = whole[half * size : (half + 1) * size]
            else:
                array, at = term
                part = array[at, pl.ds(half * size, size)]
            part = part.astype(jnp.float32)
            value = part if value is None else value + part
        value = value.reshape(row_count, half_width, LAGS)
        row = lax.broadcasted_iota(jnp.int32, value.shape, 0) + scalars[0, 3] * row_count
        col = lax.broadcasted_iota(jnp.int32, value.shape, 1) + half * half_width
        distance = jnp.abs(step * width + col - row)
        kept = (distance > 0) & (distance < reach)
        tile[:, pl.ds(half * half_width, half_width), :] = jnp.where(kept, value * norm_scale, 0.0)


def grouped(refs, places):
    terms = []
    for place in places:
        if isinstance(place, list):
            terms.append([(refs.pop(0), at) for at in place])
        else:
            terms.append((refs.pop(0), place))
    return terms


def tile_kernel(listed, norm_scale, scalars, *refs):
    rest, tiles = list(refs[: -len(listed)]), refs[-len(listed) :]
    for (step, places), tile in zip(listed, tiles):
        write_tile(scalars, step, grouped(rest, places), tile, norm_scale)


def flat(terms):
    operands, places = [], []
    for term in terms:
        listed = isinstance(term, list)
        operands += [array for array, _ in term] if listed else [term[0]]
        places.append([at for _, at in term] if listed else term[1])
    return operands, places


def finished_tiles(scalars, summed, row_count, width, norm_scale):
    operands, listed = [], []
    for step, terms in summed:
        more, places = flat(terms)
        operands += more
        listed.append((step, places))
    tile = jax.ShapeDtypeStruct((row_count, width, LAGS), jnp.float32)
    tiles = pl.pallas_call(
        functools.partial(tile_kernel, listed, norm_scale),
        out_shape=[tile] * len(listed),
        in_specs=[VMEM] + [VMEM] * len(operands),
        out_specs=[VMEM] * len(listed),
        compiler_params=PARAMS,
        cost_estimate=FREE,
    )(scalars, *operands)
    return [(step, tile) for (step, _), tile in zip(summed, tiles)]


def output_kernel(ready_steps, late, after_count, norm_scale, scalars, *refs):
    out, tiles, zeros, sems = refs[-4:]
    slots = out.shape[0]
    ready, rest = refs[: len(ready_steps)], list(refs[len(ready_steps) : -4])

    def copies(slot, source):
        return pltpu.make_async_copy(source, out.at[slot], sems.at[slot])

    def start(step, source):
        for slot in range(slots):
            pl.when(scalars[0, SLOT_AT + slot] == step)(copies(slot, source).start)

    for step, tile in zip(ready_steps, ready):
        start(step, tile)
    zeros[...] = jnp.zeros_like(zeros)
    start(-1, zeros)
    for place, (step, counts) in enumerate(late):
        terms = grouped(rest, counts)

        @pl.when(reach_of(scalars, step) > 0)
        def _(step=step, terms=terms, place=place):
            write_tile(scalars, step, terms, tiles.at[place], norm_scale)

        start(step, tiles.at[place])
    for slot in range(slots):
        copies(slot, zeros).wait()


def write_output(scalars, ready, late, slots, norm_scale, after):
    tile_shape = ready[0][1].shape
    operands, listed = [tile for _, tile in ready], []
    for step, terms in late:
        more, counts = flat(terms)
        operands += more
        listed.append((step, counts))
    return pl.pallas_call(
        functools.partial(output_kernel, [step for step, _ in ready], listed, len(after), norm_scale),
        out_shape=jax.ShapeDtypeStruct((slots,) + tile_shape, jnp.float32),
        in_specs=[VMEM] + [VMEM] * len(operands) + [ANY] * len(after),
        out_specs=ANY,
        scratch_shapes=[
            pltpu.VMEM((len(late),) + tile_shape, jnp.float32),
            pltpu.VMEM(tile_shape, jnp.float32),
            pltpu.SemaphoreType.DMA((slots,)),
        ],
        compiler_params=PARAMS,
        cost_estimate=FREE,
    )(scalars, *operands, *after)


def on_device(spectra, tile_offset, pair_reach):
    blocks = lax.axis_size("chan")
    days, cores = lax.axis_size("day"), lax.axis_size("sub")
    steps = min(MAX_STEPS, blocks - 1)
    wraps = blocks >= 3 and steps == blocks - 1 and days == 2
    local_days, local_windows, width, _, bins = spectra.shape
    norm_scale = 1.0 / math.sqrt(bins * local_days * days * local_windows * cores)
    row_count = width // (days * cores)
    slots = tile_offset.shape[1]
    day, core, block = lax.axis_index("day"), lax.axis_index("sub"), lax.axis_index("chan")
    table = jnp.asarray(lag_table(bins))

    half = width // HALVES
    halves = [
        jnp.transpose(part, (3, 0, 1, 2, 4)).reshape(2, -1, half, bins) for part in fetch_halves(spectra)
    ]
    is_last = (block == blocks - 1).astype(jnp.int32) if wraps else jnp.int32(0)
    scalars = jnp.stack([core, day, is_last, day * cores + core]).astype(jnp.int32)
    scalars = jnp.concatenate([scalars, tile_offset[0], pair_reach[0]])[None]

    def over_cores(sends):
        got = [lax.ppermute(send, "sub", [(k, (k + 1) % cores) for k in range(cores)]) for send in sends]
        got = [(array, at) for array in got for at in range(array.shape[0])]
        return [got[k : k + HALVES] for k in range(0, len(got), HALVES)]

    def over_days(pieces):
        return [
            lax.ppermute(piece, "day", [(k, (k + shift) % days) for k in range(days)])
            for shift, piece in enumerate(pieces, 1)
        ]

    def to_first(piece, shift):
        pairs = [((blocks - 1) * days + k, (k + shift) % days) for k in range(days)]
        return lax.ppermute(piece, ("chan", "day"), pairs)

    keep, sends, own_rows = own_tile(scalars, halves, table, days)
    own_sums = (keep, over_cores(sends))
    ready, late, back, settled = [], [], [], []

    pairs = [(a + 1, a) for a in range(blocks - 1)] + [(0, blocks - 1)] * wraps
    moving = [lax.ppermute(part, "chan", pairs) for part in halves]
    first = first_half_tile(scalars, own_rows, moving[0], table, days, 1, wraps)
    ahead = moving
    after = [x for pair in own_sums[1] for x in pair] if 0 else []
    keep, sends1 = second_half_tile(scalars, own_rows, moving[1], first, table, days, 1, wraps, after)
    sums = (keep, over_cores(sends1))
    pieces = [add_cores([sums, own_sums], shift) for shift in range(1, days)]
    if wraps:
        back = [to_first(add_cores([sums], shift), shift) for shift in reversed(range(days))]
    moved = over_days(pieces)
    summed = [
        (step, [(keep, 0), got[0]] + [(piece, 1 - step) for piece in moved])
        for step, (keep, got) in enumerate([own_sums, sums])
    ]
    ready += finished_tiles(scalars, summed, row_count, width, norm_scale)

    waits = [sends[0], first[0]]
    for step in range(2, steps + 1 - wraps):
        pairs = [(a + 1, a) for a in range(blocks - step)]
        ahead = [
            lax.ppermute(lax.optimization_barrier((part, wait))[0], "chan", pairs)
            for part, wait in zip(ahead, waits)
        ]
        rows = row_count * width
        arrived, block = [], {"parts": ahead}
        if days > 1:
            keep, sends2, cols = days_tile(
                scalars, own_rows, table, days, step, range(1, days), (rows // 2, rows // 2), ahead, None, pieces
            )
            sums = (keep, over_cores(sends2))
            arrived = over_days([add_cores([sums], k) for k in range(days - 1)])
            block = {"cols": cols}
        splits = (rows * 3 // 4, rows // 4)
        keep, sends2, _ = days_tile(scalars, own_rows, table, days, step, [0], splits, **block)
        got = [part for parts in over_cores(sends2) for part in parts]
        late.append((step, [(keep, 0), got] + [(piece, 0) for piece in arrived]))
    if wraps:
        terms = [(piece, 0) for piece in back]
        ((_, hosted),) = finished_tiles(scalars, [(steps, terms)], row_count, width, norm_scale)
        ready.append((steps, hosted))
        pairs = [(c, (c + 1) % cores) for c in range(cores)]
        settled = [lax.ppermute(hosted[:3, :24], "sub", pairs)]
    return write_output(scalars, ready, late, slots, norm_scale, settled)[None]


def solution(mesh):
    in_specs = (P(("groups", "day"), "sub", "chan", None, None), P("chan", None), P("chan", None))
    out_specs = P(("groups", "chan"), None, ("day", "sub"), None, None)
    return jax.shard_map(
        on_device, mesh=mesh, in_specs=in_specs, out_specs=out_specs, check_vma=False
    )
```

```python
import functools
import math

import jax
import jax.numpy as jnp
import ml_dtypes
import numpy as np
from jax import lax
from jax.experimental import pallas as pl
from jax.experimental.pallas import tpu as pltpu
from jax.sharding import PartitionSpec as P

BAND = 32
LAGS = 256
MAX_STEPS = 4
EPSILON = 1e-06
LANES = 128
ROWS = 16
OWN = 4
VMEM_LIMIT = 40 << 20
FAR = 1 << 20
HALVES = 2
SETTLED = 144
SLOT_AT = 4


def lag_table(bin_count):
    bins = np.arange(bin_count, dtype=np.float64)[:, None]
    lags = np.arange(LAGS, dtype=np.float64)[None, :] - LAGS // 2
    angle = np.pi * bins * lags / bin_count
    table = np.concatenate([np.cos(angle), -np.sin(angle)], axis=0).astype(np.float32)
    return table.astype(ml_dtypes.bfloat16)


def whiten(source):
    _, windows, channels, bins = source.shape
    width = 2 * LANES
    row = lax.broadcasted_iota(jnp.int32, (width, width), 0) // BAND
    col = lax.broadcasted_iota(jnp.int32, (width, width), 1) // BAND
    mean_matrix = jnp.where(row == col, 1.0 / BAND, 0.0).astype(jnp.bfloat16)
    for at in range(0, bins, width):
        lanes = pl.ds(at, width)
        real = source[0, :, :, lanes].astype(jnp.float32).reshape(windows * channels, width)
        imag = source[1, :, :, lanes].astype(jnp.float32).reshape(windows * channels, width)
        power = real * real + imag * imag
        high = power.astype(jnp.bfloat16)
        low = (power - high.astype(jnp.float32)).astype(jnp.bfloat16)
        pieces = jnp.concatenate([high, low], axis=0)
        means = jnp.dot(pieces, mean_matrix, preferred_element_type=jnp.float32)
        mean = means[: windows * channels] + means[windows * channels :]
        scale = lax.rsqrt(mean + EPSILON)
        shape = (windows, channels, width)
        yield (
            lanes,
            (real * scale).astype(jnp.bfloat16).astype(jnp.float32).reshape(shape),
            (imag * scale).astype(jnp.bfloat16).astype(jnp.float32).reshape(shape),
        )


def row_factors(real, imag):
    return real + imag, real, imag


def col_factors(real, imag):
    return real, -(real + imag), real - imag


def store_factors(source, target, begin, factors):
    for lanes, real, imag in whiten(source):
        for k, value in enumerate(factors(real, imag)):
            target[k, :, pl.ds(begin, source.shape[2]), lanes] = value


def reach_of(scalars, step):
    slots = (scalars.shape[1] - SLOT_AT) // 2
    picked = [
        jnp.where(scalars[0, SLOT_AT + k] == step, scalars[0, SLOT_AT + slots + k], 0) for k in range(slots)
    ]
    return functools.reduce(lambda x, y: x + y, picked)


def cross_tile(rows, cols, cross, reach, first_distance, begin=0, row_count=None):
    _, windows, all_rows, bins = rows.shape
    row_count = row_count or all_rows
    groups = cols.shape[2] // ROWS

    def body(step, carry):
        row_to = pl.multiple_of((step // groups) * 8, 8)
        row_at = pl.multiple_of(begin + row_to, 8)
        group = step % groups
        col_at = pl.multiple_of(group * ROWS, ROWS)
        nearest = first_distance + col_at - row_at
        active = (nearest - 7 < reach) & (-(nearest + ROWS - 1) < reach)

        @pl.when(active)
        def _():
            for at in range(0, bins, LANES):
                lanes = pl.ds(at, LANES)
                for first in range(0, 8, OWN):
                    sums = [[None] * 3 for _ in range(OWN)]
                    for w in range(windows):
                        for k in range(3):
                            right = cols[k, w, pl.ds(col_at, ROWS), lanes]
                            left = rows.at[k, w, pl.ds(row_at, 8), lanes]
                            for i in range(OWN):
                                product = right * left[pl.ds(first + i, 1)]
                                sums[i][k] = product if w == 0 else sums[i][k] + product
                    for i in range(OWN):
                        k1, k2, k3 = sums[i]
                        at_row = (group * row_count + row_to + first + i) * ROWS
                        place = pl.ds(pl.multiple_of(at_row, ROWS), ROWS)
                        cross[place, pl.ds(at, LANES)] = (k1 - k3).astype(jnp.bfloat16)
                        cross[place, pl.ds(bins + at, LANES)] = (k1 + k2).astype(jnp.bfloat16)

        return carry

    lax.fori_loop(0, (row_count // 8) * groups, body, 0)


def lag_block(core, cross, begin, table, size, store):
    place = pl.ds(pl.multiple_of(begin, 2 * size), 2 * size)
    lags = jnp.dot(cross[place], table[...], preferred_element_type=jnp.float32)
    low, high = lags[:size], lags[size:]
    pl.when(core == 0)(lambda: store(low, high.astype(jnp.bfloat16)))
    pl.when(core != 0)(lambda: store(high, low.astype(jnp.bfloat16)))


def lag_blocks(core, cross, blocks, table, size, store):
    lags = jnp.dot(cross[: blocks * 2 * size], table[...], preferred_element_type=jnp.float32)
    parts = [(lags[k * 2 * size :][:size], lags[(k * 2 + 1) * size :][:size]) for k in range(blocks)]

    @pl.when(core == 0)
    def _():
        for k, (low, high) in enumerate(parts):
            store(k, low, high.astype(jnp.bfloat16))

    @pl.when(core != 0)
    def _():
        for k, (low, high) in enumerate(parts):
            store(k, high, low.astype(jnp.bfloat16))


def store_at(keep, sends, shift, half):
    def store(kept, sent):
        size = sent.shape[0]
        keep[shift, pl.ds(half * size, size)] = kept
        sends[shift * HALVES + half][0] = sent

    return store


def lag_sums(scalars, cross, table, keep, sends):
    owners, size = keep.shape[0], keep.shape[1] // HALVES
    core, day = scalars[0, 0], scalars[0, 1]
    for shift in range(owners):
        owner = lax.rem(day + shift, owners)
        for half in range(HALVES):
            begin = (half * owners + owner) * (2 * size)
            lag_block(core, cross, begin, table, size, store_at(keep, sends, shift, half))


def begins_of(parts):
    return [sum(p.shape[2] for p in parts[:k]) for k in range(len(parts))]


def own_kernel(part_count, scalars, table, *refs):
    parts = refs[:part_count]
    keep, send, rows, cols, cross = refs[part_count:]
    sends = [send.at[pl.ds(k, 1)] for k in range(send.shape[0])]
    for part, begin in zip(parts, begins_of(parts)):
        for lanes, real, imag in whiten(part):
            for k in range(3):
                rows[k, :, pl.ds(begin, part.shape[2]), lanes] = row_factors(real, imag)[k]
                cols[k, :, pl.ds(begin, part.shape[2]), lanes] = col_factors(real, imag)[k]
    cross_tile(rows, cols, cross, reach_of(scalars, 0), 0)
    lag_sums(scalars, cross, table, keep, sends)


def days_kernel(shifts, owners, part_count, after_count, step, scalars, own_rows, table, *refs):
    parts, refs = refs[:part_count], refs[part_count:]
    if not parts:
        cols, *refs = refs
    keep, *sends, cross = refs[after_count:]
    if parts:
        *sends, cols = sends
    per = len(sends) // len(shifts)
    width = own_rows.shape[2]
    count = width // owners
    size = count * ROWS // 2
    core, day = scalars[0, 0], scalars[0, 1]
    reach = reach_of(scalars, step)

    def store(k, half, kept, sent):
        keep[k, pl.ds(half * size, size)] = kept
        begin = 0
        for send in sends[k * per : (k + 1) * per]:
            low = max(begin, half * size)
            high = min(begin + send.shape[1], (half + 1) * size)
            if low < high:
                send[0, pl.ds(low - begin, high - low)] = sent[low - half * size : high - half * size]
            begin += send.shape[1]

    @pl.when(reach > 0)
    def _():
        for part, begin in zip(parts, begins_of(parts)):
            store_factors(part, cols, begin, col_factors)
        for k, shift in enumerate(shifts):
            begin = lax.rem(day + shift, owners) * count
            cross_tile(own_rows, cols, cross, reach, step * width, begin, count)
            lag_blocks(core, cross, HALVES, table, size, functools.partial(store, k))


def half_cross(can_swap, step, half, scalars, own_rows, part, cols, cross, swap_refs, finish):
    width, count = own_rows.shape[2], part.shape[2]
    reach = reach_of(scalars, step)

    @pl.when(reach > 0)
    def _():
        store_factors(part, cols, 0, col_factors)
        cross_tile(own_rows, cols, cross, reach, step * width + half * count)
        finish(False)

    if can_swap:
        rows, wide_cols = swap_refs

        @pl.when(scalars[0, 2] != 0)
        def _():
            for at in range(0, own_rows.shape[3], LANES):
                lanes = pl.ds(at, LANES)
                real, imag = own_rows[1, :, :, lanes], own_rows[2, :, :, lanes]
                for k, value in enumerate(col_factors(real, imag)):
                    wide_cols[k, :, :, lanes] = value
            store_factors(part, rows, 0, row_factors)
            cross_tile(rows, wide_cols, cross, FAR, 0)
            finish(True)


def first_half_kernel(can_swap, step, scalars, own_rows, table, part, keep, send, cols, cross, *swap_refs):
    owners, size = keep.shape[0], keep.shape[1]

    def finish(swapped):
        def store(k, kept, sent):
            keep[k] = kept
            send[k] = sent

        lag_blocks(scalars[0, 0], cross, owners, table, size, store)

    half_cross(can_swap, step, 0, scalars, own_rows, part, cols, cross, swap_refs, finish)


def second_half_kernel(
    can_swap, step, after_count, scalars, own_rows, table, part, first_keep, first_send, *refs
):
    keep, *refs = refs[after_count:]
    sends = refs[: keep.shape[0] * HALVES]
    cols, cross, *swap_refs = refs[keep.shape[0] * HALVES :]
    owners, size = keep.shape[0], keep.shape[1] // HALVES
    core, day = scalars[0, 0], scalars[0, 1]

    def finish(swapped):
        def store(block, kept, sent):
            for shift in range(owners):
                owner = lax.rem(day + shift, owners)
                half = block if swapped else 1
                here = owner != 0 if swapped else owner == block
                pl.when(here)(lambda: store_at(keep, sends, shift, half)(kept, sent))

        for shift in range(owners):
            owner = lax.rem(day + shift, owners)
            if swapped:
                for half in range(HALVES):
                    copy = functools.partial(
                        store_at(keep, sends, shift, half), first_keep[half], first_send[half]
                    )
                    pl.when(owner == 0)(copy)
            else:
                store_at(keep, sends, shift, 0)(first_keep[owner], first_send[owner])
        lag_blocks(core, cross, HALVES if swapped else owners, table, size, store)

    half_cross(can_swap, step, 1, scalars, own_rows, part, cols, cross, swap_refs, finish)


VMEM = pl.BlockSpec(memory_space=pltpu.VMEM)
ANY = pl.BlockSpec(memory_space=pl.ANY)
FREE = pl.CostEstimate(flops=0, bytes_accessed=0, transcendentals=0)
PARAMS = pltpu.CompilerParams(vmem_limit_bytes=VMEM_LIMIT)


def sums_shapes(owners, width):
    size = width * width // (2 * owners * HALVES)
    return [jax.ShapeDtypeStruct((owners, HALVES * size, LAGS), jnp.float32)] + [
        jax.ShapeDtypeStruct((1, size, LAGS), jnp.bfloat16)
    ] * (owners * HALVES)


def fetch_kernel(source, *refs):
    *parts, sems = refs
    half = parts[0].shape[2]
    copies = [
        pltpu.make_async_copy(source.at[:, :, pl.ds(k * half, half)], part, sems.at[k])
        for k, part in enumerate(parts)
    ]
    for copy in copies:
        copy.start()
    for copy in copies:
        copy.wait()


def fetch_halves(spectra):
    days, windows, width, parts, bins = spectra.shape
    shape = jax.ShapeDtypeStruct((days, windows, width // HALVES, parts, bins), spectra.dtype)
    return pl.pallas_call(
        fetch_kernel,
        out_shape=[shape] * HALVES,
        in_specs=[ANY],
        out_specs=[VMEM] * HALVES,
        scratch_shapes=[pltpu.SemaphoreType.DMA((HALVES,))],
        compiler_params=PARAMS,
        cost_estimate=FREE,
    )(spectra)


def own_tile(scalars, parts, table, owners):
    _, windows, _, bins = parts[0].shape
    width = sum(part.shape[2] for part in parts)
    factors = (3, windows, width, bins)
    keep_shape, *send_shapes = sums_shapes(owners, width)
    sent = jax.ShapeDtypeStruct((len(send_shapes),) + send_shapes[0].shape[1:], send_shapes[0].dtype)
    keep, send, rows = pl.pallas_call(
        functools.partial(own_kernel, len(parts)),
        out_shape=[keep_shape, sent, jax.ShapeDtypeStruct(factors, jnp.float32)],
        in_specs=[VMEM] + [VMEM] * (1 + len(parts)),
        out_specs=[VMEM] * 3,
        scratch_shapes=[
            pltpu.VMEM(factors, jnp.float32),
            pltpu.VMEM((width * width, 2 * bins), jnp.bfloat16),
        ],
        compiler_params=PARAMS,
        cost_estimate=FREE,
    )(scalars, table, *parts)
    return keep, [send], rows


def days_tile(scalars, own_rows, table, owners, step, shifts, splits, parts=(), cols=None, after=()):
    _, windows, width, bins = own_rows.shape
    col_shape = (3, windows, width, bins)
    shapes = [jax.ShapeDtypeStruct((len(shifts), sum(splits), LAGS), jnp.float32)]
    shapes += [jax.ShapeDtypeStruct((1, rows, LAGS), jnp.bfloat16) for rows in splits] * len(shifts)
    if cols is None:
        shapes.append(jax.ShapeDtypeStruct(col_shape, jnp.float32))
    operands = list(parts) if cols is None else [cols]
    keep, *sends = pl.pallas_call(
        functools.partial(days_kernel, shifts, owners, len(parts), len(after), step),
        out_shape=shapes,
        in_specs=[VMEM] * (3 + len(operands)) + [ANY] * len(after),
        out_specs=[VMEM] * len(shapes),
        scratch_shapes=[pltpu.VMEM((width // owners * width, 2 * bins), jnp.bfloat16)],
        compiler_params=PARAMS,
        cost_estimate=FREE,
    )(scalars, own_rows, table, *operands, *after)
    if cols is None:
        *sends, cols = sends
    return keep, sends, cols


def half_scratch(own_rows, can_swap):
    _, windows, width, bins = own_rows.shape
    half = width // HALVES
    wide, narrow = (3, windows, width, bins), (3, windows, half, bins)
    scratch = [pltpu.VMEM(narrow, jnp.float32), pltpu.VMEM((width * half, 2 * bins), jnp.bfloat16)]
    if can_swap:
        scratch += [pltpu.VMEM(narrow, jnp.float32), pltpu.VMEM(wide, jnp.float32)]
    return scratch


def first_half_tile(scalars, own_rows, part, table, owners, step, can_swap):
    width = own_rows.shape[2]
    size = width * width // (2 * owners * HALVES)
    return pl.pallas_call(
        functools.partial(first_half_kernel, can_swap, step),
        out_shape=[
            jax.ShapeDtypeStruct((owners, size, LAGS), jnp.float32),
            jax.ShapeDtypeStruct((owners, size, LAGS), jnp.bfloat16),
        ],
        in_specs=[VMEM, VMEM, VMEM, VMEM],
        out_specs=[VMEM, VMEM],
        scratch_shapes=half_scratch(own_rows, can_swap),
        compiler_params=PARAMS,
        cost_estimate=FREE,
    )(scalars, own_rows, table, part)


def second_half_tile(scalars, own_rows, part, first, table, owners, step, can_swap, after):
    keep, *sends = pl.pallas_call(
        functools.partial(second_half_kernel, can_swap, step, len(after)),
        out_shape=sums_shapes(owners, own_rows.shape[2]),
        in_specs=[VMEM] + [VMEM] * 5 + [ANY] * len(after),
        out_specs=[VMEM] * (owners * HALVES + 1),
        scratch_shapes=half_scratch(own_rows, can_swap),
        compiler_params=PARAMS,
        cost_estimate=FREE,
    )(scalars, own_rows, table, part, *first, *after)
    return keep, sends


def add_kernel(tiles, shift, *refs):
    out = refs[-1]
    for tile, places in enumerate(tiles):
        keep, *got = refs[tile * (1 + HALVES) : (tile + 1) * (1 + HALVES)]
        for half, (sent, at) in enumerate(zip(got, places)):
            place = pl.ds(half * sent.shape[1], sent.shape[1])
            out[tile, place] = (keep[shift, place] + sent[at].astype(jnp.float32)).astype(out.dtype)


def add_cores(tiles, shift, after=()):
    operands = [term for keep, got in tiles for term in [keep] + [array for array, _ in got[shift]]]
    places = [[at for _, at in got[shift]] for _, got in tiles]
    rows = tiles[0][0].shape[1]
    return pl.pallas_call(
        functools.partial(add_kernel, places, shift),
        out_shape=jax.ShapeDtypeStruct((len(tiles), rows, LAGS), jnp.bfloat16),
        in_specs=[VMEM] * len(operands) + [ANY] * len(after),
        out_specs=VMEM,
        compiler_params=PARAMS,
        cost_estimate=FREE,
    )(*operands, *after)


def write_tile(scalars, step, terms, tile, norm_scale):
    row_count, width, _ = tile.shape
    slots = (scalars.shape[1] - SLOT_AT) // 2
    reach = reach_of(scalars, step)
    half_width = width // HALVES
    size = row_count * half_width
    for half in range(HALVES):
        value = None
        for term in terms:
            if isinstance(term, list):
                whole = jnp.concatenate([array[at].astype(jnp.float32) for array, at in term], axis=0)
                part = whole[half * size : (half + 1) * size]
            else:
                array, at = term
                part = array[at, pl.ds(half * size, size)]
            part = part.astype(jnp.float32)
            value = part if value is None else value + part
        value = value.reshape(row_count, half_width, LAGS)
        row = lax.broadcasted_iota(jnp.int32, value.shape, 0) + scalars[0, 3] * row_count
        col = lax.broadcasted_iota(jnp.int32, value.shape, 1) + half * half_width
        distance = jnp.abs(step * width + col - row)
        kept = (distance > 0) & (distance < reach)
        tile[:, pl.ds(half * half_width, half_width), :] = jnp.where(kept, value * norm_scale, 0.0)


def grouped(refs, places):
    terms = []
    for place in places:
        if isinstance(place, list):
            terms.append([(refs.pop(0), at) for at in place])
        else:
            terms.append((refs.pop(0), place))
    return terms


def tile_kernel(listed, norm_scale, scalars, *refs):
    rest, tiles = list(refs[: -len(listed)]), refs[-len(listed) :]
    for (step, places), tile in zip(listed, tiles):
        write_tile(scalars, step, grouped(rest, places), tile, norm_scale)


def flat(terms):
    operands, places = [], []
    for term in terms:
        listed = isinstance(term, list)
        operands += [array for array, _ in term] if listed else [term[0]]
        places.append([at for _, at in term] if listed else term[1])
    return operands, places


def finished_tiles(scalars, summed, row_count, width, norm_scale):
    operands, listed = [], []
    for step, terms in summed:
        more, places = flat(terms)
        operands += more
        listed.append((step, places))
    tile = jax.ShapeDtypeStruct((row_count, width, LAGS), jnp.float32)
    tiles = pl.pallas_call(
        functools.partial(tile_kernel, listed, norm_scale),
        out_shape=[tile] * len(listed),
        in_specs=[VMEM] + [VMEM] * len(operands),
        out_specs=[VMEM] * len(listed),
        compiler_params=PARAMS,
        cost_estimate=FREE,
    )(scalars, *operands)
    return [(step, tile) for (step, _), tile in zip(summed, tiles)]


def output_kernel(ready_steps, late, after_count, norm_scale, scalars, *refs):
    out, tiles, zeros, sems = refs[-4:]
    slots = out.shape[0]
    ready, rest = refs[: len(ready_steps)], list(refs[len(ready_steps) : -4])

    def copies(slot, source):
        return pltpu.make_async_copy(source, out.at[slot], sems.at[slot])

    def start(step, source):
        for slot in range(slots):
            pl.when(scalars[0, SLOT_AT + slot] == step)(copies(slot, source).start)

    for step, tile in zip(ready_steps, ready):
        start(step, tile)
    zeros[...] = jnp.zeros_like(zeros)
    start(-1, zeros)
    for place, (step, counts) in enumerate(late):
        terms = grouped(rest, counts)

        @pl.when(reach_of(scalars, step) > 0)
        def _(step=step, terms=terms, place=place):
            write_tile(scalars, step, terms, tiles.at[place], norm_scale)

        start(step, tiles.at[place])
    for slot in range(slots):
        copies(slot, zeros).wait()


def write_output(scalars, ready, late, slots, norm_scale, after):
    tile_shape = ready[0][1].shape
    operands, listed = [tile for _, tile in ready], []
    for step, terms in late:
        more, counts = flat(terms)
        operands += more
        listed.append((step, counts))
    return pl.pallas_call(
        functools.partial(output_kernel, [step for step, _ in ready], listed, len(after), norm_scale),
        out_shape=jax.ShapeDtypeStruct((slots,) + tile_shape, jnp.float32),
        in_specs=[VMEM] + [VMEM] * len(operands) + [ANY] * len(after),
        out_specs=ANY,
        scratch_shapes=[
            pltpu.VMEM((len(late),) + tile_shape, jnp.float32),
            pltpu.VMEM(tile_shape, jnp.float32),
            pltpu.SemaphoreType.DMA((slots,)),
        ],
        compiler_params=PARAMS,
        cost_estimate=FREE,
    )(scalars, *operands, *after)


def on_device(spectra, tile_offset, pair_reach):
    blocks = lax.axis_size("chan")
    days, cores = lax.axis_size("day"), lax.axis_size("sub")
    steps = min(MAX_STEPS, blocks - 1)
    wraps = blocks >= 3 and steps == blocks - 1 and days == 2
    local_days, local_windows, width, _, bins = spectra.shape
    norm_scale = 1.0 / math.sqrt(bins * local_days * days * local_windows * cores)
    row_count = width // (days * cores)
    slots = tile_offset.shape[1]
    day, core, block = lax.axis_index("day"), lax.axis_index("sub"), lax.axis_index("chan")
    table = jnp.asarray(lag_table(bins))

    half = width // HALVES
    halves = [
        jnp.transpose(part, (3, 0, 1, 2, 4)).reshape(2, -1, half, bins) for part in fetch_halves(spectra)
    ]
    is_last = (block == blocks - 1).astype(jnp.int32) if wraps else jnp.int32(0)
    scalars = jnp.stack([core, day, is_last, day * cores + core]).astype(jnp.int32)
    scalars = jnp.concatenate([scalars, tile_offset[0], pair_reach[0]])[None]

    def over_cores(sends):
        got = [lax.ppermute(send, "sub", [(k, (k + 1) % cores) for k in range(cores)]) for send in sends]
        got = [(array, at) for array in got for at in range(array.shape[0])]
        return [got[k : k + HALVES] for k in range(0, len(got), HALVES)]

    def over_days(pieces):
        return [
            lax.ppermute(piece, "day", [(k, (k + shift) % days) for k in range(days)])
            for shift, piece in enumerate(pieces, 1)
        ]

    def to_first(piece, shift):
        pairs = [((blocks - 1) * days + k, (k + shift) % days) for k in range(days)]
        return lax.ppermute(piece, ("chan", "day"), pairs)

    keep, sends, own_rows = own_tile(scalars, halves, table, days)
    own_sums = (keep, over_cores(sends))
    ready, late, back, settled = [], [], [], []

    pairs = [(a + 1, a) for a in range(blocks - 1)] + [(0, blocks - 1)] * wraps
    moving = [lax.ppermute(part, "chan", pairs) for part in halves]
    first = first_half_tile(scalars, own_rows, moving[0], table, days, 1, wraps)
    ahead = moving
    after = [x for pair in own_sums[1] for x in pair] if 0 else []
    keep, sends1 = second_half_tile(scalars, own_rows, moving[1], first, table, days, 1, wraps, after)
    sums = (keep, over_cores(sends1))
    pieces = [add_cores([sums, own_sums], shift) for shift in range(1, days)]
    if wraps:
        back = [to_first(add_cores([sums], shift), shift) for shift in reversed(range(days))]
    moved = over_days(pieces)
    summed = [
        (step, [(keep, 0), got[0]] + [(piece, 1 - step) for piece in moved])
        for step, (keep, got) in enumerate([own_sums, sums])
    ]
    ready += finished_tiles(scalars, summed, row_count, width, norm_scale)

    waits = [sends[0], first[0]]
    for step in range(2, steps + 1 - wraps):
        pairs = [(a + 1, a) for a in range(blocks - step)]
        ahead = [
            lax.ppermute(lax.optimization_barrier((part, wait))[0], "chan", pairs)
            for part, wait in zip(ahead, waits)
        ]
        rows = row_count * width
        arrived, block = [], {"parts": ahead}
        if days > 1:
            keep, sends2, cols = days_tile(
                scalars, own_rows, table, days, step, range(1, days), (rows // 2, rows // 2), ahead, None, pieces
            )
            sums = (keep, over_cores(sends2))
            arrived = over_days([add_cores([sums], k) for k in range(days - 1)])
            block = {"cols": cols}
        splits = (rows * 3 // 4, rows // 4)
        keep, sends2, _ = days_tile(scalars, own_rows, table, days, step, [0], splits, **block)
        got = [part for parts in over_cores(sends2) for part in parts]
        late.append((step, [(keep, 0), got] + [(piece, 0) for piece in arrived]))
    if wraps:
        terms = [(piece, 0) for piece in back]
        ((_, hosted),) = finished_tiles(scalars, [(steps, terms)], row_count, width, norm_scale)
        ready.append((steps, hosted))
        pairs = [(c, (c + 1) % cores) for c in range(cores)]
        settled = [lax.ppermute(hosted[:3, :24], "sub", pairs)]
    return write_output(scalars, ready, late, slots, norm_scale, settled)[None]


def solution(mesh):
    in_specs = (P(("groups", "day"), "sub", "chan", None, None), P("chan", None), P("chan", None))
    out_specs = P(("groups", "chan"), None, ("day", "sub"), None, None)
    return jax.shard_map(
        on_device, mesh=mesh, in_specs=in_specs, out_specs=out_specs, check_vma=False
    )
```
